32 devices in a mesh: seq: 8 (over z, x), kv: 4 (over y, core).
Axes of the slice: x: 2, y: 2, z: 4, core: 2. Of those that a mesh axis runs over, the one named last changes fastest.
Arguments:
- tokens: bfloat16 [8192, 2048], P('seq'), may hold values from -6 to 6
- attention_norm_gain: bfloat16 [2048], replicated, may hold values from 0.5 to 1.5
- query_weight: bfloat16 [2048, 2048], P(None, 'kv'), may hold values from -0.125 to 0.125
- key_weight: bfloat16 [2048, 512], P(None, 'kv'), may hold values from -0.125 to 0.125
- value_weight: bfloat16 [2048, 512], P(None, 'kv'), may hold values from -0.125 to 0.125
- query_down_adapter: bfloat16 [2048, 8], replicated, may hold values from -0.125 to 0.125
- query_up_adapter: bfloat16 [8, 32, 64], P(None, 'kv'), may hold values from -2 to 2
- key_down_adapter: bfloat16 [2048, 8], replicated, may hold values from -0.125 to 0.125
- key_up_adapter: bfloat16 [8, 8, 64], P(None, 'kv'), may hold values from -2 to 2
- value_down_adapter: bfloat16 [2048, 8], replicated, may hold values from -0.125 to 0.125
- value_up_adapter: bfloat16 [8, 8, 64], P(None, 'kv'), may hold values from -2 to 2
- query_feature_map: bfloat16 [32, 64, 64], P('kv'), may hold values from -0.75 to 0.75
- key_feature_map: bfloat16 [8, 64, 64], P('kv'), may hold values from -0.75 to 0.75
- output_weight: bfloat16 [2048, 2048], P('kv'), may hold values from -0.5 to 0.5
- output_down_adapter: bfloat16 [32, 64, 8], P('kv'), may hold values from -0.125 to 0.125
- output_up_adapter: bfloat16 [8, 2048], replicated, may hold values from -4 to 4
- feedforward_norm_gain: bfloat16 [2048], replicated, may hold values from 0.5 to 1.5
- gate_weight: bfloat16 [2048, 8192], P(None, 'kv'), may hold values from -0.125 to 0.125
- up_weight: bfloat16 [2048, 8192], P(None, 'kv'), may hold values from -0.125 to 0.125
- down_weight: bfloat16 [8192, 2048], P('kv'), may hold values from -0.0625 to 0.0625
- document_start_mask: int32 [8192], P('seq'), may hold values from 0 to 1, as said below
- output_cotangent: bfloat16 [8192, 2048], P('seq'), may hold values from -6 to 6
Outputs:
- output: bfloat16 [8192, 2048], P('seq')
- grad_tokens: float32 [8192, 2048], P('seq')
- grad_norm1: float32 [2048], P('seq')
- grad_wq: float32 [2048, 2048], P('seq', 'kv')
- grad_wk: float32 [2048, 512], P('seq', 'kv')
- grad_wv: float32 [2048, 512], P('seq', 'kv')
- grad_aq: float32 [2048, 8], P('seq')
- grad_bq: float32 [8, 32, 64], P(None, 'kv', 'seq')
- grad_ak: float32 [2048, 8], P('seq')
- grad_bk: float32 [8, 8, 64], P(None, 'kv', 'seq')
- grad_av: float32 [2048, 8], P('seq')
- grad_bv: float32 [8, 8, 64], P(None, 'kv', 'seq')
- grad_featq: float32 [32, 64, 64], P('kv', 'seq')
- grad_featk: float32 [8, 64, 64], P('kv', 'seq')
- grad_wo: float32 [2048, 2048], P('kv', 'seq')
- grad_ao: float32 [32, 64, 8], P('kv', 'seq')
- grad_bo: float32 [8, 2048], P(None, 'seq')
- grad_norm2: float32 [2048], P('seq')
- grad_gate: float32 [2048, 8192], P('seq', 'kv')
- grad_up: float32 [2048, 8192], P('seq', 'kv')
- grad_down: float32 [8192, 2048], P('kv', 'seq')
The draws below stay inside these ranges and needn't reach their ends.
Inputs may be any that keep to these rules, and one draw needn't show every extreme that they name: `document_start_mask`: position 0 begins a document. One document begins in the first 512 positions and runs into the last 1024 positions of the stream; the other documents lie before or after it.
All inputs are finite; a program needn't handle non-finite values.
Results may differ from the reference program's by a relative error of at most 0.02.
Values may be sent and summed in bfloat16 or wider, within the bound.
No kernel may reach another device: no remote copies, remote signals or barrier semaphores. Data moves between devices by JAX's collectives and lax.ppermute only.
A program may use at most 384 MiB of HBM per device.

```python
import jax
import jax.numpy as jnp
from jax import lax

MODEL_WIDTH = 2048
QUERY_HEAD_COUNT = 32
KEY_VALUE_HEADS = 8
HEAD_SIZE = 64
FF = 8192
ADAPTER_RANK = 8
WIN = 64
TOK_DEV = 1024
STREAM_TOKENS = 8192


def draw_document_start_mask(key, part):
    key_first = jax.random.fold_in(key, 11)
    key_last = jax.random.fold_in(key, 23)
    key_extra = jax.random.fold_in(key, 37)
    positions = jnp.arange(STREAM_TOKENS, dtype=jnp.int32)
    opening = jax.random.randint(key_first, (), 1, TOK_DEV // 2)
    closing = STREAM_TOKENS - TOK_DEV + jax.random.randint(key_last, (), TOK_DEV // 2, TOK_DEV)
    extra = jax.random.randint(key_extra, (STREAM_TOKENS,), 0, WIN) == 0
    outside = (positions < opening) | (positions > closing)
    starts = (positions == 0) | (positions == opening) | (positions == closing) | extra & outside
    return starts.astype(jnp.int32)


def block_levels(key, shape, pieces, least, largest):
    def one(dim, blocks):
        heights = jax.random.uniform(jax.random.fold_in(jax.random.fold_in(key, 6), dim), (blocks,), jnp.float32, least / len(pieces), largest / len(pieces))
        return jnp.repeat(jnp.exp(heights), shape[dim] // blocks).reshape((-1,) + (1,) * (len(shape) - dim - 1))

    level = one(*pieces[0])
    for cut in pieces[1:]:
        level = level * one(*cut)
    return level


def normal_values(rng, shape, width, most, pieces=(), kind=jnp.bfloat16):
    values = width * jax.random.normal(rng, shape, jnp.float32)
    if pieces:
        values = values * block_levels(rng, shape, pieces, -0.22, 0.18)
    return jnp.clip(values, -most, most).astype(kind)


def setup_inputs(seed: int = 0) -> dict:
    splits = jax.random.split(jax.random.key(seed), 23)
    tokens = normal_values(splits[0], (STREAM_TOKENS, MODEL_WIDTH), 1.0, 6.0, ((0, 8),))
    attention_norm_gain = jnp.clip(1.0 + 0.1 * jax.random.normal(splits[1], (MODEL_WIDTH,), jnp.float32), 0.5, 1.5).astype(jnp.bfloat16)
    query_weight = normal_values(splits[2], (MODEL_WIDTH, QUERY_HEAD_COUNT * HEAD_SIZE), MODEL_WIDTH ** -0.5, 0.125, ((1, 4),))
    key_weight = normal_values(splits[3], (MODEL_WIDTH, KEY_VALUE_HEADS * HEAD_SIZE), MODEL_WIDTH ** -0.5, 0.125, ((1, 4),))
    value_weight = normal_values(splits[4], (MODEL_WIDTH, KEY_VALUE_HEADS * HEAD_SIZE), MODEL_WIDTH ** -0.5, 0.125, ((1, 4),))
    query_down_adapter = normal_values(splits[5], (MODEL_WIDTH, ADAPTER_RANK), MODEL_WIDTH ** -0.5, 0.125)
    query_up_adapter = normal_values(splits[6], (ADAPTER_RANK, QUERY_HEAD_COUNT, HEAD_SIZE), ADAPTER_RANK ** -0.5, 2.0, ((1, 4),))
    key_down_adapter = normal_values(splits[7], (MODEL_WIDTH, ADAPTER_RANK), MODEL_WIDTH ** -0.5, 0.125)
    key_up_adapter = normal_values(splits[8], (ADAPTER_RANK, KEY_VALUE_HEADS, HEAD_SIZE), ADAPTER_RANK ** -0.5, 2.0, ((1, 4),))
    value_down_adapter = normal_values(splits[9], (MODEL_WIDTH, ADAPTER_RANK), MODEL_WIDTH ** -0.5, 0.125)
    value_up_adapter = normal_values(splits[10], (ADAPTER_RANK, KEY_VALUE_HEADS, HEAD_SIZE), ADAPTER_RANK ** -0.5, 2.0, ((1, 4),))
    query_feature_map = normal_values(splits[11], (QUERY_HEAD_COUNT, HEAD_SIZE, HEAD_SIZE), HEAD_SIZE ** -0.5, 0.75, ((0, 4),))
    key_feature_map = normal_values(splits[12], (KEY_VALUE_HEADS, HEAD_SIZE, HEAD_SIZE), HEAD_SIZE ** -0.5, 0.75, ((0, 4),))
    output_weight = normal_values(splits[13], (QUERY_HEAD_COUNT * HEAD_SIZE, MODEL_WIDTH), (QUERY_HEAD_COUNT * HEAD_SIZE // 16) ** -0.5, 0.5, ((0, 4),))
    output_down_adapter = normal_values(splits[14], (QUERY_HEAD_COUNT, HEAD_SIZE, ADAPTER_RANK), (QUERY_HEAD_COUNT * HEAD_SIZE) ** -0.5, 0.125, ((0, 4),))
    output_up_adapter = normal_values(splits[15], (ADAPTER_RANK, MODEL_WIDTH), (max(ADAPTER_RANK // 4, 1)) ** -0.5, 4.0)
    feedforward_norm_gain = jnp.clip(1.0 + 0.1 * jax.random.normal(splits[16], (MODEL_WIDTH,), jnp.float32), 0.5, 1.5).astype(jnp.bfloat16)
    gate_weight = normal_values(splits[17], (MODEL_WIDTH, FF), MODEL_WIDTH ** -0.5, 0.125, ((1, 4),))
    up_weight = normal_values(splits[18], (MODEL_WIDTH, FF), MODEL_WIDTH ** -0.5, 0.125, ((1, 4),))
    down_weight = normal_values(splits[19], (FF, MODEL_WIDTH), FF ** -0.5, 0.0625, ((0, 4),))
    document_start_mask = draw_document_start_mask(jax.random.fold_in(splits[22], 71), 0)
    output_cotangent = normal_values(splits[21], (STREAM_TOKENS, MODEL_WIDTH), 1.0, 6.0, ((0, 8),))
    return {"tokens": tokens, "attention_norm_gain": attention_norm_gain, "query_weight": query_weight, "key_weight": key_weight, "value_weight": value_weight, "query_down_adapter": query_down_adapter, "query_up_adapter": query_up_adapter, "key_down_adapter": key_down_adapter, "key_up_adapter": key_up_adapter, "value_down_adapter": value_down_adapter, "value_up_adapter": value_up_adapter, "query_feature_map": query_feature_map, "key_feature_map": key_feature_map, "output_weight": output_weight, "output_down_adapter": output_down_adapter, "output_up_adapter": output_up_adapter, "feedforward_norm_gain": feedforward_norm_gain, "gate_weight": gate_weight, "up_weight": up_weight, "down_weight": down_weight, "document_start_mask": document_start_mask, "output_cotangent": output_cotangent}


EPSILON = 1e-05
MATRIX_EXACTNESS = lax.Precision.HIGHEST

@jax.custom_vjp
def adapter_product(v):
    return lax.optimization_barrier(v.astype(jnp.bfloat16)).astype(jnp.float32)

@jax.custom_vjp
def adapter_backward(v):
    return v

def low_keep(v):
    return (adapter_product(v), None)

def low_pass(kept, grad):
    return (grad,)

def back_keep(v):
    return (v, None)

def back_low(kept, grad):
    return (adapter_product(grad),)
adapter_product.defvjp(low_keep, low_pass)
adapter_backward.defvjp(back_keep, back_low)

def matrix_product(left, right):
    return jnp.dot(left, right, precision=MATRIX_EXACTNESS)

def feature(inputs, table):
    logits = adapter_backward(jnp.einsum('nhd,hde->nhe', inputs, table, precision=MATRIX_EXACTNESS))
    return adapter_product(jnp.concatenate([jax.nn.softmax(logits, -1), jax.nn.softmax(-logits, -1)], -1))

def project_heads(rms_normalized, weight_matrix, down_adapter, up_adapter):
    adapter_apply = matrix_product(rms_normalized, down_adapter)
    return adapter_product(adapter_backward(matrix_product(rms_normalized, weight_matrix) + matrix_product(adapter_apply, up_adapter.reshape(up_adapter.shape[0], -1))))

def reference(tokens, attention_norm_gain, query_weight, key_weight, value_weight, query_down_adapter, query_up_adapter, key_down_adapter, key_up_adapter, value_down_adapter, value_up_adapter, query_feature_map, key_feature_map, output_weight, output_down_adapter, output_up_adapter, feedforward_norm_gain, gate_weight, up_weight, down_weight, document_start_mask, output_cotangent):
    positions = jnp.arange(STREAM_TOKENS, dtype=jnp.int32)
    opened = lax.cummax(jnp.where(document_start_mask == 1, positions, jnp.int32(-1)), axis=0)
    blocks = STREAM_TOKENS // TOK_DEV
    group_size = QUERY_HEAD_COUNT // KEY_VALUE_HEADS
    scale = HEAD_SIZE ** (-0.5)
    rows_index = jnp.arange(TOK_DEV, dtype=jnp.int32)[:, None]
    cols_index = jnp.arange(TOK_DEV + WIN, dtype=jnp.int32)[None, :]

    def attend(carry, inputs):
        state, normal, key_prev, value_prev, phi_prev = carry
        index, query_blk, key_blk, value_blk, qphi_blk, kphi_blk = inputs
        offset = index * TOK_DEV
        opened_blk = lax.dynamic_slice_in_dim(opened, offset, TOK_DEV)
        last_reset = lax.dynamic_index_in_dim(opened, offset + TOK_DEV - WIN - 1, keepdims=False)
        resets = (last_reset >= offset - WIN).astype(jnp.float32)
        ext_pos = offset - WIN + jnp.arange(TOK_DEV + WIN, dtype=jnp.int32)
        same_doc = ext_pos[None, :] >= opened_blk[:, None]
        win_mask = ((cols_index > rows_index) & (cols_index <= rows_index + WIN) & same_doc).astype(jnp.float32)
        lin_mask = ((cols_index <= rows_index) & same_doc).astype(jnp.float32)
        carry_on = (opened_blk < offset - WIN).astype(jnp.float32)
        key_keep = ((jnp.arange(TOK_DEV + WIN, dtype=jnp.int32) < TOK_DEV) & (ext_pos >= last_reset)).astype(jnp.float32)
        keys = jnp.concatenate([key_prev, key_blk], 0)
        values = jnp.concatenate([value_prev, value_blk], 0)
        kphi = jnp.concatenate([phi_prev, kphi_blk], 0)
        query_grouped = query_blk.reshape(TOK_DEV, KEY_VALUE_HEADS, group_size, HEAD_SIZE)
        qphi_grouped = qphi_blk.reshape(TOK_DEV, KEY_VALUE_HEADS, group_size, 2 * HEAD_SIZE)
        scores = adapter_backward(jnp.einsum('ikgd,ekd->kgie', query_grouped, keys, precision=MATRIX_EXACTNESS)) * scale
        linear = adapter_backward(jnp.einsum('ikgf,ekf->kgie', qphi_grouped, kphi, precision=MATRIX_EXACTNESS))
        weight_matrix = jnp.exp(scores) * win_mask + linear * lin_mask
        carried = jnp.einsum('ikgf,kfd->kgid', qphi_grouped, state, precision=MATRIX_EXACTNESS) * carry_on[None, None, :, None]
        carried_norm = jnp.einsum('ikgf,kf->kgi', qphi_grouped, normal, precision=MATRIX_EXACTNESS) * carry_on[None, None, :]
        totals = lax.optimization_barrier(jnp.sum(weight_matrix, -1)) + carried_norm
        shares = adapter_product(weight_matrix / totals[..., None])
        mixture = jnp.einsum('kgie,ekd->kgid', shares, values, precision=MATRIX_EXACTNESS) + carried / totals[..., None]
        weighted = kphi * key_keep[:, None, None]
        state_new = jnp.einsum('ekf,ekd->kfd', weighted, values, precision=MATRIX_EXACTNESS) + (1.0 - resets) * state
        normal_new = lax.optimization_barrier(jnp.sum(weighted, 0)) + (1.0 - resets) * normal
        result = jnp.transpose(mixture, (2, 0, 1, 3)).reshape(TOK_DEV, QUERY_HEAD_COUNT * HEAD_SIZE)
        return ((state_new, normal_new, key_blk[TOK_DEV - WIN:], value_blk[TOK_DEV - WIN:], kphi_blk[TOK_DEV - WIN:]), result)

    def layer_forward(tokens, attention_norm_gain, query_weight, key_weight, value_weight, query_down_adapter, query_up_adapter, key_down_adapter, key_up_adapter, value_down_adapter, value_up_adapter, query_feature_map, key_feature_map, output_weight, output_down_adapter, output_up_adapter, feedforward_norm_gain, gate_weight, up_weight, down_weight):
        rms_one = lax.rsqrt(lax.optimization_barrier(jnp.mean(tokens * tokens, -1, keepdims=True)) + EPSILON)
        attention_normed_input = adapter_product(tokens * rms_one * attention_norm_gain)
        query_rows = project_heads(attention_normed_input, query_weight, query_down_adapter, query_up_adapter).reshape(STREAM_TOKENS, QUERY_HEAD_COUNT, HEAD_SIZE)
        key = project_heads(attention_normed_input, key_weight, key_down_adapter, key_up_adapter).reshape(STREAM_TOKENS, KEY_VALUE_HEADS, HEAD_SIZE)
        value_rows = project_heads(attention_normed_input, value_weight, value_down_adapter, value_up_adapter).reshape(STREAM_TOKENS, KEY_VALUE_HEADS, HEAD_SIZE)
        qphi = feature(query_rows, query_feature_map)
        kphi = feature(key, key_feature_map)
        init = (jnp.zeros((KEY_VALUE_HEADS, 2 * HEAD_SIZE, HEAD_SIZE), jnp.float32), jnp.zeros((KEY_VALUE_HEADS, 2 * HEAD_SIZE), jnp.float32), jnp.zeros((WIN, KEY_VALUE_HEADS, HEAD_SIZE), jnp.float32), jnp.zeros((WIN, KEY_VALUE_HEADS, HEAD_SIZE), jnp.float32), jnp.zeros((WIN, KEY_VALUE_HEADS, 2 * HEAD_SIZE), jnp.float32))
        inputs = (jnp.arange(blocks, dtype=jnp.int32), query_rows.reshape(blocks, TOK_DEV, QUERY_HEAD_COUNT, HEAD_SIZE), key.reshape(blocks, TOK_DEV, KEY_VALUE_HEADS, HEAD_SIZE), value_rows.reshape(blocks, TOK_DEV, KEY_VALUE_HEADS, HEAD_SIZE), qphi.reshape(blocks, TOK_DEV, QUERY_HEAD_COUNT, 2 * HEAD_SIZE), kphi.reshape(blocks, TOK_DEV, KEY_VALUE_HEADS, 2 * HEAD_SIZE))
        _, heads = lax.scan(jax.checkpoint(attend), init, inputs)
        head_outputs = adapter_product(adapter_backward(heads.reshape(STREAM_TOKENS, QUERY_HEAD_COUNT * HEAD_SIZE)))
        output_adapter_path = matrix_product(head_outputs, output_down_adapter.reshape(QUERY_HEAD_COUNT * HEAD_SIZE, -1))
        attention_result = adapter_backward(matrix_product(head_outputs, output_weight) + matrix_product(output_adapter_path, output_up_adapter))
        resid = tokens + attention_result
        rms_two = lax.rsqrt(lax.optimization_barrier(jnp.mean(resid * resid, -1, keepdims=True)) + EPSILON)
        normed_two = adapter_product(resid * rms_two * feedforward_norm_gain)
        gate_pre = adapter_backward(matrix_product(normed_two, gate_weight))
        up_pre = adapter_backward(matrix_product(normed_two, up_weight))
        hidden = adapter_product(jax.nn.silu(gate_pre) * up_pre)
        return adapter_product(resid + matrix_product(hidden, down_weight))
    layer_parameters = tuple((adapter_entry.astype(jnp.float32) for adapter_entry in (tokens, attention_norm_gain, query_weight, key_weight, value_weight, query_down_adapter, query_up_adapter, key_down_adapter, key_up_adapter, value_down_adapter, value_up_adapter, query_feature_map, key_feature_map, output_weight, output_down_adapter, output_up_adapter, feedforward_norm_gain, gate_weight, up_weight, down_weight)))
    output, pull = jax.vjp(layer_forward, *layer_parameters)
    grads = pull(output_cotangent.astype(jnp.float32))
    return (output.astype(jnp.bfloat16), grads[0], grads[1], grads[2], grads[3], grads[4], grads[5], grads[6], grads[7], grads[8], grads[9], grads[10], grads[11], grads[12], grads[13], grads[14], grads[15], grads[16], grads[17], grads[18], grads[19])
```

```python
import jax
import jax.numpy as jnp
from jax import lax
from jax.sharding import PartitionSpec as P

WIN = 64
EPSILON = 1e-05
EXACT = lax.Precision.HIGHEST
F32 = jnp.float32
BF16 = jnp.bfloat16


def dot(a, b, out=F32):
    return jnp.dot(a, b, preferred_element_type=F32).astype(out)


def dot_nt(a, b, out=F32):
    return lax.dot_general(a, b, (((1,), (1,)), ((), ())), preferred_element_type=F32).astype(out)


def dot_tn(a, b, out=F32):
    return lax.dot_general(a, b, (((0,), (0,)), ((), ())), preferred_element_type=F32).astype(out)


def take(x, i):
    return lax.dynamic_index_in_dim(x, i, 0, False)


class Grid:
    def __init__(self):
        self.kv = lax.axis_size("kv")
        self.seq = lax.axis_size("seq")
        self.outer = self.kv // 2
        self.line = self.seq // 2
        k = lax.axis_index("kv")
        s = lax.axis_index("seq")
        self.core, self.y = k % 2, k // 2
        self.x, self.z = s % 2, s // 2
        self.s = s
        self.core_swap = [(i, i ^ 1) for i in range(self.kv)]
        self.x_swap = [(i, i ^ 1) for i in range(self.seq)]
        self.z_groups = [[2 * z + x for z in range(self.line)] for x in range(2)]

    def y_shift(self, j):
        m = self.outer
        return [(y * 2 + c, (y + j) % m * 2 + c) for y in range(m) for c in range(2)]

    def first_row(self, rows):
        return self.core * (rows // 2) + self.y * (rows // self.kv)

    def share(self, x):
        rows = x.shape[0]
        return lax.dynamic_slice_in_dim(x, self.first_row(rows), rows // self.kv, 0)

    def reduce_rows(self, part):
        rows, width = part.shape
        halves = part.reshape(2, rows // 2, width)
        got = lax.ppermute(take(halves, 1 - self.core), "kv", self.core_swap)
        half = take(halves, self.core).astype(F32) + got.astype(F32)
        m = self.outer
        blocks = half.reshape(m, rows // self.kv, width)
        total = take(blocks, self.y)
        for j in range(1, m):
            out = take(blocks, (self.y + j) % m).astype(BF16)
            total = total + lax.ppermute(out, "kv", self.y_shift(j)).astype(F32)
        return total

    def gather_rows(self, share):
        rows, width = share.shape
        m = self.outer
        got = [share] + [lax.ppermute(share, "kv", self.y_shift(j)) for j in range(1, m)]
        if m == 2:
            first = self.y == 0
            half = jnp.concatenate(
                [jnp.where(first, got[0], got[1]), jnp.where(first, got[1], got[0])], 0
            )
        else:
            half = jnp.zeros((m, rows, width), share.dtype)
            for j in range(m):
                half = lax.dynamic_update_index_in_dim(half, got[j], (self.y - j) % m, 0)
            half = half.reshape(m * rows, width)
        other = lax.ppermute(half, "kv", self.core_swap)
        first = self.core == 0
        return jnp.concatenate([jnp.where(first, half, other), jnp.where(first, other, half)], 0)

    def sum_kv(self, x):
        x = x + lax.ppermute(x, "kv", self.core_swap).astype(F32)
        total = x
        for j in range(1, self.outer):
            total = total + lax.ppermute(x, "kv", self.y_shift(j))
        return total

    def pair_columns(self, x):
        rows, width = x.shape
        cut = x.reshape(rows, self.line, 2, width // self.seq)
        other = lax.dynamic_index_in_dim(cut, 1 - self.x, 2, False)
        own = lax.dynamic_index_in_dim(cut, self.x, 2, False)
        return other.reshape(rows, width // 2), own.reshape(rows, width // 2)

    def weight_grad(self, left, right):
        got = lax.ppermute(dot_tn(left[0], right, BF16), "seq", self.x_swap)
        part = (dot_tn(left[1], right) + got.astype(F32)).astype(BF16)
        return self.line_scatter(part).astype(F32)

    def line_scatter(self, part):
        return lax.psum_scatter(
            part, "seq", scatter_dimension=0, tiled=True, axis_index_groups=self.z_groups
        )

    def scatter_blocks(self, blocks):
        cut = blocks.reshape(self.line, 2, -1)
        other = lax.dynamic_index_in_dim(cut, 1 - self.x, 1, False).astype(BF16)
        own = lax.dynamic_index_in_dim(cut, self.x, 1, False)
        part = own + lax.ppermute(other, "seq", self.x_swap).astype(F32)
        total = take(part, self.z)
        m = self.line
        for j in range(1, m):
            pairs = [(z * 2 + x, (z + j) % m * 2 + x) for z in range(m) for x in range(2)]
            out = take(part, (self.z + j) % m).astype(BF16)
            total = total + lax.ppermute(out, "seq", pairs).astype(F32)
        return total

    def shift_seq(self, x, by):
        n = self.seq
        return lax.ppermute(x, "seq", [(i, i + by) for i in range(n) if 0 <= i + by < n])

    def sum_before(self, x, sign):
        total = x
        by = 1
        while by < self.seq:
            total = total + self.shift_seq(total, sign * by)
            by *= 2
        return total - x


def feature(inputs, table):
    logits = jnp.einsum("nhd,hde->nhe", inputs, table, preferred_element_type=F32)
    phi = jnp.concatenate([jax.nn.softmax(logits, -1), jax.nn.softmax(-logits, -1)], -1)
    return logits, phi.astype(BF16)


def feature_back(logits, grad_phi):
    half = logits.shape[-1]
    plus = jax.nn.softmax(logits, -1)
    minus = jax.nn.softmax(-logits, -1)
    grad_plus = grad_phi[..., :half]
    grad_minus = grad_phi[..., half:]
    inner = plus * (grad_plus - jnp.sum(plus * grad_plus, -1, keepdims=True))
    outer = minus * (grad_minus - jnp.sum(minus * grad_minus, -1, keepdims=True))
    return (inner - outer).astype(BF16)


def local(
    tokens,
    gain_one,
    query_weight,
    key_weight,
    value_weight,
    query_down,
    query_up,
    key_down,
    key_up,
    value_down,
    value_up,
    query_map,
    key_map,
    output_weight,
    output_down,
    output_up,
    gain_two,
    gate_weight,
    up_weight,
    down_weight,
    start_mask,
    cotangent,
):
    grid = Grid()
    rows = tokens.shape[0]
    rank = query_down.shape[1]
    hd = key_map.shape[-1]
    hk = key_map.shape[0]
    hq = query_map.shape[0]
    group = hq // hk
    scale = hd**-0.5
    offset = grid.s * rows
    positions = offset + jnp.arange(rows, dtype=jnp.int32)
    starts = jnp.where(start_mask == 1, positions, jnp.int32(-1))
    earlier = jnp.arange(rows)[:, None] <= jnp.arange(rows)[None, :]
    opened = jnp.max(jnp.where(earlier, starts[:, None], jnp.int32(-1)), 0)
    last_reset = jnp.max(starts[: rows - WIN])
    ext_pos = offset - WIN + jnp.arange(rows + WIN, dtype=jnp.int32)
    rows_index = jnp.arange(rows, dtype=jnp.int32)[:, None]
    cols_index = jnp.arange(rows + WIN, dtype=jnp.int32)[None, :]
    same_doc = ext_pos[None, :] >= opened[:, None]
    win_mask = ((cols_index > rows_index) & (cols_index <= rows_index + WIN) & same_doc).astype(F32)
    lin_mask = ((cols_index <= rows_index) & same_doc).astype(F32)
    carry_on = (opened < offset - WIN).astype(F32)
    key_keep = ((jnp.arange(rows + WIN) < rows) & (ext_pos >= last_reset)).astype(F32)

    g1 = gain_one.astype(F32)
    g2 = gain_two.astype(F32)
    stream = tokens.astype(F32)
    rms_one = lax.rsqrt(jnp.mean(stream * stream, -1, keepdims=True) + EPSILON)
    normed_one = (stream * rms_one * g1).astype(BF16)
    qup, kup, vup = (u.reshape(rank, -1) for u in (query_up, key_up, value_up))
    weight_qkv = jnp.concatenate(
        [
            (query_weight.astype(F32) + dot(query_down, qup)).astype(BF16),
            (key_weight.astype(F32) + dot(key_down, kup)).astype(BF16),
            (value_weight.astype(F32) + dot(value_down, vup)).astype(BF16),
        ],
        1,
    )
    qw, kw = hq * hd, hk * hd
    low_f32 = dot(normed_one, jnp.concatenate([query_down, key_down, value_down], 1))
    low_all = low_f32.astype(BF16)
    low_rest = (low_f32 - low_all.astype(F32)).astype(BF16)
    up_all = jax.scipy.linalg.block_diag(qup, kup, vup)
    qkv = (
        dot(normed_one, jnp.concatenate([query_weight, key_weight, value_weight], 1))
        + dot(jnp.concatenate([low_all, low_rest], 1), jnp.concatenate([up_all, up_all], 0))
    ).astype(BF16)
    query, key, value = qkv[:, :qw], qkv[:, qw : qw + kw], qkv[:, qw + kw :]
    edge = grid.shift_seq(qkv[rows - WIN :, qw:], 1)
    key_heads = jnp.concatenate([edge[:, :kw], key], 0).reshape(rows + WIN, hk, hd)
    value_heads = jnp.concatenate([edge[:, kw:], value], 0).reshape(rows + WIN, hk, hd)
    query_heads = query.reshape(rows, hq, hd)
    q_logit, q_phi = feature(query_heads, query_map)
    k_logit, k_phi = feature(key_heads, key_map)
    query_grouped = query_heads.reshape(rows, hk, group, hd)
    qphi_grouped = q_phi.reshape(rows, hk, group, 2 * hd)
    weighted = k_phi * key_keep[:, None, None].astype(BF16)
    value_ext = jnp.concatenate([value_heads, jnp.ones((rows + WIN, hk, 1), BF16)], 2)
    state_elem = jnp.einsum("ekf,ekd->kfd", weighted, value_ext, preferred_element_type=F32)
    prior = grid.sum_before(state_elem, 1)
    state_prev, norm_prev = prior[..., :hd], prior[..., hd]
    scores = (
        jnp.einsum("ikgd,ekd->kgie", query_grouped, key_heads, preferred_element_type=F32) * scale
    )
    linear = jnp.einsum("ikgf,ekf->kgie", qphi_grouped, k_phi, preferred_element_type=F32)
    exp_window = jnp.exp(scores) * win_mask
    weight_matrix = exp_window + linear * lin_mask
    qphi_carry = qphi_grouped.astype(F32) * carry_on[:, None, None, None]
    carried = jnp.einsum("ikgf,kfd->kgid", qphi_carry, state_prev, precision=EXACT)
    carried_norm = jnp.einsum("ikgf,kf->kgi", qphi_carry, norm_prev, precision=EXACT)
    totals = jnp.sum(weight_matrix, -1) + carried_norm
    shares = (weight_matrix / totals[..., None]).astype(BF16)
    mixture = (
        jnp.einsum("kgie,ekd->kgid", shares, value_heads, preferred_element_type=F32)
        + carried / totals[..., None]
    )
    heads = jnp.transpose(mixture, (2, 0, 1, 3)).reshape(rows, -1).astype(BF16)

    oup = output_up
    odown = output_down.reshape(-1, rank)
    weight_o = (output_weight.astype(F32) + dot(odown, oup)).astype(BF16)
    attn = grid.reduce_rows(dot(heads, weight_o, BF16))
    resid = grid.share(tokens).astype(F32) + attn
    rms_two = lax.rsqrt(jnp.mean(resid * resid, -1, keepdims=True) + EPSILON)
    normed_two = grid.gather_rows((resid * rms_two * g2).astype(BF16))

    g_hidden = dot_nt(cotangent, down_weight)
    cot_cols = grid.pair_columns(cotangent)
    gate = dot(normed_two, gate_weight)
    up = dot(normed_two, up_weight)
    sig = jax.nn.sigmoid(gate)
    silu = gate * sig
    hidden = (silu * up).astype(BF16)
    grad_down = grid.weight_grad(cot_cols, hidden)
    g_gate = (g_hidden * up * sig * (1.0 + gate * (1.0 - sig))).astype(BF16)
    g_up = (g_hidden * silu).astype(BF16)
    g_two = grid.reduce_rows((dot_nt(g_gate, gate_weight) + dot_nt(g_up, up_weight)).astype(BF16))
    normed_cols = grid.pair_columns(normed_two)
    grad_gate = grid.weight_grad(normed_cols, g_gate)
    grad_up = grid.weight_grad(normed_cols, g_up)
    down = grid.reduce_rows(dot(hidden, down_weight, BF16))
    output = grid.gather_rows((resid + down).astype(BF16))

    norm2_part = jnp.sum(g_two * resid * rms_two, 0)
    s_two = g_two * g2
    g_resid = (
        grid.share(cotangent).astype(F32)
        + rms_two * s_two
        - resid * rms_two**3 * jnp.mean(resid * s_two, -1, keepdims=True)
    )
    g_attn = grid.gather_rows(g_resid.astype(BF16))

    g_heads = dot_nt(g_attn, weight_o, BF16)
    g_attn_cols = grid.pair_columns(g_attn)
    grad_wo = grid.weight_grad(g_attn_cols, heads)
    g_low_o = dot_nt(g_attn, oup, BF16)
    low_o = dot(heads, odown, BF16)
    bo_part = dot_tn(low_o, g_attn)
    ao_part = dot_tn(heads, g_low_o)

    g_mixture = g_heads.reshape(rows, hk, group, hd)
    g_mix_float = jnp.transpose(g_mixture.astype(F32), (1, 2, 0, 3))
    g_share = jnp.einsum("ikgd,ekd->kgie", g_mixture, value_heads, preferred_element_type=F32)
    g_value = jnp.einsum("kgie,ikgd->ekd", shares, g_mixture, preferred_element_type=F32)
    g_total = -(jnp.sum(g_share * weight_matrix, -1) + jnp.sum(g_mix_float * carried, -1)) / (
        totals * totals
    )
    g_weight = g_share / totals[..., None] + g_total[..., None]
    g_carried = g_mix_float / totals[..., None]
    g_scores = (g_weight * exp_window).astype(BF16)
    g_linear = (g_weight * lin_mask).astype(BF16)
    g_query = (
        jnp.einsum("kgie,ekd->ikgd", g_scores, key_heads, preferred_element_type=F32) * scale
    )
    g_key = (
        jnp.einsum("kgie,ikgd->ekd", g_scores, query_grouped, preferred_element_type=F32) * scale
    )
    g_qphi = jnp.einsum("kgie,ekf->ikgf", g_linear, k_phi, preferred_element_type=F32)
    g_carried_ext = jnp.concatenate([g_carried, g_total[..., None]], -1)
    g_qphi = g_qphi + carry_on[:, None, None, None] * (
        jnp.einsum("kgid,kfd->ikgf", g_carried_ext, prior, precision=EXACT)
    )
    g_kphi = jnp.einsum("kgie,ikgf->ekf", g_linear, qphi_grouped, preferred_element_type=F32)
    g_state = jnp.einsum("ikgf,kgid->kfd", qphi_carry, g_carried_ext, precision=EXACT)
    later = grid.sum_before(g_state, -1)
    keep_three = key_keep[:, None, None]
    g_kphi = g_kphi + keep_three * jnp.einsum(
        "kfd,ekd->ekf", later, value_ext.astype(F32), precision=EXACT
    )
    g_value = g_value + keep_three * jnp.einsum(
        "ekf,kfd->ekd", k_phi.astype(F32), later[..., :hd], precision=EXACT
    )
    back_rows = jnp.concatenate(
        [
            g_key[:WIN].reshape(WIN, -1),
            g_value[:WIN].reshape(WIN, -1),
            g_kphi[:WIN].reshape(WIN, -1),
        ],
        1,
    )
    back = grid.shift_seq(back_rows.astype(BF16), -1).astype(F32)
    back = jnp.concatenate([jnp.zeros((rows - WIN, back.shape[1]), F32), back], 0)
    g_kphi_own = g_kphi[WIN:] + back[:, 2 * kw :].reshape(rows, hk, 2 * hd)
    gq_logit = feature_back(q_logit, g_qphi.reshape(rows, hq, 2 * hd))
    g_q = (
        g_query.reshape(rows, -1)
        + jnp.einsum("nhe,hde->nhd", gq_logit, query_map, preferred_element_type=F32).reshape(
            rows, -1
        )
    ).astype(BF16)
    featq_part = jnp.einsum("nhd,nhe->hde", query_heads, gq_logit, preferred_element_type=F32)
    gk_logit = feature_back(k_logit[WIN:], g_kphi_own)
    g_k = (
        g_key[WIN:].reshape(rows, -1)
        + back[:, :kw]
        + jnp.einsum("nhe,hde->nhd", gk_logit, key_map, preferred_element_type=F32).reshape(
            rows, -1
        )
    ).astype(BF16)
    featk_part = jnp.einsum("nhd,nhe->hde", key_heads[WIN:], gk_logit, preferred_element_type=F32)
    g_v = (g_value[WIN:].reshape(rows, -1) + back[:, kw : 2 * kw]).astype(BF16)

    g_qkv = jnp.concatenate([g_q, g_k, g_v], 1)
    g_one = grid.reduce_rows(dot_nt(g_qkv, weight_qkv, BF16))
    grad_qkv = grid.weight_grad(grid.pair_columns(normed_one), g_qkv)
    g_low = jnp.concatenate([dot_nt(g_q, qup, BF16), dot_nt(g_k, kup, BF16), dot_nt(g_v, vup, BF16)], 1)
    a_part = dot_tn(normed_one, g_low)
    bq_part = dot_tn(low_all[:, :rank], g_q)
    bk_part = dot_tn(low_all[:, rank : 2 * rank], g_k)
    bv_part = dot_tn(low_all[:, 2 * rank :], g_v)
    stream_share = grid.share(tokens).astype(F32)
    rms_share = grid.share(rms_one)
    norm1_part = jnp.sum(g_one * stream_share * rms_share, 0)
    s_one = g_one * g1
    grad_tokens = (
        g_resid
        + rms_share * s_one
        - stream_share * rms_share**3 * jnp.mean(stream_share * s_one, -1, keepdims=True)
    )
    grad_tokens = grid.gather_rows(grad_tokens.astype(BF16)).astype(F32)

    n = grid.seq

    def blocks(x, dim):
        shape = x.shape
        x = x.reshape(shape[:dim] + (n, shape[dim] // n) + shape[dim + 1 :])
        return jnp.moveaxis(x, dim, 0).reshape(n, -1)

    both = [(norm1_part, 0), (norm2_part, 0), (a_part, 0), (bo_part, 1)]
    own = [
        (bq_part.reshape(query_up.shape), 2),
        (bk_part.reshape(key_up.shape), 2),
        (bv_part.reshape(value_up.shape), 2),
        (featq_part, 1),
        (featk_part, 1),
        (ao_part.reshape(output_down.shape), 1),
    ]
    cut = [blocks(x, d) for x, d in both + own]
    summed = grid.scatter_blocks(jnp.concatenate(cut, 1))
    n_both = sum(c.shape[1] for c in cut[: len(both)])
    flat = jnp.concatenate([grid.sum_kv(summed[:n_both].astype(BF16)), summed[n_both:]])
    done = []
    at = 0
    for x, d in both + own:
        shape = list(x.shape)
        shape[d] //= n
        size = x.size // n
        done.append(flat[at : at + size].reshape(shape))
        at += size
    norm1, norm2, grad_a, grad_bo, bq, bk, bv, featq, featk, grad_ao = done
    return (
        output,
        grad_tokens,
        norm1,
        grad_qkv[:, :qw],
        grad_qkv[:, qw : qw + kw],
        grad_qkv[:, qw + kw :],
        grad_a[:, :rank],
        bq,
        grad_a[:, rank : 2 * rank],
        bk,
        grad_a[:, 2 * rank :],
        bv,
        featq,
        featk,
        grad_wo.T,
        grad_ao,
        grad_bo,
        norm2,
        grad_gate,
        grad_up,
        grad_down.T,
    )


def solution(mesh):
    placed = (
        P("seq", None),
        P(),
        P(None, "kv"),
        P(None, "kv"),
        P(None, "kv"),
        P(),
        P(None, "kv", None),
        P(),
        P(None, "kv", None),
        P(),
        P(None, "kv", None),
        P("kv", None, None),
        P("kv", None, None),
        P("kv", None),
        P("kv", None, None),
        P(),
        P(),
        P(None, "kv"),
        P(None, "kv"),
        P("kv", None),
        P("seq"),
        P("seq", None),
    )
    return jax.shard_map(
        local,
        mesh=mesh,
        in_specs=placed,
        out_specs=(
            P("seq", None),
            P("seq", None),
            P("seq"),
            P("seq", "kv"),
            P("seq", "kv"),
            P("seq", "kv"),
            P("seq", None),
            P(None, "kv", "seq"),
            P("seq", None),
            P(None, "kv", "seq"),
            P("seq", None),
            P(None, "kv", "seq"),
            P("kv", "seq", None),
            P("kv", "seq", None),
            P("kv", "seq"),
            P("kv", "seq", None),
            P(None, "seq"),
            P("seq"),
            P("seq", "kv"),
            P("seq", "kv"),
            P("kv", "seq"),
        ),
        check_vma=False,
    )
```

```python
import jax
import jax.numpy as jnp
from jax import lax
from jax.experimental import pallas as pl
from jax.experimental.pallas import tpu as pltpu
from jax.sharding import PartitionSpec as P

WIN = 64
CHUNK = 128
ANY = pl.BlockSpec(memory_space=pl.ANY)
COST = pl.CostEstimate(flops=1, bytes_accessed=1, transcendentals=0)
EPSILON = 1e-05
EXACT = lax.Precision.HIGHEST
F32 = jnp.float32
BF16 = jnp.bfloat16


def dot(a, b, out=F32):
    return jnp.dot(a, b, preferred_element_type=F32).astype(out)


def dot_nt(a, b, out=F32):
    return lax.dot_general(a, b, (((1,), (1,)), ((), ())), preferred_element_type=F32).astype(out)


def dot_tn(a, b, out=F32):
    return lax.dot_general(a, b, (((0,), (0,)), ((), ())), preferred_element_type=F32).astype(out)


def dot_tt(a, b, out=F32):
    return lax.dot_general(a, b, (((0,), (1,)), ((), ())), preferred_element_type=F32).astype(out)


def tie(*xs):
    return lax.optimization_barrier(xs)


def add(terms):
    total = terms[0].astype(F32)
    for t in terms[1:]:
        total = total + t.astype(F32)
    return total


def take(x, i):
    return lax.dynamic_index_in_dim(x, i, 0, False)


class Grid:
    def __init__(self):
        self.kv = lax.axis_size("kv")
        self.seq = lax.axis_size("seq")
        self.outer = self.kv // 2
        self.line = self.seq // 2
        k = lax.axis_index("kv")
        s = lax.axis_index("seq")
        self.core, self.y = k % 2, k // 2
        self.x, self.z = s % 2, s // 2
        self.s = s
        self.core_swap = [(i, i ^ 1) for i in range(self.kv)]
        self.x_swap = [(i, i ^ 1) for i in range(self.seq)]
        self.z_groups = [[2 * z + x for z in range(self.line)] for x in range(2)]

    def y_shift(self, j):
        m = self.outer
        return [(y * 2 + c, (y + j) % m * 2 + c) for y in range(m) for c in range(2)]

    def own_rows(self, x, parts):
        rows, width = x.shape
        cut = x.reshape(parts, 2, rows // (2 * parts), width)
        return lax.dynamic_index_in_dim(cut, self.core, 1, False).reshape(rows // 2, width)

    def other_rows(self, x, parts):
        rows, width = x.shape
        cut = x.reshape(parts, 2, rows // (2 * parts), width)
        return lax.dynamic_index_in_dim(cut, 1 - self.core, 1, False).reshape(rows // 2, width)

    def across_cores(self, x):
        return lax.ppermute(x, "kv", self.core_swap)

    def core_sum(self, part, parts):
        got = self.across_cores(self.other_rows(part, parts))
        return (self.own_rows(part, parts).astype(F32) + got.astype(F32)).astype(BF16)

    def outer_terms(self, half):
        terms = [half] + [lax.ppermute(half, "kv", self.y_shift(j)) for j in range(1, self.outer)]
        if self.outer == 2:
            return terms
        stack = jnp.stack(terms)
        return [take(stack, (self.y - i) % self.outer) for i in range(self.outer)]

    def gather_rows(self, own, parts):
        other = self.across_cores(own)
        first = self.core == 0
        shape = (parts, 1, own.shape[0] // parts, own.shape[1])
        low = jnp.where(first, own, other).reshape(shape)
        high = jnp.where(first, other, own).reshape(shape)
        return jnp.concatenate([low, high], 1).reshape(2 * own.shape[0], own.shape[1])

    def sum_kv(self, x):
        x = x + lax.ppermute(x, "kv", self.core_swap).astype(F32)
        total = x
        for j in range(1, self.outer):
            total = total + lax.ppermute(x, "kv", self.y_shift(j))
        return total

    def line_scatter(self, part):
        return lax.psum_scatter(
            part, "seq", scatter_dimension=0, tiled=True, axis_index_groups=self.z_groups
        )

    def scatter_blocks(self, blocks):
        cut = blocks.reshape(self.line, 2, -1)
        other = lax.dynamic_index_in_dim(cut, 1 - self.x, 1, False).astype(BF16)
        own = lax.dynamic_index_in_dim(cut, self.x, 1, False)
        part = own + lax.ppermute(other, "seq", self.x_swap).astype(F32)
        total = take(part, self.z)
        m = self.line
        for j in range(1, m):
            pairs = [(z * 2 + x, (z + j) % m * 2 + x) for z in range(m) for x in range(2)]
            out = take(part, (self.z + j) % m).astype(BF16)
            total = total + lax.ppermute(out, "seq", pairs).astype(F32)
        return total

    def shift_seq(self, x, by):
        n = self.seq
        return lax.ppermute(x, "seq", [(i, i + by) for i in range(n) if 0 <= i + by < n])

    def sum_before(self, x, sign):
        near = self.shift_seq(x, sign)
        total = x + near
        by = 2
        while by < self.seq:
            total = total + self.shift_seq(total, sign * by)
            by *= 2
        return total - x, near


def softmax_pair(logits):
    top = jnp.exp(logits - jnp.max(logits, 0, keepdims=True))
    low = jnp.exp(jnp.min(logits, 0, keepdims=True) - logits)
    return top * (1.0 / jnp.sum(top, 0, keepdims=True)), low * (1.0 / jnp.sum(low, 0, keepdims=True))


def softmax_pair_back(p, n, grad):
    hd = p.shape[0]
    up, un = p * grad[:hd], n * grad[hd:]
    return up - p * jnp.sum(up, 0, keepdims=True) - (un - n * jnp.sum(un, 0, keepdims=True))


def halves(x):
    top = x.astype(BF16)
    return top, (x - top.astype(F32)).astype(BF16)


def dot2(x, b):
    top, rest = halves(x)
    return dot(top, b) + dot(rest, b)


def value_rows(v, keep):
    hd, n = v.shape
    ones = (lax.broadcasted_iota(jnp.int32, (hd, n), 0) == 0).astype(F32)
    return (jnp.concatenate([v.astype(F32), ones], 0) * keep).astype(BF16)


def key_kernel(kv_ref, map_ref, keep_ref, phi_cols_ref, phi_ref, k_ref, v_ref, state_ref):
    hk, hd = map_ref.shape[:2]
    for g in range(hk):
        k = kv_ref[g * hd : (g + 1) * hd, :]
        v = kv_ref[(hk + g) * hd : (hk + g + 1) * hd, :]
        p, n = softmax_pair(dot(map_ref[g], k))
        phi = jnp.concatenate([p, n], 0)
        phi_cols_ref[g] = phi.astype(BF16)
        phi_ref[g] = phi.T.astype(BF16)
        kv = jnp.concatenate([k, v], 0).astype(F32).T
        k_ref[g] = kv[:, :hd].astype(BF16)
        v_ref[g] = kv[:, hd:].astype(BF16)
        state_ref[g] = dot_nt(value_rows(v, keep_ref[...]), phi.astype(BF16))


def masks(open_ref, base):
    shape = (2 * CHUNK, CHUNK)
    a = lax.broadcasted_iota(jnp.int32, shape, 0)
    b = lax.broadcasted_iota(jnp.int32, shape, 1)
    start = open_ref[:, pl.ds(base, CHUNK)] - base
    doc = a >= start
    near = a > b + (CHUNK - WIN)
    return doc & near & (a <= b + CHUNK), doc & ~near, (start < 0).astype(F32)


def lanes(parts):
    return jnp.concatenate(parts, 1)


def attend_kernel(
    q_ref, kv_ref, phi_cols_ref, phi_ref, k_ref, map_ref, prior_ref, open_ref, keep_ref, cont_ref,
    heads_ref, total_ref, states_ref, state,
):
    hk, hd = phi_ref.shape[0], map_ref.shape[1]
    hq = map_ref.shape[0]
    group = hq // hk
    scale = hd**-0.5
    state[...] = prior_ref[...]

    def chunk(i, _):
        base = pl.multiple_of(i * CHUNK, CHUNK)
        here = pl.ds(base, CHUNK)
        keys = pl.ds(base, 2 * CHUNK)
        win, lin, far = masks(open_ref, base)
        for g in range(hk):
            q = [q_ref[h * hd : (h + 1) * hd, here] for h in range(g * group, (g + 1) * group)]
            phi = []
            for j in range(group):
                p, n = softmax_pair(dot(map_ref[g * group + j], q[j]))
                phi.append(jnp.concatenate([p, n], 0).astype(BF16))
            phi4 = lanes(phi)
            past = state[g]
            states_ref[i, g] = past
            scores = dot(k_ref[g, keys, :], lanes(q)) * scale
            linear = dot(phi_ref[g, keys, :], phi4)
            carried = dot2(past[: hd + 8], phi4)
            weights = []
            totals = []
            for j in range(group):
                cut = slice(j * CHUNK, (j + 1) * CHUNK)
                w = jnp.where(win, jnp.exp(scores[:, cut]), 0.0) + jnp.where(lin, linear[:, cut], 0.0)
                weights.append(w.astype(BF16))
                totals.append(jnp.sum(w, 0, keepdims=True) + far * carried[hd : hd + 1, cut])
            v = kv_ref[(hk + g) * hd : (hk + g + 1) * hd, keys]
            mixed = dot(v, lanes(weights))
            for j in range(group):
                cut = slice(j * CHUNK, (j + 1) * CHUNK)
                h = g * group + j
                out = (mixed[:, cut] + far * carried[:hd, cut]) * (1.0 / totals[j])
                heads_ref[h * hd : (h + 1) * hd, here] = out.astype(BF16)
                total_ref[h : h + 1, here] = totals[j]
            own = value_rows(kv_ref[(hk + g) * hd : (hk + g + 1) * hd, here], keep_ref[:, here])
            state[g] = cont_ref[i] * past + dot_nt(own, phi_cols_ref[g, :, here])
        return 0

    lax.fori_loop(0, heads_ref.shape[1] // CHUNK, chunk, 0)


def attend_back_kernel(
    q_ref, kv_ref, phi_cols_ref, phi_ref, k_ref, v_ref, map_ref, map_t_ref, states_ref, heads_ref,
    total_ref, g_ref, open_ref, keep_ref, cont_ref,
    gq_ref, feat_ref, gk_ref, gv_ref, gphi_ref, first_ref, gl_ref, grad_t,
):
    hk, hd = phi_ref.shape[0], map_ref.shape[1]
    hq = map_ref.shape[0]
    group = hq // hk
    scale = hd**-0.5
    count = heads_ref.shape[1] // CHUNK
    first_ref[...] = jnp.zeros_like(first_ref)
    grad_t[...] = jnp.zeros_like(grad_t)
    gk_ref[...] = jnp.zeros_like(gk_ref)
    gv_ref[...] = jnp.zeros_like(gv_ref)
    gphi_ref[...] = jnp.zeros_like(gphi_ref)

    def chunk(step, _):
        i = count - 1 - step
        base = pl.multiple_of(i * CHUNK, CHUNK)
        here = pl.ds(base, CHUNK)
        keys = pl.ds(base, 2 * CHUNK)
        win, lin, far = masks(open_ref, base)
        for g in range(hk):
            rows = [slice(h * hd, (h + 1) * hd) for h in range(g * group, (g + 1) * group)]
            key_rows = slice(g * hd, (g + 1) * hd)
            value_row = slice((hk + g) * hd, (hk + g + 1) * hd)
            q4 = lanes([q_ref[r, here] for r in rows])
            g4 = lanes([g_ref[r, here] for r in rows])
            pairs = [softmax_pair(dot(map_ref[g * group + j], q_ref[rows[j], here])) for j in range(group)]
            phi = [jnp.concatenate([p, n], 0) for p, n in pairs]
            phi4 = lanes([x.astype(BF16) for x in phi])
            scores = dot(k_ref[g, keys, :], q4) * scale
            linear = dot(phi_ref[g, keys, :], phi4)
            g_w = dot(v_ref[g, keys, :], g4)
            shares, g_scores, g_linear, g_ext = [], [], [], []
            for j in range(group):
                cut = slice(j * CHUNK, (j + 1) * CHUNK)
                h = g * group + j
                inv = 1.0 / total_ref[h : h + 1, here]
                g_here = g_ref[rows[j], here].astype(F32)
                g_total = -inv * jnp.sum(g_here * heads_ref[rows[j], here].astype(F32), 0, keepdims=True)
                ex = jnp.where(win, jnp.exp(scores[:, cut]), 0.0)
                w = ex + jnp.where(lin, linear[:, cut], 0.0)
                shares.append((w * inv).astype(BF16))
                g_weight = g_w[:, cut] * inv + g_total
                g_scores.append((g_weight * ex).astype(BF16))
                g_linear.append(jnp.where(lin, g_weight, 0.0).astype(BF16))
                row = lax.broadcasted_iota(jnp.int32, (hd, CHUNK), 0) == 0
                g_ext.append(
                    (jnp.concatenate([g_here * inv, jnp.where(row, g_total, 0.0)], 0) * far).astype(BF16)
                )
            shares, g_scores, g_linear, g_ext = map(lanes, (shares, g_scores, g_linear, g_ext))
            gv_ref[key_rows, keys] += dot_nt(g4, shares)
            gk_ref[key_rows, keys] += dot_nt(q4, g_scores) * scale
            gphi_ref[g, :, keys] += dot_nt(phi4, g_linear)
            g_query = dot(kv_ref[key_rows, keys], g_scores) * scale
            past = states_ref[i, g].T
            g_phi = dot(phi_cols_ref[g, :, keys], g_linear) + dot2(past, g_ext)
            for j in range(group):
                cut = slice(j * CHUNK, (j + 1) * CHUNK)
                gl = softmax_pair_back(*pairs[j], g_phi[:, cut]).astype(BF16)
                gl_ref[rows[j], here] = gl
                gq = g_query[:, cut] + dot(map_t_ref[g * group + j], gl)
                gq_ref[rows[j], here] = gq.astype(BF16)
            keep = keep_ref[:, here]
            own = value_rows(kv_ref[value_row, here], keep)
            gphi_ref[g, :, here] += dot2(grad_t[g], own)
            gv_ref[key_rows, here] += dot2(first_ref[g, :hd, :], phi_cols_ref[g, :, here]) * keep
            cont = cont_ref[i]
            first_ref[g] = cont * first_ref[g] + dot_nt(g_ext, phi4)
            grad_t[g] = cont * grad_t[g] + dot_nt(phi4, g_ext)
        return 0

    lax.fori_loop(0, count, chunk, 0)
    for h in range(hq):
        r = slice(h * hd, (h + 1) * hd)
        feat_ref[h] = dot_nt(q_ref[r, :], gl_ref[r, :])


def key_back_kernel(
    kv_ref, phi_cols_ref, map_ref, map_t_ref, gk_ref, gv_ref, gphi_ref, edge_ref, later_ref, last_ref,
    keep_ref, g_ref, feat_ref,
):
    hk, hd = map_ref.shape[:2]
    n = kv_ref.shape[1]
    cut = n - CHUNK

    def joined(own, edge):
        return jnp.concatenate([own[:, : cut - CHUNK], own[:, cut - CHUNK :] + edge.astype(F32)], 1)

    for g in range(hk):
        key_rows = slice(g * hd, (g + 1) * hd)
        k = kv_ref[key_rows, CHUNK:]
        v = kv_ref[(hk + g) * hd : (hk + g + 1) * hd, CHUNK:]
        keep = keep_ref[:, CHUNK:]
        phi = phi_cols_ref[g, :, CHUNK:]
        own = value_rows(v, keep)
        one = value_rows(v[:, cut - CHUNK :], jnp.ones((1, CHUNK), F32))
        later, last = later_ref[g], last_ref[g]
        g_phi = gphi_ref[g, :, CHUNK:] + lanes(
            [dot2(later.T, own[:, : cut - CHUNK]), dot2(last.T, one)]
        )
        g_phi = joined(g_phi, edge_ref[2 * hk * hd + g * 2 * hd : 2 * hk * hd + (g + 1) * 2 * hd, :])
        g_v = gv_ref[key_rows, CHUNK:] + lanes(
            [
                dot2(later[:hd], phi[:, : cut - CHUNK]) * keep[:, : cut - CHUNK],
                dot2(last[:hd], phi[:, cut - CHUNK :]),
            ]
        )
        g_v = joined(g_v, edge_ref[(hk + g) * hd : (hk + g + 1) * hd, :])
        g_ref[(hk + g) * hd : (hk + g + 1) * hd, :] = g_v.astype(BF16)
        p, q = softmax_pair(dot(map_ref[g], k))
        gl = softmax_pair_back(p, q, g_phi).astype(BF16)
        g_k = joined(gk_ref[key_rows, CHUNK:], edge_ref[key_rows, :]) + dot(map_t_ref[g], gl)
        g_ref[key_rows, :] = g_k.astype(BF16)
        feat_ref[g] = dot_nt(k, gl)


def call(kernel, outs, args, scratch=(), smem=(), after=()):
    count = len(args)
    vmem = pl.BlockSpec(memory_space=pltpu.VMEM)
    specs = [pl.BlockSpec(memory_space=pltpu.SMEM) if i in smem else vmem for i in range(len(args))]
    return pl.pallas_call(
        lambda *refs: kernel(*refs[:count], *refs[count + len(after) :]),
        out_shape=[jax.ShapeDtypeStruct(s, d) for s, d in outs],
        in_specs=specs + [ANY] * len(after),
        out_specs=[vmem] * len(outs),
        scratch_shapes=[pltpu.VMEM(s, d) for s, d in scratch],
        compiler_params=pltpu.CompilerParams(vmem_limit_bytes=48 * 2**20),
        cost_estimate=COST,
    )(*args, *after)


def project_kernel(
    x_ref, gain_ref, wq_ref, wk_ref, wv_ref, down_ref, up_ref, normed_ref, q_ref, kv_ref, low_ref
):
    x = x_ref[...].astype(F32)
    rms = lax.rsqrt(jnp.mean(x * x, -1, keepdims=True) + EPSILON)
    normed = (x * rms * gain_ref[...].astype(F32)).astype(BF16)
    normed_ref[...] = normed
    low, rest = halves(dot(normed, down_ref[...]))
    low_ref[...] = low
    qw, kw = wq_ref.shape[1], wk_ref.shape[1]

    def rows(weight, at, width):
        up = up_ref[:, at : at + width]
        return (dot(normed, weight[...]) + dot(low, up) + dot(rest, up)).T.astype(BF16)

    kv_ref[:kw, :] = rows(wk_ref, qw, kw)
    kv_ref[kw:, :] = rows(wv_ref, qw + kw, kw)
    q_ref[...] = rows(wq_ref, 0, qw)


def project(tokens, gain, wq, wk, wv, down, up, tile=256):
    t, d = tokens.shape
    qw, kw = wq.shape[1], wk.shape[1]
    whole = lambda a: pl.BlockSpec(a.shape, lambda i: (0,) * a.ndim)
    row = lambda w: pl.BlockSpec((tile, w), lambda i: (i, 0))
    col = lambda h: pl.BlockSpec((h, tile), lambda i: (0, i))
    gain = gain[None]
    return pl.pallas_call(
        project_kernel,
        grid=(t // tile,),
        in_specs=[row(d)] + [whole(a) for a in (gain, wq, wk, wv, down, up)],
        out_specs=[row(d), col(qw), col(2 * kw), row(down.shape[1])],
        out_shape=[
            jax.ShapeDtypeStruct((t, d), BF16),
            jax.ShapeDtypeStruct((qw, t), BF16),
            jax.ShapeDtypeStruct((2 * kw, t), BF16),
            jax.ShapeDtypeStruct((t, down.shape[1]), BF16),
        ],
        compiler_params=pltpu.CompilerParams(vmem_limit_bytes=48 * 2**20),
        cost_estimate=COST,
    )(tokens, gain, wq, wk, wv, down, up)


def matmul_kernel(product, pairs, out_ref):
    sub = min(256, out_ref.shape[0])
    for r in range(0, out_ref.shape[0], sub):
        total = None
        for a_ref, b_ref in pairs:
            term = product(a_ref[r : r + sub, :], b_ref[...])
            total = term if total is None else total + term
        out_ref[r : r + sub, :] = total.astype(out_ref.dtype)


def matmul(pairs, transposed, out, tile=512, after=()):
    rows = pairs[0][0].shape[0]
    width = pairs[0][1].shape[0 if transposed else 1]
    product = dot_nt if transposed else dot
    specs, args = [], []
    for a, b in pairs:
        specs.append(pl.BlockSpec(a.shape, lambda i: (0, 0)))
        if transposed:
            specs.append(pl.BlockSpec((tile, b.shape[1]), lambda i: (i, 0)))
        else:
            specs.append(pl.BlockSpec((b.shape[0], tile), lambda i: (0, i)))
        args += [a, b]

    def kernel(*refs):
        used = refs[: 2 * len(pairs)]
        matmul_kernel(product, list(zip(used[::2], used[1::2])), refs[-1])

    return pl.pallas_call(
        kernel,
        grid=(width // tile,),
        in_specs=specs + [ANY] * len(after),
        out_specs=pl.BlockSpec((rows, tile), lambda i: (0, i)),
        out_shape=jax.ShapeDtypeStruct((rows, width), out),
        compiler_params=pltpu.CompilerParams(vmem_limit_bytes=56 * 2**20),
        cost_estimate=COST,
    )(*args, *after)


def grad_block(line, select, a, b, product, piece=(0, 1), got=None, after=()):
    rows, width = a.shape
    block = width // (2 * line)
    if product is dot_tt:
        n = b.shape[0]
        b_spec = pl.BlockSpec(b.shape, lambda j, s: (0, 0))
    else:
        n = b.shape[1] // piece[1]
        b_spec = pl.BlockSpec((rows, n), lambda j, s: (0, piece[0]))

    def kernel(sel_ref, a_ref, b_ref, *refs):
        value = product(a_ref[...], b_ref[...])
        if got is not None:
            value = value + refs[0][...].astype(F32)
        refs[-1][...] = value.astype(BF16)

    spec = pl.BlockSpec((block, n), lambda j, s: (j, 0))
    more = [] if got is None else [got]
    return pl.pallas_call(
        kernel,
        grid_spec=pltpu.PrefetchScalarGridSpec(
            num_scalar_prefetch=1,
            grid=(line,),
            in_specs=[
                pl.BlockSpec((rows, block), lambda j, s: (0, 2 * j + s[0])),
                b_spec,
            ]
            + [spec] * len(more)
            + [ANY] * len(after),
            out_specs=spec,
        ),
        out_shape=jax.ShapeDtypeStruct((line * block, n), BF16),
        compiler_params=pltpu.CompilerParams(vmem_limit_bytes=48 * 2**20),
        cost_estimate=COST,
    )(select, a, b, *more, *after)


def gated_kernel(core_ref, own_ref, other_ref, wg_ref, wu_ref, gh_ref, *refs):
    normed_ref, hidden_ref, gate_ref, up_ref = refs[-4:]
    half = own_ref.shape[0]

    @pl.when(pl.program_id(0) == 0)
    def _():
        first = core_ref[0] == 0

        @pl.when(first)
        def _():
            normed_ref[:half, :] = own_ref[...]
            normed_ref[half:, :] = other_ref[...]

        @pl.when(jnp.logical_not(first))
        def _():
            normed_ref[:half, :] = other_ref[...]
            normed_ref[half:, :] = own_ref[...]

    for r in range(0, 2 * half, half):
        cut = slice(r, r + half)
        x = normed_ref[cut, :]
        gate = dot(x, wg_ref[...])
        up = dot(x, wu_ref[...])
        sig = 1.0 / (1.0 + jnp.exp(-gate))
        silu = gate * sig
        hidden_ref[cut, :] = (silu * up).astype(BF16)
        g = gh_ref[cut, :].astype(F32)
        gate_ref[cut, :] = (g * up * (sig + silu * (1.0 - sig))).astype(BF16)
        up_ref[cut, :] = (g * silu).astype(BF16)


def gated(c, rows, core, own, other, wg, wu, gh, held, tile=512):
    half, d = own.shape
    f = wg.shape[1]
    here = pl.BlockSpec((2 * half, tile), lambda i, s: (c, i))
    part = pl.BlockSpec((2 * half, tile), lambda i, s: (0, i))
    held_specs = [pl.BlockSpec(memory_space=pl.ANY)] * len(held)
    shapes = [jax.ShapeDtypeStruct((rows, d), BF16)] + [jax.ShapeDtypeStruct((rows, f), BF16)] * 3
    return pl.pallas_call(
        gated_kernel,
        grid_spec=pltpu.PrefetchScalarGridSpec(
            num_scalar_prefetch=1,
            grid=(f // tile,),
            in_specs=[
                pl.BlockSpec((half, d), lambda i, s: (0, 0)),
                pl.BlockSpec((half, d), lambda i, s: (0, 0)),
                pl.BlockSpec((d, tile), lambda i, s: (0, i)),
                pl.BlockSpec((d, tile), lambda i, s: (0, i)),
                part,
            ]
            + held_specs,
            out_specs=[pl.BlockSpec((2 * half, d), lambda i, s: (c, 0)), here, here, here],
        ),
        out_shape=shapes,
        input_output_aliases={6 + i: i for i in range(len(held))},
        compiler_params=pltpu.CompilerParams(vmem_limit_bytes=56 * 2**20),
        cost_estimate=COST,
    )(core, own, other, wg, wu, gh, *held)


def local(
    tokens,
    gain_one,
    query_weight,
    key_weight,
    value_weight,
    query_down,
    query_up,
    key_down,
    key_up,
    value_down,
    value_up,
    query_map,
    key_map,
    output_weight,
    output_down,
    output_up,
    gain_two,
    gate_weight,
    up_weight,
    down_weight,
    start_mask,
    cotangent,
):
    grid = Grid()
    rows = tokens.shape[0]
    rank = query_down.shape[1]
    hd = key_map.shape[-1]
    hk = key_map.shape[0]
    hq = query_map.shape[0]
    group = hq // hk
    count = rows // CHUNK
    length = rows + CHUNK
    index = jnp.arange(rows, dtype=jnp.int32)
    starts = jnp.where(start_mask == 1, index + CHUNK, jnp.int32(-1))
    opened = jnp.max(jnp.where(index[:, None] <= index[None, :], starts[:, None], jnp.int32(-1)), 0)
    ends = jnp.concatenate([jnp.full((1,), -1, jnp.int32), opened[CHUNK - 1 : -1 : CHUNK]])
    cont = (ends < jnp.arange(count, dtype=jnp.int32) * CHUNK).astype(F32)
    place = jnp.arange(length, dtype=jnp.int32)
    ends_at = jnp.concatenate([jnp.repeat(ends, CHUNK), jnp.full((CHUNK,), length, jnp.int32)])
    keep = (place >= ends_at).astype(F32)[None]
    keep_all = ((place >= ends[count - 1]) & (place < rows)).astype(F32)[None]
    opened = opened[None]

    g1 = gain_one.astype(F32)
    g2 = gain_two.astype(F32)
    qup, kup, vup = (u.reshape(rank, -1) for u in (query_up, key_up, value_up))
    qw, kw = hq * hd, hk * hd
    wide = 128 - 3 * rank
    up_all = jnp.pad(jax.scipy.linalg.block_diag(qup, kup, vup), ((0, wide), (0, 0)))
    down_all = jnp.pad(jnp.concatenate([query_down, key_down, value_down], 1), ((0, 0), (0, wide)))
    normed_one, query, kv, low_all = project(
        tokens, gain_one, query_weight, key_weight, value_weight, down_all, up_all
    )
    edge = grid.shift_seq(kv[:, rows - CHUNK :], 1)
    kv = jnp.concatenate([edge, kv], 1)

    query_map_t = jnp.swapaxes(query_map, 1, 2)
    key_map_t = jnp.swapaxes(key_map, 1, 2)
    phi_dim = 2 * hd
    phi_cols, phi, key, value, state = call(
        key_kernel,
        [
            ((hk, phi_dim, length), BF16),
            ((hk, length, phi_dim), BF16),
            ((hk, length, hd), BF16),
            ((hk, length, hd), BF16),
            ((hk, phi_dim, phi_dim), F32),
        ],
        (kv, key_map_t, keep_all),
    )
    prior, _ = grid.sum_before(state, 1)
    parts = 2
    chunk = rows // parts
    g_hidden = matmul([(cotangent[:chunk], down_weight)], True, F32)
    oup = output_up
    odown = output_down.reshape(-1, rank)
    weight_o = (output_weight.astype(F32) + dot(odown, oup)).astype(BF16)
    prior, g_hidden, weight_o = tie(prior, g_hidden, weight_o)
    heads, totals, states = call(
        attend_kernel,
        [((qw, rows), BF16), ((hq, rows), F32), ((count, hk, phi_dim, phi_dim), F32)],
        (query, kv, phi_cols, phi, key, query_map_t, prior, opened, keep, cont),
        scratch=[((hk, phi_dim, phi_dim), F32)],
        smem=(9,),
    )

    part = [dot_tn(heads[:, c * chunk : (c + 1) * chunk], weight_o, BF16) for c in range(parts)]
    half = [grid.core_sum(p, 1) for p in part]
    own_tokens = [grid.own_rows(tokens[c * chunk : (c + 1) * chunk], 1) for c in range(parts)]
    own_tokens[0], half[1] = tie(own_tokens[0], half[1])
    terms = [grid.outer_terms(h) for h in half]
    held = ()
    resid, rms_two = [], []
    for c in range(parts):
        if c:
            held = list(held)
            terms[c][-1], held[0] = tie(terms[c][-1], held[0])
        r = own_tokens[c].astype(F32) + add(terms[c])
        rms = lax.rsqrt(jnp.mean(r * r, -1, keepdims=True) + EPSILON)
        own = (r * rms * g2).astype(BF16)
        core = grid.core.astype(jnp.int32)[None]
        if c:
            g_hidden = g_rest
        else:
            g_rest = matmul([(cotangent[chunk:], down_weight)], True, F32, after=[own])
        held = gated(
            c, rows, core, own, grid.across_cores(own), gate_weight, up_weight, g_hidden, held
        )
        resid.append(r)
        rms_two.append(rms)
    normed_two, hidden, g_gate, g_up = held
    resid = jnp.concatenate(resid, 0)
    rms_two = jnp.concatenate(rms_two, 0)

    mine = grid.x.astype(jnp.int32)[None]
    yours = 1 - mine

    early, late = (0, 2), (1, 2)

    def to_pair(a, b, product=dot_tn, piece=(0, 1), after=()):
        return grad_block(grid.line, yours, a, b, product, piece, None, after)

    def from_pair(a, b, got, product=dot_tn, piece=(0, 1), after=()):
        return grad_block(grid.line, mine, a, b, product, piece, got, after)

    def swap(x):
        return lax.ppermute(x, "seq", grid.x_swap)

    s_d0 = to_pair(cotangent, hidden, dot_tn, early)
    s_d1 = to_pair(cotangent, hidden, dot_tn, late, [s_d0])
    r_d0, r_d1 = swap(s_d0), swap(s_d1)
    g_two = matmul([(g_gate, gate_weight), (g_up, up_weight)], True, BF16, after=[s_d1])
    half = grid.core_sum(g_two, parts)
    terms = grid.outer_terms(half)
    s_g0 = to_pair(normed_two, g_gate, dot_tn, early, [g_two])
    s_g1 = to_pair(normed_two, g_gate, dot_tn, late, [s_g0])
    r_g0, r_g1 = swap(s_g0), swap(s_g1)
    k_d0 = from_pair(cotangent, hidden, r_d0, dot_tn, early, [s_g1])
    grad_d0 = grid.line_scatter(k_d0)
    s_u0 = to_pair(normed_two, g_up, dot_tn, early, [k_d0])
    s_u1 = to_pair(normed_two, g_up, dot_tn, late, [s_u0])
    r_u0, r_u1 = swap(s_u0), swap(s_u1)
    down = matmul([(hidden, down_weight)], False, BF16, after=[s_u1])
    terms[-1], down = tie(terms[-1], down)

    g_two = add(terms)
    norm2_part = jnp.sum(g_two * resid * rms_two, 0)
    s_two = g_two * g2
    g_resid = (
        grid.own_rows(cotangent, parts).astype(F32)
        + rms_two * s_two
        - resid * rms_two**3 * jnp.mean(resid * s_two, -1, keepdims=True)
    )
    own_attn = g_resid.astype(BF16)
    g_attn = grid.gather_rows(own_attn, parts)
    k_d1 = from_pair(cotangent, hidden, r_d1, dot_tn, late, [own_attn])
    grad_d1 = grid.line_scatter(k_d1)
    half = grid.core_sum(down, parts)
    down_terms = grid.outer_terms(half)
    weight_qkv = jnp.concatenate([query_weight, key_weight, value_weight], 1)
    weight_qkv = (weight_qkv.astype(F32) + dot(down_all, up_all)).astype(BF16)
    g_attn, weight_qkv = tie(g_attn, weight_qkv)

    g_heads = dot_nt(weight_o, g_attn, BF16)
    g_q, featq_part, gk, gv, gphi, first = call(
        attend_back_kernel,
        [
            ((qw, rows), BF16),
            ((hq, hd, hd), F32),
            ((kw, length), F32),
            ((kw, length), F32),
            ((hk, phi_dim, length), F32),
            ((hk, phi_dim, phi_dim), F32),
        ],
        (
            query, kv, phi_cols, phi, key, value, query_map_t, query_map, states, heads,
            totals, g_heads, opened, keep, cont,
        ),
        scratch=[((qw, rows), BF16), ((hk, phi_dim, phi_dim), F32)],
        smem=(14,),
        after=[half, k_d1],
    )
    later, near = grid.sum_before(first, -1)
    back = [gk[:, :CHUNK], gv[:, :CHUNK], gphi[:, :, :CHUNK].reshape(hk * phi_dim, CHUNK)]
    back = grid.shift_seq(jnp.concatenate(back, 0).astype(BF16), -1)
    s_o = to_pair(g_attn, heads, dot_tt, after=[g_q])
    r_o = swap(s_o)
    k_g0 = from_pair(normed_two, g_gate, r_g0, dot_tn, early, [s_o, grad_d0])
    grad_g0 = grid.line_scatter(k_g0)
    g_kv, featk_part = call(
        key_back_kernel,
        [((2 * kw, rows), BF16), ((hk, hd, hd), F32)],
        (kv, phi_cols, key_map_t, key_map, gk, gv, gphi, back, later, later - near, keep_all),
        after=[k_g0],
    )

    g_qkv = jnp.concatenate([g_q, g_kv], 0)
    g_one = dot_tt(g_qkv, weight_qkv, BF16)
    terms = grid.outer_terms(grid.core_sum(g_one, parts))
    s_qkv = to_pair(normed_one, g_qkv, dot_tt, after=[g_one])
    k_g1 = from_pair(normed_two, g_gate, r_g1, dot_tn, late, [s_qkv, grad_d1])
    grad_g1 = grid.line_scatter(k_g1)
    g_low = dot(up_all, g_qkv, BF16)
    a_part = dot(g_low, normed_one)
    b_part = dot_tt(low_all, g_qkv)
    bq_part = b_part[:rank, :qw]
    bk_part = b_part[rank : 2 * rank, qw : qw + kw]
    bv_part = b_part[2 * rank : 3 * rank, qw + kw :]
    g_low_o = dot_nt(g_attn, oup, BF16)
    low_o = dot_tn(odown, heads, BF16)
    bo_part = dot(low_o, g_attn)
    ao_part = dot(heads, g_low_o)
    down_terms[-1], s_qkv = tie(down_terms[-1], s_qkv)
    r_qkv = swap(s_qkv)
    output = grid.gather_rows((resid + add(down_terms)).astype(BF16), parts)
    terms[-1], k_g1, a_part, b_part, bo_part, ao_part, output = tie(
        terms[-1], k_g1, a_part, b_part, bo_part, ao_part, output
    )

    stream = grid.own_rows(tokens, parts).astype(F32)
    rms_one = lax.rsqrt(jnp.mean(stream * stream, -1, keepdims=True) + EPSILON)
    g_one = add(terms)
    norm1_part = jnp.sum(g_one * stream * rms_one, 0)
    s_one = g_one * g1
    own_grad = (
        g_resid
        + rms_one * s_one
        - stream * rms_one**3 * jnp.mean(stream * s_one, -1, keepdims=True)
    ).astype(BF16)
    grad_tokens = grid.gather_rows(own_grad, parts).astype(F32)
    k_u0 = from_pair(normed_two, g_up, r_u0, dot_tn, early, [own_grad, grad_g0])
    grad_u0 = grid.line_scatter(k_u0)
    k_u1 = from_pair(normed_two, g_up, r_u1, dot_tn, late, [k_u0, grad_g1])
    grad_u1 = grid.line_scatter(k_u1)
    k_o = from_pair(g_attn, heads, r_o, dot_tt, after=[k_u1, grad_u0])
    grad_wo = grid.line_scatter(k_o).astype(F32)
    k_qkv = from_pair(normed_one, g_qkv, r_qkv, dot_tt, after=[k_o])
    grad_qkv = grid.line_scatter(k_qkv).astype(F32)
    grad_gate = jnp.concatenate([grad_g0, grad_g1], 1).astype(F32)
    grad_up = jnp.concatenate([grad_u0, grad_u1], 1).astype(F32)
    grad_down = jnp.concatenate([grad_d0.T, grad_d1.T], 0).astype(F32)

    n = grid.seq

    def blocks(x, dim):
        shape = x.shape
        x = x.reshape(shape[:dim] + (n, shape[dim] // n) + shape[dim + 1 :])
        return jnp.moveaxis(x, dim, 0).reshape(n, -1)

    norm_parts = [p * (1.0 / grid.outer) for p in (norm1_part, norm2_part)]
    both = [(norm_parts[0], 0), (norm_parts[1], 0), (a_part[: 3 * rank], 1), (bo_part, 1)]
    own = [
        (bq_part.reshape(query_up.shape), 2),
        (bk_part.reshape(key_up.shape), 2),
        (bv_part.reshape(value_up.shape), 2),
        (featq_part, 1),
        (featk_part, 1),
        (ao_part.reshape(output_down.shape), 1),
    ]
    cut = [blocks(x, d) for x, d in both + own]
    summed = grid.scatter_blocks(jnp.concatenate(cut, 1))
    n_both = sum(c.shape[1] for c in cut[: len(both)])
    flat = jnp.concatenate([grid.sum_kv(summed[:n_both].astype(BF16)), summed[n_both:]])
    done = []
    at = 0
    for x, d in both + own:
        shape = list(x.shape)
        shape[d] //= n
        size = x.size // n
        done.append(flat[at : at + size].reshape(shape))
        at += size
    norm1, norm2, grad_a, grad_bo, bq, bk, bv, featq, featk, grad_ao = done
    return (
        output,
        grad_tokens,
        norm1,
        grad_qkv[:, :qw],
        grad_qkv[:, qw : qw + kw],
        grad_qkv[:, qw + kw :],
        grad_a[:rank].T,
        bq,
        grad_a[rank : 2 * rank].T,
        bk,
        grad_a[2 * rank :].T,
        bv,
        featq,
        featk,
        grad_wo.T,
        grad_ao,
        grad_bo,
        norm2,
        grad_gate,
        grad_up,
        grad_down,
    )


def solution(mesh):
    placed = (
        P("seq", None),
        P(),
        P(None, "kv"),
        P(None, "kv"),
        P(None, "kv"),
        P(),
        P(None, "kv", None),
        P(),
        P(None, "kv", None),
        P(),
        P(None, "kv", None),
        P("kv", None, None),
        P("kv", None, None),
        P("kv", None),
        P("kv", None, None),
        P(),
        P(),
        P(None, "kv"),
        P(None, "kv"),
        P("kv", None),
        P("seq"),
        P("seq", None),
    )
    return jax.shard_map(
        local,
        mesh=mesh,
        in_specs=placed,
        out_specs=(
            P("seq", None),
            P("seq", None),
            P("seq"),
            P("seq", "kv"),
            P("seq", "kv"),
            P("seq", "kv"),
            P("seq", None),
            P(None, "kv", "seq"),
            P("seq", None),
            P(None, "kv", "seq"),
            P("seq", None),
            P(None, "kv", "seq"),
            P("kv", "seq", None),
            P("kv", "seq", None),
            P("kv", "seq"),
            P("kv", "seq", None),
            P(None, "seq"),
            P("seq"),
            P("seq", "kv"),
            P("seq", "kv"),
            P("kv", "seq"),
        ),
        check_vma=False,
    )
```

```python
import jax
import jax.numpy as jnp
from jax import lax
from jax.experimental import pallas as pl
from jax.experimental.pallas import tpu as pltpu
from jax.sharding import PartitionSpec as P

WIN = 64
CHUNK = 128
ANY = pl.BlockSpec(memory_space=pl.ANY)
EPSILON = 1e-05
EXACT = lax.Precision.HIGHEST
F32 = jnp.float32
BF16 = jnp.bfloat16


def cost(us):
    return pl.CostEstimate(flops=int(us * 0.45e9), bytes_accessed=1, transcendentals=0)


def dot(a, b, out=F32):
    return jnp.dot(a, b, preferred_element_type=F32).astype(out)


def dot_nt(a, b, out=F32):
    return lax.dot_general(a, b, (((1,), (1,)), ((), ())), preferred_element_type=F32).astype(out)


def dot_tn(a, b, out=F32):
    return lax.dot_general(a, b, (((0,), (0,)), ((), ())), preferred_element_type=F32).astype(out)


def dot_tt(a, b, out=F32):
    return lax.dot_general(a, b, (((0,), (1,)), ((), ())), preferred_element_type=F32).astype(out)


def tie(*xs):
    return lax.optimization_barrier(xs)


def add(terms):
    total = terms[0].astype(F32)
    for t in terms[1:]:
        total = total + t.astype(F32)
    return total


def take(x, i):
    return lax.dynamic_index_in_dim(x, i, 0, False)


class Grid:
    def __init__(self):
        self.kv = lax.axis_size("kv")
        self.seq = lax.axis_size("seq")
        self.outer = self.kv // 2
        self.line = self.seq // 2
        k = lax.axis_index("kv")
        s = lax.axis_index("seq")
        self.core, self.y = k % 2, k // 2
        self.x, self.z = s % 2, s // 2
        self.s = s
        self.core_swap = [(i, i ^ 1) for i in range(self.kv)]
        self.x_swap = [(i, i ^ 1) for i in range(self.seq)]
        self.z_groups = [[2 * z + x for z in range(self.line)] for x in range(2)]

    def y_shift(self, j):
        m = self.outer
        return [(y * 2 + c, (y + j) % m * 2 + c) for y in range(m) for c in range(2)]

    def own_rows(self, x, parts):
        rows, width = x.shape
        cut = x.reshape(parts, 2, rows // (2 * parts), width)
        return lax.dynamic_index_in_dim(cut, self.core, 1, False).reshape(rows // 2, width)

    def across_cores(self, x, pieces=1):
        rows = x.shape[0] // pieces
        cuts = [x[i * rows : (i + 1) * rows] for i in range(pieces)]
        got = [lax.ppermute(c, "kv", self.core_swap) for c in cuts]
        return jnp.concatenate(got, 0) if pieces > 1 else got[0]

    def core_sum(self, keep, send):
        return (keep.astype(F32) + self.across_cores(send, 4).astype(F32)).astype(BF16)

    def swap(self, x):
        return lax.ppermute(x, "seq", self.x_swap)

    def pair_sum(self, keep, got):
        return (keep.astype(F32) + got.astype(F32)).astype(BF16)

    def outer_terms(self, half):
        terms = [half] + [lax.ppermute(half, "kv", self.y_shift(j)) for j in range(1, self.outer)]
        if self.outer == 2:
            return terms
        stack = jnp.stack(terms)
        return [take(stack, (self.y - i) % self.outer) for i in range(self.outer)]

    def gather_rows(self, own, parts):
        other = self.across_cores(own, 4)
        first = self.core == 0
        shape = (parts, 1, own.shape[0] // parts, own.shape[1])
        low = jnp.where(first, own, other).reshape(shape)
        high = jnp.where(first, other, own).reshape(shape)
        return jnp.concatenate([low, high], 1).reshape(2 * own.shape[0], own.shape[1])

    def sum_kv(self, x):
        x = x + lax.ppermute(x, "kv", self.core_swap).astype(F32)
        total = x
        for j in range(1, self.outer):
            total = total + lax.ppermute(x, "kv", self.y_shift(j))
        return total

    def line_scatter(self, part):
        return lax.psum_scatter(
            part, "seq", scatter_dimension=0, tiled=True, axis_index_groups=self.z_groups
        )

    def finish(self, x):
        cut = x.reshape(2, x.shape[0] // 2, x.shape[1])
        got = self.swap(take(cut, 1 - self.x))
        own = take(cut, self.x)
        first = self.x == 0
        return jnp.where(first, own, got), jnp.where(first, got, own)

    def scatter_blocks(self, blocks):
        cut = blocks.reshape(self.line, 2, -1)
        other = lax.dynamic_index_in_dim(cut, 1 - self.x, 1, False).astype(BF16)
        own = lax.dynamic_index_in_dim(cut, self.x, 1, False)
        part = own + lax.ppermute(other, "seq", self.x_swap).astype(F32)
        total = take(part, self.z)
        m = self.line
        for j in range(1, m):
            pairs = [(z * 2 + x, (z + j) % m * 2 + x) for z in range(m) for x in range(2)]
            out = take(part, (self.z + j) % m).astype(BF16)
            total = total + lax.ppermute(out, "seq", pairs).astype(F32)
        return total

    def shift_seq(self, x, by):
        n = self.seq
        pairs = [(i, i + by) for i in range(n) if 0 <= i + by < n]
        return lax.ppermute(x, "seq", pairs)

    def sum_before(self, x, sign, kind):
        near = self.shift_seq(x.astype(kind), sign).astype(F32)
        total = x + near
        by = 2
        while by < self.seq:
            total = total + self.shift_seq(total.astype(kind), sign * by).astype(F32)
            by *= 2
        return total - x, near


def softmax_pair(logits):
    top = jnp.exp(logits - jnp.max(logits, 0, keepdims=True))
    low = jnp.exp(jnp.min(logits, 0, keepdims=True) - logits)
    return top * (1.0 / jnp.sum(top, 0, keepdims=True)), low * (1.0 / jnp.sum(low, 0, keepdims=True))


def softmax_pair_back(p, n, grad):
    hd = p.shape[0]
    up, un = p * grad[:hd], n * grad[hd:]
    return up - p * jnp.sum(up, 0, keepdims=True) - (un - n * jnp.sum(un, 0, keepdims=True))


def halves(x):
    top = x.astype(BF16)
    return top, (x - top.astype(F32)).astype(BF16)


def dot2(x, b):
    top, rest = halves(x)
    return dot(top, b) + dot(rest, b)


def value_rows(v, keep):
    hd, n = v.shape
    ones = (lax.broadcasted_iota(jnp.int32, (16, n), 0) == 0).astype(F32)
    return (jnp.concatenate([v.astype(F32), ones], 0) * keep).astype(BF16)


def key_kernel(kv_ref, map_ref, keep_ref, phi_cols_ref, phi_ref, k_ref, v_ref, state_ref):
    hk, hd = map_ref.shape[:2]
    for g in range(hk):
        k = kv_ref[g * hd : (g + 1) * hd, :]
        v = kv_ref[(hk + g) * hd : (hk + g + 1) * hd, :]
        p, n = softmax_pair(dot(map_ref[g], k))
        phi = jnp.concatenate([p, n], 0)
        phi_cols_ref[g] = phi.astype(BF16)
        phi_ref[g] = phi.T.astype(BF16)
        kv = jnp.concatenate([k, v], 0).astype(F32).T
        k_ref[g] = kv[:, :hd].astype(BF16)
        v_ref[g] = kv[:, hd:].astype(BF16)
        state_ref[g] = dot_nt(value_rows(v, keep_ref[...]), phi.astype(BF16))


def masks(open_ref, base):
    shape = (2 * CHUNK, CHUNK)
    a = lax.broadcasted_iota(jnp.int32, shape, 0)
    b = lax.broadcasted_iota(jnp.int32, shape, 1)
    start = open_ref[:, pl.ds(base, CHUNK)] - base
    doc = a >= start
    near = a > b + (CHUNK - WIN)
    return doc & near & (a <= b + CHUNK), doc & ~near, (start < 0).astype(F32)


def lanes(parts):
    return jnp.concatenate(parts, 1)


def attend_kernel(
    q_ref, kv_ref, phi_cols_ref, phi_ref, k_ref, map_ref, prior_ref, open_ref, keep_ref, cont_ref,
    heads_ref, total_ref, states_ref, state,
):
    hk, hd = phi_ref.shape[0], map_ref.shape[1]
    hq = map_ref.shape[0]
    group = hq // hk
    scale = hd**-0.5
    state[...] = prior_ref[...]

    def chunk(i, _):
        base = pl.multiple_of(i * CHUNK, CHUNK)
        here = pl.ds(base, CHUNK)
        keys = pl.ds(base, 2 * CHUNK)
        win, lin, far = masks(open_ref, base)
        for g in range(hk):
            q = [q_ref[h * hd : (h + 1) * hd, here] for h in range(g * group, (g + 1) * group)]
            phi = []
            for j in range(group):
                p, n = softmax_pair(dot(map_ref[g * group + j], q[j]))
                phi.append(jnp.concatenate([p, n], 0).astype(BF16))
            phi4 = lanes(phi)
            past = state[g]
            states_ref[i, g] = past
            scores = dot(k_ref[g, keys, :], lanes(q)) * scale
            linear = dot(phi_ref[g, keys, :], phi4)
            carried = dot2(past, phi4)
            weights = []
            totals = []
            for j in range(group):
                cut = slice(j * CHUNK, (j + 1) * CHUNK)
                w = jnp.where(win, jnp.exp(scores[:, cut]), 0.0) + jnp.where(lin, linear[:, cut], 0.0)
                weights.append(w.astype(BF16))
                totals.append(jnp.sum(w, 0, keepdims=True) + far * carried[hd : hd + 1, cut])
            v = kv_ref[(hk + g) * hd : (hk + g + 1) * hd, keys]
            mixed = dot(v, lanes(weights))
            for j in range(group):
                cut = slice(j * CHUNK, (j + 1) * CHUNK)
                h = g * group + j
                out = (mixed[:, cut] + far * carried[:hd, cut]) * (1.0 / totals[j])
                heads_ref[h * hd : (h + 1) * hd, here] = out.astype(BF16)
                total_ref[h : h + 1, here] = totals[j]
            own = value_rows(kv_ref[(hk + g) * hd : (hk + g + 1) * hd, here], keep_ref[:, here])
            state[g] = cont_ref[i] * past + dot_nt(own, phi_cols_ref[g, :, here])
        return 0

    lax.fori_loop(0, heads_ref.shape[1] // CHUNK, chunk, 0)


def attend_back_kernel(
    q_ref, kv_ref, phi_cols_ref, phi_ref, k_ref, v_ref, map_ref, map_t_ref, states_ref, heads_ref,
    total_ref, g_ref, open_ref, keep_ref, cont_ref,
    gq_ref, feat_ref, gk_ref, gv_ref, gphi_ref, first_ref, gl_ref, grad_t,
):
    hk, hd = phi_ref.shape[0], map_ref.shape[1]
    hq = map_ref.shape[0]
    group = hq // hk
    scale = hd**-0.5
    count = heads_ref.shape[1] // CHUNK
    first_ref[...] = jnp.zeros_like(first_ref)
    grad_t[...] = jnp.zeros_like(grad_t)
    gk_ref[...] = jnp.zeros_like(gk_ref)
    gv_ref[...] = jnp.zeros_like(gv_ref)
    gphi_ref[...] = jnp.zeros_like(gphi_ref)

    def chunk(step, _):
        i = count - 1 - step
        base = pl.multiple_of(i * CHUNK, CHUNK)
        here = pl.ds(base, CHUNK)
        keys = pl.ds(base, 2 * CHUNK)
        win, lin, far = masks(open_ref, base)
        for g in range(hk):
            rows = [slice(h * hd, (h + 1) * hd) for h in range(g * group, (g + 1) * group)]
            key_rows = slice(g * hd, (g + 1) * hd)
            value_row = slice((hk + g) * hd, (hk + g + 1) * hd)
            q4 = lanes([q_ref[r, here] for r in rows])
            g4 = lanes([g_ref[r, here] for r in rows])
            pairs = [softmax_pair(dot(map_ref[g * group + j], q_ref[rows[j], here])) for j in range(group)]
            phi = [jnp.concatenate([p, n], 0) for p, n in pairs]
            phi4 = lanes([x.astype(BF16) for x in phi])
            scores = dot(k_ref[g, keys, :], q4) * scale
            linear = dot(phi_ref[g, keys, :], phi4)
            g_w = dot(v_ref[g, keys, :], g4)
            shares, g_scores, g_linear, g_ext = [], [], [], []
            for j in range(group):
                cut = slice(j * CHUNK, (j + 1) * CHUNK)
                h = g * group + j
                inv = 1.0 / total_ref[h : h + 1, here]
                g_here = g_ref[rows[j], here].astype(F32)
                g_total = -inv * jnp.sum(g_here * heads_ref[rows[j], here].astype(F32), 0, keepdims=True)
                ex = jnp.where(win, jnp.exp(scores[:, cut]), 0.0)
                w = ex + jnp.where(lin, linear[:, cut], 0.0)
                shares.append((w * inv).astype(BF16))
                g_weight = g_w[:, cut] * inv + g_total
                g_scores.append((g_weight * ex).astype(BF16))
                g_linear.append(jnp.where(lin, g_weight, 0.0).astype(BF16))
                row = lax.broadcasted_iota(jnp.int32, (16, CHUNK), 0) == 0
                g_ext.append(
                    (jnp.concatenate([g_here * inv, jnp.where(row, g_total, 0.0)], 0) * far).astype(BF16)
                )
            shares, g_scores, g_linear, g_ext = map(lanes, (shares, g_scores, g_linear, g_ext))
            gv_ref[key_rows, keys] += dot_nt(g4, shares)
            gk_ref[key_rows, keys] += dot_nt(q4, g_scores) * scale
            gphi_ref[g, :, keys] += dot_nt(phi4, g_linear)
            g_query = dot(kv_ref[key_rows, keys], g_scores) * scale
            past = states_ref[i, g].T
            g_phi = dot(phi_cols_ref[g, :, keys], g_linear) + dot2(past, g_ext)
            for j in range(group):
                cut = slice(j * CHUNK, (j + 1) * CHUNK)
                gl = softmax_pair_back(*pairs[j], g_phi[:, cut]).astype(BF16)
                gl_ref[rows[j], here] = gl
                gq = g_query[:, cut] + dot(map_t_ref[g * group + j], gl)
                gq_ref[rows[j], here] = gq.astype(BF16)
            keep = keep_ref[:, here]
            own = value_rows(kv_ref[value_row, here], keep)
            gphi_ref[g, :, here] += dot2(grad_t[g], own)
            gv_ref[key_rows, here] += dot2(first_ref[g, :hd, :], phi_cols_ref[g, :, here]) * keep
            cont = cont_ref[i]
            first_ref[g] = cont * first_ref[g] + dot_nt(g_ext, phi4)
            grad_t[g] = cont * grad_t[g] + dot_nt(phi4, g_ext)
        return 0

    lax.fori_loop(0, count, chunk, 0)
    for h in range(hq):
        r = slice(h * hd, (h + 1) * hd)
        feat_ref[h] = dot_nt(q_ref[r, :], gl_ref[r, :])


def key_back_kernel(
    kv_ref, phi_cols_ref, map_ref, map_t_ref, gk_ref, gv_ref, gphi_ref, edge_ref, later_ref, last_ref,
    keep_ref, g_ref, feat_ref,
):
    hk, hd = map_ref.shape[:2]
    n = kv_ref.shape[1]
    cut = n - CHUNK

    def joined(own, edge):
        return jnp.concatenate([own[:, : cut - CHUNK], own[:, cut - CHUNK :] + edge.astype(F32)], 1)

    for g in range(hk):
        key_rows = slice(g * hd, (g + 1) * hd)
        k = kv_ref[key_rows, CHUNK:]
        v = kv_ref[(hk + g) * hd : (hk + g + 1) * hd, CHUNK:]
        keep = keep_ref[:, CHUNK:]
        phi = phi_cols_ref[g, :, CHUNK:]
        own = value_rows(v, keep)
        one = value_rows(v[:, cut - CHUNK :], jnp.ones((1, CHUNK), F32))
        later, last = later_ref[g], last_ref[g]
        g_phi = gphi_ref[g, :, CHUNK:] + lanes(
            [dot2(later.T, own[:, : cut - CHUNK]), dot2(last.T, one)]
        )
        g_phi = joined(g_phi, edge_ref[2 * hk * hd + g * 2 * hd : 2 * hk * hd + (g + 1) * 2 * hd, :])
        g_v = gv_ref[key_rows, CHUNK:] + lanes(
            [
                dot2(later[:hd], phi[:, : cut - CHUNK]) * keep[:, : cut - CHUNK],
                dot2(last[:hd], phi[:, cut - CHUNK :]),
            ]
        )
        g_v = joined(g_v, edge_ref[(hk + g) * hd : (hk + g + 1) * hd, :])
        g_ref[(hk + g) * hd : (hk + g + 1) * hd, :] = g_v.astype(BF16)
        p, q = softmax_pair(dot(map_ref[g], k))
        gl = softmax_pair_back(p, q, g_phi).astype(BF16)
        g_k = joined(gk_ref[key_rows, CHUNK:], edge_ref[key_rows, :]) + dot(map_t_ref[g], gl)
        g_ref[key_rows, :] = g_k.astype(BF16)
        feat_ref[g] = dot_nt(k, gl)


def call(us, kernel, outs, args, scratch=(), smem=(), after=()):
    count = len(args)
    vmem = pl.BlockSpec(memory_space=pltpu.VMEM)
    specs = [pl.BlockSpec(memory_space=pltpu.SMEM) if i in smem else vmem for i in range(len(args))]
    return pl.pallas_call(
        lambda *refs: kernel(*refs[:count], *refs[count + len(after) :]),
        out_shape=[jax.ShapeDtypeStruct(s, d) for s, d in outs],
        in_specs=specs + [ANY] * len(after),
        out_specs=[vmem] * len(outs),
        scratch_shapes=[pltpu.VMEM(s, d) for s, d in scratch],
        compiler_params=pltpu.CompilerParams(vmem_limit_bytes=48 * 2**20),
        cost_estimate=cost(us),
    )(*args, *after)


def project_kernel(
    x_ref, gain_ref, wq_ref, wk_ref, wv_ref, down_ref, up_ref, normed_ref, q_ref, kv_ref, low_ref
):
    x = x_ref[...].astype(F32)
    rms = lax.rsqrt(jnp.mean(x * x, -1, keepdims=True) + EPSILON)
    normed = (x * rms * gain_ref[...].astype(F32)).astype(BF16)
    normed_ref[...] = normed
    low, rest = halves(dot(normed, down_ref[...]))
    low_ref[...] = low
    qw, kw = wq_ref.shape[1], wk_ref.shape[1]

    def rows(weight, at, width):
        up = up_ref[:, at : at + width]
        return (dot(normed, weight[...]) + dot(low, up) + dot(rest, up)).T.astype(BF16)

    kv_ref[:kw, :] = rows(wk_ref, qw, kw)
    kv_ref[kw:, :] = rows(wv_ref, qw + kw, kw)
    q_ref[...] = rows(wq_ref, 0, qw)


def project(tokens, gain, wq, wk, wv, down, up, tile=256):
    t, d = tokens.shape
    qw, kw = wq.shape[1], wk.shape[1]
    whole = lambda a: pl.BlockSpec(a.shape, lambda i: (0,) * a.ndim)
    row = lambda w: pl.BlockSpec((tile, w), lambda i: (i, 0))
    col = lambda h: pl.BlockSpec((h, tile), lambda i: (0, i))
    gain = gain[None]
    return pl.pallas_call(
        project_kernel,
        grid=(t // tile,),
        in_specs=[row(d)] + [whole(a) for a in (gain, wq, wk, wv, down, up)],
        out_specs=[row(d), col(qw), col(2 * kw), row(down.shape[1])],
        out_shape=[
            jax.ShapeDtypeStruct((t, d), BF16),
            jax.ShapeDtypeStruct((qw, t), BF16),
            jax.ShapeDtypeStruct((2 * kw, t), BF16),
            jax.ShapeDtypeStruct((t, down.shape[1]), BF16),
        ],
        compiler_params=pltpu.CompilerParams(vmem_limit_bytes=48 * 2**20),
        cost_estimate=cost(10.0),
    )(tokens, gain, wq, wk, wv, down, up)


def matmul(pairs, mode, chosen, out, split=None, tile=512, after=()):
    a0, b0 = pairs[0]
    over = 0 if mode in ("left", "both") else 1
    rows = a0.shape[1 - over]
    half = a0.shape[over]
    width = {"rows": b0.shape[0] // 2, "columns": b0.shape[0], "both": b0.shape[0]}.get(mode, b0.shape[1])
    tile = min(tile, width)
    product = {"rows": dot_nt, "columns": dot_nt, "inner": dot, "left": dot_tn, "both": dot_tt}[mode]
    b_spec = {
        "rows": pl.BlockSpec((tile, half), lambda i, s: (s[0] * (width // tile) + i, 0)),
        "columns": pl.BlockSpec((tile, half), lambda i, s: (i, s[0])),
        "inner": pl.BlockSpec((half, tile), lambda i, s: (s[0], i)),
        "left": pl.BlockSpec((half, tile), lambda i, s: (0, i)),
        "both": pl.BlockSpec((tile, half), lambda i, s: (i, 0)),
    }[mode]
    specs, args = [], []
    for a, b in pairs:
        specs += [pl.BlockSpec(a.shape, lambda i, s: (0, 0)), b_spec]
        args += [a, b]
    sub = rows // 4
    core = jnp.zeros((), jnp.int32) if split is None else split

    def kernel(sel, *refs):
        used = refs[: 2 * len(pairs)]
        outs = refs[2 * len(pairs) + len(after) :]

        def block(start):
            total = None
            for a_ref, b_ref in zip(used[::2], used[1::2]):
                a = a_ref[pl.ds(start, sub), :] if over else a_ref[:, pl.ds(start, sub)]
                term = product(a, b_ref[...])
                total = term if total is None else total + term
            return total.astype(out)

        for c in range(2):
            for k in range(2):
                if split is None:
                    at = (2 * c + k) * sub
                    outs[0][at : at + sub, :] = block(at)
                else:
                    other = sel[1] if k == 0 else 1 - sel[1]
                    start = pl.multiple_of((2 * c + other) * sub, sub)
                    outs[k][c * sub : (c + 1) * sub, :] = block(start)

    n_out = 1 if split is None else 2
    us = 1.0 + sum(a.size for a, _ in pairs) * width * 1.5e-9
    made = pl.pallas_call(
        kernel,
        grid_spec=pltpu.PrefetchScalarGridSpec(
            num_scalar_prefetch=1,
            grid=(width // tile,),
            in_specs=specs + [ANY] * len(after),
            out_specs=[pl.BlockSpec((rows // n_out, tile), lambda i, s: (0, i))] * n_out,
        ),
        out_shape=[jax.ShapeDtypeStruct((rows // n_out, width), out)] * n_out,
        compiler_params=pltpu.CompilerParams(vmem_limit_bytes=56 * 2**20),
        cost_estimate=cost(us),
    )(jnp.stack([chosen, core]).astype(jnp.int32), *args, *after)
    return made if split is not None else made[0]


def grad_pair(count, pairs, after=()):
    rows, width = pairs[0][0].shape
    n = pairs[0][1].shape[1]
    block = width // count
    specs = [pl.BlockSpec((rows, block), lambda j: (0, j)), pl.BlockSpec((rows, n), lambda j: (0, 0))]

    def kernel(*refs):
        value = dot_tn(refs[0][...], refs[1][...])
        for i in range(1, len(pairs)):
            value = value + dot_tn(refs[2 * i][...], refs[2 * i + 1][...])
        refs[-1][...] = value.astype(BF16)

    return pl.pallas_call(
        kernel,
        grid=(count,),
        in_specs=specs * len(pairs) + [ANY] * len(after),
        out_specs=pl.BlockSpec((block, n), lambda j: (j, 0)),
        out_shape=jax.ShapeDtypeStruct((width, n), BF16),
        compiler_params=pltpu.CompilerParams(vmem_limit_bytes=48 * 2**20),
        cost_estimate=cost(13.0),
    )(*[x for pair in pairs for x in pair], *after)


def grad_block(line, select, a, b, product, got=None, after=()):
    rows, width = a.shape
    block = width // (2 * line)
    n = b.shape[0] if product is dot_tt else b.shape[1]
    more = [] if got is None else [got]

    def kernel(sel, a_ref, b_ref, *rest):
        value = product(a_ref[...], b_ref[...])
        if got is not None:
            value = value + rest[0][...].astype(F32)
        rest[-1][...] = value.astype(BF16)

    spec = pl.BlockSpec((block, n), lambda j, s: (j, 0))
    return pl.pallas_call(
        kernel,
        grid_spec=pltpu.PrefetchScalarGridSpec(
            num_scalar_prefetch=1,
            grid=(line,),
            in_specs=[
                pl.BlockSpec((rows, block), lambda j, s: (0, 2 * j + s[0])),
                pl.BlockSpec(b.shape, lambda j, s: (0, 0)),
            ]
            + [spec] * len(more)
            + [ANY] * len(after),
            out_specs=spec,
        ),
        out_shape=jax.ShapeDtypeStruct((line * block, n), BF16),
        compiler_params=pltpu.CompilerParams(vmem_limit_bytes=48 * 2**20),
        cost_estimate=cost(1.0),
    )(select.astype(jnp.int32)[None], a, b, *more, *after)


def gated_kernel(sel_ref, own_ref, other_ref, wg_ref, wu_ref, gh_ref, *refs):
    normed_ref, hidden_ref, gate_ref, up_ref = refs[-4:]
    half = own_ref.shape[0]

    @pl.when(pl.program_id(0) == 0)
    def _():
        first = sel_ref[0] == 0

        @pl.when(first)
        def _():
            normed_ref[:half, :] = own_ref[...]
            normed_ref[half:, :] = other_ref[...]

        @pl.when(jnp.logical_not(first))
        def _():
            normed_ref[:half, :] = other_ref[...]
            normed_ref[half:, :] = own_ref[...]

    for r in range(0, 2 * half, half):
        cut = slice(r, r + half)
        x = normed_ref[cut, :]
        gate = dot(x, wg_ref[...])
        up = dot(x, wu_ref[...])
        sig = 1.0 / (1.0 + jnp.exp(-gate))
        silu = gate * sig
        hidden_ref[cut, :] = (silu * up).astype(BF16)
        g = gh_ref[cut, :].astype(F32)
        gate_ref[cut, :] = (g * up * (sig + silu * (1.0 - sig))).astype(BF16)
        up_ref[cut, :] = (g * silu).astype(BF16)


def gated(c, rows, sel, own, other, wg, wu, gh, held, after, tile=256):
    half, d = own.shape
    f = wg.shape[1] // 2
    here = pl.BlockSpec((2 * half, tile), lambda i, s: (c, i))
    weight = pl.BlockSpec((d, tile), lambda i, s: (0, s[1] * (f // tile) + i))
    shapes = [jax.ShapeDtypeStruct((rows, d), BF16)] + [jax.ShapeDtypeStruct((rows, f), BF16)] * 3
    return pl.pallas_call(
        gated_kernel,
        grid_spec=pltpu.PrefetchScalarGridSpec(
            num_scalar_prefetch=1,
            grid=(f // tile,),
            in_specs=[
                pl.BlockSpec((half, d), lambda i, s: (0, 0)),
                pl.BlockSpec((half, d), lambda i, s: (0, 0)),
                weight,
                weight,
                here,
            ]
            + [ANY] * (len(held) + len(after)),
            out_specs=[pl.BlockSpec((2 * half, d), lambda i, s: (c, 0)), here, here, here],
        ),
        out_shape=shapes,
        input_output_aliases={6 + i: i for i in range(len(held))},
        compiler_params=pltpu.CompilerParams(vmem_limit_bytes=56 * 2**20),
        cost_estimate=cost(11.0),
    )(sel, own, other, wg, wu, gh, *held, *after)


def local(
    tokens,
    gain_one,
    query_weight,
    key_weight,
    value_weight,
    query_down,
    query_up,
    key_down,
    key_up,
    value_down,
    value_up,
    query_map,
    key_map,
    output_weight,
    output_down,
    output_up,
    gain_two,
    gate_weight,
    up_weight,
    down_weight,
    start_mask,
    cotangent,
):
    grid = Grid()
    rows = tokens.shape[0]
    rank = query_down.shape[1]
    hd = key_map.shape[-1]
    hk = key_map.shape[0]
    hq = query_map.shape[0]
    group = hq // hk
    count = rows // CHUNK
    length = rows + CHUNK
    index = jnp.arange(rows, dtype=jnp.int32)
    starts = jnp.where(start_mask == 1, index + CHUNK, jnp.int32(-1))
    opened = jnp.max(jnp.where(index[:, None] <= index[None, :], starts[:, None], jnp.int32(-1)), 0)
    ends = jnp.concatenate([jnp.full((1,), -1, jnp.int32), opened[CHUNK - 1 : -1 : CHUNK]])
    cont = (ends < jnp.arange(count, dtype=jnp.int32) * CHUNK).astype(F32)
    place = jnp.arange(length, dtype=jnp.int32)
    ends_at = jnp.concatenate([jnp.repeat(ends, CHUNK), jnp.full((CHUNK,), length, jnp.int32)])
    keep = (place >= ends_at).astype(F32)[None]
    keep_all = ((place >= ends[count - 1]) & (place < rows)).astype(F32)[None]
    opened = opened[None]

    g1 = gain_one.astype(F32)
    g2 = gain_two.astype(F32)
    qup, kup, vup = (u.reshape(rank, -1) for u in (query_up, key_up, value_up))
    qw, kw = hq * hd, hk * hd
    wide = 128 - 3 * rank
    up_all = jnp.pad(jax.scipy.linalg.block_diag(qup, kup, vup), ((0, wide), (0, 0)))
    down_all = jnp.pad(jnp.concatenate([query_down, key_down, value_down], 1), ((0, 0), (0, wide)))
    normed_one, query, kv, low_all = project(
        tokens, gain_one, query_weight, key_weight, value_weight, down_all, up_all
    )
    edge = grid.shift_seq(kv[:, rows - CHUNK :], 1)
    kv = jnp.concatenate([edge, kv], 1)

    query_map_t = jnp.swapaxes(query_map, 1, 2)
    key_map_t = jnp.swapaxes(key_map, 1, 2)
    phi_dim = 2 * hd
    phi_cols, phi, key, value, state = call(
        2.0,
        key_kernel,
        [
            ((hk, phi_dim, length), BF16),
            ((hk, length, phi_dim), BF16),
            ((hk, length, hd), BF16),
            ((hk, length, hd), BF16),
            ((hk, hd + 16, phi_dim), F32),
        ],
        (kv, key_map_t, keep_all),
    )
    prior, _ = grid.sum_before(state, 1, F32)
    parts = 2
    chunk = rows // parts
    core, mine = grid.core.astype(jnp.int32), grid.x.astype(jnp.int32)
    g_hidden = matmul([(cotangent, down_weight)], "rows", mine, F32)
    oup = output_up
    odown = output_down.reshape(-1, rank)
    weight_o = (output_weight.astype(F32) + dot(odown, oup)).astype(BF16)
    cot_own = grid.own_rows(cotangent, parts)
    prior, g_hidden, weight_o, cot_own = tie(prior, g_hidden, weight_o, cot_own)
    cot_got = grid.swap(cot_own)
    heads, totals, states = call(
        9.0,
        attend_kernel,
        [((qw, rows), BF16), ((hq, rows), F32), ((count, hk, hd + 16, phi_dim), F32)],
        (query, kv, phi_cols, phi, key, query_map_t, prior, opened, keep, cont),
        scratch=[((hk, hd + 16, phi_dim), F32)],
        smem=(9,),
    )

    kept, sent = matmul([(heads, weight_o)], "left", mine, BF16, core)
    cuts = [slice(c * chunk // 2, (c + 1) * chunk // 2) for c in range(parts)]
    half = [grid.core_sum(kept[cut], sent[cut]) for cut in cuts]
    own_tokens = [grid.own_rows(tokens[c * chunk : (c + 1) * chunk], 1) for c in range(parts)]
    own_tokens[0], half[1] = tie(own_tokens[0], half[1])
    terms = [grid.outer_terms(h) for h in half]
    cot_got, terms[0][-1] = tie(cot_got, terms[0][-1])
    held, held_pair = (), ()
    resid, rms_two, own, got = [], [], [], []
    select = jnp.stack([core, mine])

    def normed(c):
        r = own_tokens[c].astype(F32) + add(terms[c])
        rms = lax.rsqrt(jnp.mean(r * r, -1, keepdims=True) + EPSILON)
        resid.append(r)
        rms_two.append(rms)
        own.append((r * rms * g2).astype(BF16))
        got.append(None)

    def inner(c, mine_c, gh, held, after):
        return gated(
            c, rows, select, mine_c, grid.across_cores(mine_c), gate_weight, up_weight, gh, held, after
        )

    normed(0)
    got[0] = grid.swap(own[0])
    held = list(inner(0, own[0], g_hidden, held, []))
    terms[1][-1], held[1] = tie(terms[1][-1], held[1])
    normed(1)
    got[1] = grid.swap(own[1])
    cot_got, mark = tie(cot_got, own[1])
    cot_pair = grid.gather_rows(cot_got, parts)
    g_pair = matmul([(cot_pair, down_weight)], "rows", mine, F32, after=[mark])
    held = inner(1, own[1], g_hidden, held, [g_pair])
    held_pair = list(inner(0, got[0], g_pair, held_pair, [held[1]]))
    got[1], held_pair[1] = tie(got[1], held_pair[1])
    held_pair = inner(1, got[1], g_pair, held_pair, [])
    normed_two, hidden, g_gate, g_up = held
    normed_pair, hidden_pair, gate_pair, up_pair = held_pair
    resid = jnp.concatenate(resid, 0)
    rms_two = jnp.concatenate(rms_two, 0)

    count_d = 2 * grid.line
    yours = 1 - mine

    def to_pair(a, b, product=dot_tn, after=()):
        return grad_block(grid.line, yours, a, b, product, None, after)

    def from_pair(a, b, got, product=dot_tn, after=()):
        return grad_block(grid.line, mine, a, b, product, got, after)

    kept, sent = matmul(
        [(gate_pair, gate_weight), (up_pair, up_weight)], "columns", mine, BF16, core
    )
    theirs = grid.core_sum(kept, sent)
    kept, sent = matmul(
        [(g_gate, gate_weight), (g_up, up_weight)], "columns", mine, BF16, core, after=[kept]
    )
    ours = grid.core_sum(kept, sent)
    w_d = grad_pair(count_d, [(cotangent, hidden), (cot_pair, hidden_pair)], after=[kept])
    w_g = grad_pair(count_d, [(normed_two, g_gate), (normed_pair, gate_pair)], after=[w_d])
    theirs = grid.swap(theirs)
    theirs, w_d, w_g = tie(theirs, w_d, w_g)
    grad_d = grid.line_scatter(w_d)
    grad_g = grid.line_scatter(w_g)
    half = grid.pair_sum(ours, theirs)
    terms = grid.outer_terms(half)
    down_theirs = matmul([(hidden_pair, down_weight)], "inner", mine, BF16, core, after=[half])
    down_ours = matmul([(hidden, down_weight)], "inner", mine, BF16, core, after=[down_theirs[0]])
    w_u = grad_pair(
        count_d, [(normed_two, g_up), (normed_pair, up_pair)], after=[down_ours[0]]
    )
    terms[-1], w_u, *down_ours = tie(terms[-1], w_u, *down_ours)
    grad_u = grid.line_scatter(w_u)

    g_two = add(terms)
    norm2_part = jnp.sum(g_two * resid * rms_two, 0)
    s_two = g_two * g2
    g_resid = (
        cot_own.astype(F32)
        + rms_two * s_two
        - resid * rms_two**3 * jnp.mean(resid * s_two, -1, keepdims=True)
    )
    own_attn = g_resid.astype(BF16)
    g_attn = grid.gather_rows(own_attn, parts)
    down_got = grid.swap(grid.core_sum(*down_theirs))
    down_half = grid.core_sum(*down_ours)
    weight_qkv = jnp.concatenate([query_weight, key_weight, value_weight], 1)
    weight_qkv = (weight_qkv.astype(F32) + dot(down_all, up_all)).astype(BF16)
    g_attn, weight_qkv = tie(g_attn, weight_qkv)

    g_heads = dot_nt(weight_o, g_attn, BF16)
    g_q, featq_part, gk, gv, gphi, first = call(
        24.0,
        attend_back_kernel,
        [
            ((qw, rows), BF16),
            ((hq, hd, hd), F32),
            ((kw, length), F32),
            ((kw, length), F32),
            ((hk, phi_dim, length), F32),
            ((hk, hd + 16, phi_dim), F32),
        ],
        (
            query, kv, phi_cols, phi, key, value, query_map_t, query_map, states, heads,
            totals, g_heads, opened, keep, cont,
        ),
        scratch=[((qw, rows), BF16), ((hk, phi_dim, hd + 16), F32)],
        smem=(14,),
        after=[grad_d],
    )
    first, down_got, down_half = tie(first, down_got, down_half)
    down_half = grid.pair_sum(down_half, down_got)
    later, near = grid.sum_before(first, -1, BF16)
    back = [gk[:, :CHUNK], gv[:, :CHUNK], gphi[:, :, :CHUNK].reshape(hk * phi_dim, CHUNK)]
    back = grid.shift_seq(jnp.concatenate(back, 0).astype(BF16), -1)
    s_o = to_pair(g_attn, heads, dot_tt, after=[g_q])
    r_o = grid.swap(s_o)
    g_kv, featk_part = call(
        2.0,
        key_back_kernel,
        [((2 * kw, rows), BF16), ((hk, hd, hd), F32)],
        (kv, phi_cols, key_map_t, key_map, gk, gv, gphi, back, later, later - near, keep_all),
        after=[s_o],
    )

    g_qkv = jnp.concatenate([g_q, g_kv], 0)
    kept, sent = matmul([(g_qkv, weight_qkv)], "both", mine, BF16, core)
    half = grid.core_sum(kept, sent)
    half, down_half = tie(half, down_half)
    terms = grid.outer_terms(half)
    down_terms = grid.outer_terms(down_half)
    s_qkv = to_pair(normed_one, g_qkv, dot_tt, after=[half])
    r_qkv = grid.swap(s_qkv)
    g_late, s_qkv = tie(g_attn, s_qkv)
    g_low_o = dot_nt(g_late, oup, BF16)
    low_o = dot_tn(odown, heads, BF16)
    bo_part = dot(low_o, g_late)
    ao_part = dot(heads, g_low_o)
    k_o = from_pair(g_attn, heads, r_o, dot_tt, after=[s_qkv])
    g_low = dot(up_all, g_qkv, BF16)
    a_part = dot(g_low, normed_one)
    b_part = dot_tt(low_all, g_qkv)
    bq_part = b_part[:rank, :qw]
    bk_part = b_part[rank : 2 * rank, qw : qw + kw]
    bv_part = b_part[2 * rank : 3 * rank, qw + kw :]
    terms[-1], a_part, b_part, bo_part, ao_part, r_qkv, grad_u, grad_g, k_o = tie(
        terms[-1], a_part, b_part, bo_part, ao_part, r_qkv, grad_u, grad_g, k_o
    )
    grad_o = grid.line_scatter(k_o)
    k_qkv = from_pair(normed_one, g_qkv, r_qkv, dot_tt, after=[k_o])

    terms[-1], k_qkv = tie(terms[-1], k_qkv)
    stream = grid.own_rows(tokens, parts).astype(F32)
    rms_one = lax.rsqrt(jnp.mean(stream * stream, -1, keepdims=True) + EPSILON)
    g_one = add(terms)
    norm1_part = jnp.sum(g_one * stream * rms_one, 0)
    s_one = g_one * g1
    own_grad = (
        g_resid
        + rms_one * s_one
        - stream * rms_one**3 * jnp.mean(stream * s_one, -1, keepdims=True)
    ).astype(BF16)
    grad_qkv = grid.line_scatter(k_qkv).astype(F32)
    output = grid.gather_rows((resid + add(down_terms)).astype(BF16), parts)
    grad_tokens = grid.gather_rows(own_grad, parts).astype(F32)
    own_grad, grad_d, grad_g, grad_u = tie(own_grad, grad_d, grad_g, grad_u)
    down_low, down_high = grid.finish(grad_d)
    gate_low, gate_high = grid.finish(grad_g)
    up_low, up_high = grid.finish(grad_u)
    grad_wo = grad_o.astype(F32)
    grad_gate = jnp.concatenate([gate_low, gate_high], 1).astype(F32)
    grad_up = jnp.concatenate([up_low, up_high], 1).astype(F32)
    grad_down = jnp.concatenate([down_low.T, down_high.T], 0).astype(F32)

    n = grid.seq

    def blocks(x, dim):
        shape = x.shape
        x = x.reshape(shape[:dim] + (n, shape[dim] // n) + shape[dim + 1 :])
        return jnp.moveaxis(x, dim, 0).reshape(n, -1)

    norm_parts = [p * (1.0 / grid.outer) for p in (norm1_part, norm2_part)]
    both = [(norm_parts[0], 0), (norm_parts[1], 0), (a_part[: 3 * rank], 1), (bo_part, 1)]
    own = [
        (bq_part.reshape(query_up.shape), 2),
        (bk_part.reshape(key_up.shape), 2),
        (bv_part.reshape(value_up.shape), 2),
        (featq_part, 1),
        (featk_part, 1),
        (ao_part.reshape(output_down.shape), 1),
    ]
    cut = [blocks(x, d) for x, d in both + own]
    summed = grid.scatter_blocks(jnp.concatenate(cut, 1))
    summed, grad_qkv, grad_wo = tie(summed, grad_qkv, grad_wo)
    n_both = sum(c.shape[1] for c in cut[: len(both)])
    flat = jnp.concatenate([grid.sum_kv(summed[:n_both].astype(BF16)), summed[n_both:]])
    done = []
    at = 0
    for x, d in both + own:
        shape = list(x.shape)
        shape[d] //= n
        size = x.size // n
        done.append(flat[at : at + size].reshape(shape))
        at += size
    norm1, norm2, grad_a, grad_bo, bq, bk, bv, featq, featk, grad_ao = done
    return (
        output,
        grad_tokens,
        norm1,
        grad_qkv[:, :qw],
        grad_qkv[:, qw : qw + kw],
        grad_qkv[:, qw + kw :],
        grad_a[:rank].T,
        bq,
        grad_a[rank : 2 * rank].T,
        bk,
        grad_a[2 * rank :].T,
        bv,
        featq,
        featk,
        grad_wo.T,
        grad_ao,
        grad_bo,
        norm2,
        grad_gate,
        grad_up,
        grad_down,
    )


def solution(mesh):
    placed = (
        P("seq", None),
        P(),
        P(None, "kv"),
        P(None, "kv"),
        P(None, "kv"),
        P(),
        P(None, "kv", None),
        P(),
        P(None, "kv", None),
        P(),
        P(None, "kv", None),
        P("kv", None, None),
        P("kv", None, None),
        P("kv", None),
        P("kv", None, None),
        P(),
        P(),
        P(None, "kv"),
        P(None, "kv"),
        P("kv", None),
        P("seq"),
        P("seq", None),
    )
    return jax.shard_map(
        local,
        mesh=mesh,
        in_specs=placed,
        out_specs=(
            P("seq", None),
            P("seq", None),
            P("seq"),
            P("seq", "kv"),
            P("seq", "kv"),
            P("seq", "kv"),
            P("seq", None),
            P(None, "kv", "seq"),
            P("seq", None),
            P(None, "kv", "seq"),
            P("seq", None),
            P(None, "kv", "seq"),
            P("kv", "seq", None),
            P("kv", "seq", None),
            P("kv", "seq"),
            P("kv", "seq", None),
            P(None, "seq"),
            P("seq"),
            P("seq", "kv"),
            P("seq", "kv"),
            P("kv", "seq"),
        ),
        check_vma=False,
    )
```

```python
import jax
import jax.numpy as jnp
from jax import lax
from jax.experimental import pallas as pl
from jax.experimental.pallas import tpu as pltpu
from jax.sharding import PartitionSpec as P

WIN = 64
CHUNK = 128
ANY = pl.BlockSpec(memory_space=pl.ANY)
EPSILON = 1e-05
EXACT = lax.Precision.HIGHEST
F32 = jnp.float32
BF16 = jnp.bfloat16


def cost(us):
    return pl.CostEstimate(flops=int(us * 0.45e9), bytes_accessed=1, transcendentals=0)


def dot(a, b, out=F32):
    return jnp.dot(a, b, preferred_element_type=F32).astype(out)


def dot_nt(a, b, out=F32):
    return lax.dot_general(a, b, (((1,), (1,)), ((), ())), preferred_element_type=F32).astype(out)


def dot_tn(a, b, out=F32):
    return lax.dot_general(a, b, (((0,), (0,)), ((), ())), preferred_element_type=F32).astype(out)


def dot_tt(a, b, out=F32):
    return lax.dot_general(a, b, (((0,), (1,)), ((), ())), preferred_element_type=F32).astype(out)


def tie(*xs):
    return lax.optimization_barrier(xs)


def add(terms):
    total = terms[0].astype(F32)
    for t in terms[1:]:
        total = total + t.astype(F32)
    return total


def take(x, i):
    return lax.dynamic_index_in_dim(x, i, 0, False)


class Grid:
    def __init__(self):
        self.kv = lax.axis_size("kv")
        self.seq = lax.axis_size("seq")
        self.outer = self.kv // 2
        self.line = self.seq // 2
        k = lax.axis_index("kv")
        s = lax.axis_index("seq")
        self.core, self.y = k % 2, k // 2
        self.x, self.z = s % 2, s // 2
        self.s = s
        self.core_swap = [(i, i ^ 1) for i in range(self.kv)]
        self.x_swap = [(i, i ^ 1) for i in range(self.seq)]
        self.z_groups = [[2 * z + x for z in range(self.line)] for x in range(2)]

    def y_shift(self, j):
        m = self.outer
        return [(y * 2 + c, (y + j) % m * 2 + c) for y in range(m) for c in range(2)]

    def own_rows(self, x, parts):
        rows, width = x.shape
        cut = x.reshape(parts, 2, rows // (2 * parts), width)
        return lax.dynamic_index_in_dim(cut, self.core, 1, False).reshape(rows // 2, width)

    def across_cores(self, x):
        return lax.ppermute(x, "kv", self.core_swap)

    def blocks_across(self, x):
        rows = x.shape[0] // 4
        return [self.across_cores(x[i * rows : (i + 1) * rows]) for i in range(4)]

    def core_sum(self, keep, send):
        return sum_rows(keep, self.blocks_across(send))

    def swap(self, x):
        return lax.ppermute(x, "seq", self.x_swap)

    def pair_sum(self, keep, got):
        return sum_rows(keep, [got])

    def outer_terms(self, half):
        terms = [half] + [lax.ppermute(half, "kv", self.y_shift(j)) for j in range(1, self.outer)]
        if self.outer == 2:
            return terms
        stack = jnp.stack(terms)
        return [take(stack, (self.y - i) % self.outer) for i in range(self.outer)]

    def gather_rows(self, own, out=BF16):
        return merge_rows(self.core, own, self.blocks_across(own), out)

    def sum_kv(self, x):
        x = x + lax.ppermute(x, "kv", self.core_swap).astype(F32)
        total = x
        for j in range(1, self.outer):
            total = total + lax.ppermute(x, "kv", self.y_shift(j))
        return total

    def line_scatter(self, part):
        return lax.psum_scatter(
            part, "seq", scatter_dimension=0, tiled=True, axis_index_groups=self.z_groups
        )

    def pair_half(self, x):
        return take(x.reshape(2, x.shape[0] // 2, x.shape[1]), 1 - self.x)

    def scatter_blocks(self, blocks):
        cut = blocks.reshape(self.line, 2, -1)
        other = lax.dynamic_index_in_dim(cut, 1 - self.x, 1, False).astype(BF16)
        own = lax.dynamic_index_in_dim(cut, self.x, 1, False)
        part = own + lax.ppermute(other, "seq", self.x_swap).astype(F32)
        total = take(part, self.z)
        m = self.line
        for j in range(1, m):
            pairs = [(z * 2 + x, (z + j) % m * 2 + x) for z in range(m) for x in range(2)]
            out = take(part, (self.z + j) % m).astype(BF16)
            total = total + lax.ppermute(out, "seq", pairs).astype(F32)
        return total

    def shift_seq(self, x, by):
        n = self.seq
        pairs = [(i, i + by) for i in range(n) if 0 <= i + by < n]
        return lax.ppermute(x, "seq", pairs)

    def sum_before(self, x, sign, kind):
        near = self.shift_seq(x.astype(kind), sign).astype(F32)
        total = x + near
        by = 2
        while by < self.seq:
            total = total + self.shift_seq(total.astype(kind), sign * by).astype(F32)
            by *= 2
        return total - x, near


def softmax_pair(logits):
    top = jnp.exp(logits - jnp.max(logits, 0, keepdims=True))
    low = jnp.exp(jnp.min(logits, 0, keepdims=True) - logits)
    return top * (1.0 / jnp.sum(top, 0, keepdims=True)), low * (1.0 / jnp.sum(low, 0, keepdims=True))


def softmax_pair_back(p, n, grad):
    hd = p.shape[0]
    up, un = p * grad[:hd], n * grad[hd:]
    return up - p * jnp.sum(up, 0, keepdims=True) - (un - n * jnp.sum(un, 0, keepdims=True))


def halves(x):
    top = x.astype(BF16)
    return top, (x - top.astype(F32)).astype(BF16)


def dot2(x, b):
    top, rest = halves(x)
    return dot(top, b) + dot(rest, b)


def value_rows(v, keep):
    hd, n = v.shape
    ones = (lax.broadcasted_iota(jnp.int32, (16, n), 0) == 0).astype(F32)
    return (jnp.concatenate([v.astype(F32), ones], 0) * keep).astype(BF16)


def key_kernel(kv_ref, map_ref, keep_ref, phi_cols_ref, phi_ref, k_ref, v_ref, state_ref):
    hk, hd = map_ref.shape[:2]
    for g in range(hk):
        k = kv_ref[g * hd : (g + 1) * hd, :]
        v = kv_ref[(hk + g) * hd : (hk + g + 1) * hd, :]
        p, n = softmax_pair(dot(map_ref[g], k))
        phi = jnp.concatenate([p, n], 0)
        phi_cols_ref[g] = phi.astype(BF16)
        phi_ref[g] = phi.T.astype(BF16)
        kv = jnp.concatenate([k, v], 0).astype(F32).T
        k_ref[g] = kv[:, :hd].astype(BF16)
        v_ref[g] = kv[:, hd:].astype(BF16)
        state_ref[g] = dot_nt(value_rows(v, keep_ref[...]), phi.astype(BF16))


def masks(open_ref, base):
    shape = (2 * CHUNK, CHUNK)
    a = lax.broadcasted_iota(jnp.int32, shape, 0)
    b = lax.broadcasted_iota(jnp.int32, shape, 1)
    start = open_ref[:, pl.ds(base, CHUNK)] - base
    doc = a >= start
    near = a > b + (CHUNK - WIN)
    return doc & near & (a <= b + CHUNK), doc & ~near, (start < 0).astype(F32)


def lanes(parts):
    return jnp.concatenate(parts, 1)


def attend_kernel(
    q_ref, kv_ref, phi_cols_ref, phi_ref, k_ref, map_ref, prior_ref, open_ref, keep_ref, cont_ref,
    heads_ref, total_ref, states_ref, state,
):
    hk, hd = phi_ref.shape[0], map_ref.shape[1]
    hq = map_ref.shape[0]
    group = hq // hk
    scale = hd**-0.5
    state[...] = prior_ref[...]

    def chunk(i, _):
        base = pl.multiple_of(i * CHUNK, CHUNK)
        here = pl.ds(base, CHUNK)
        keys = pl.ds(base, 2 * CHUNK)
        win, lin, far = masks(open_ref, base)
        for g in range(hk):
            q = [q_ref[h * hd : (h + 1) * hd, here] for h in range(g * group, (g + 1) * group)]
            phi = []
            for j in range(group):
                p, n = softmax_pair(dot(map_ref[g * group + j], q[j]))
                phi.append(jnp.concatenate([p, n], 0).astype(BF16))
            phi4 = lanes(phi)
            past = state[g]
            states_ref[i, g] = past
            scores = dot(k_ref[g, keys, :], lanes(q)) * scale
            linear = dot(phi_ref[g, keys, :], phi4)
            carried = dot2(past, phi4)
            weights = []
            totals = []
            for j in range(group):
                cut = slice(j * CHUNK, (j + 1) * CHUNK)
                w = jnp.where(win, jnp.exp(scores[:, cut]), 0.0) + jnp.where(lin, linear[:, cut], 0.0)
                weights.append(w.astype(BF16))
                totals.append(jnp.sum(w, 0, keepdims=True) + far * carried[hd : hd + 1, cut])
            v = kv_ref[(hk + g) * hd : (hk + g + 1) * hd, keys]
            mixed = dot(v, lanes(weights))
            for j in range(group):
                cut = slice(j * CHUNK, (j + 1) * CHUNK)
                h = g * group + j
                out = (mixed[:, cut] + far * carried[:hd, cut]) * (1.0 / totals[j])
                heads_ref[h * hd : (h + 1) * hd, here] = out.astype(BF16)
                total_ref[h : h + 1, here] = totals[j]
            own = value_rows(kv_ref[(hk + g) * hd : (hk + g + 1) * hd, here], keep_ref[:, here])
            state[g] = cont_ref[i] * past + dot_nt(own, phi_cols_ref[g, :, here])
        return 0

    lax.fori_loop(0, heads_ref.shape[1] // CHUNK, chunk, 0)


def attend_back_kernel(
    q_ref, kv_ref, phi_cols_ref, phi_ref, k_ref, v_ref, map_ref, map_t_ref, states_ref, heads_ref,
    total_ref, g_ref, open_ref, keep_ref, cont_ref,
    gq_ref, feat_ref, gk_ref, gv_ref, gphi_ref, first_ref, gl_ref, grad_t,
):
    hk, hd = phi_ref.shape[0], map_ref.shape[1]
    hq = map_ref.shape[0]
    group = hq // hk
    scale = hd**-0.5
    count = heads_ref.shape[1] // CHUNK
    first_ref[...] = jnp.zeros_like(first_ref)
    grad_t[...] = jnp.zeros_like(grad_t)
    gk_ref[...] = jnp.zeros_like(gk_ref)
    gv_ref[...] = jnp.zeros_like(gv_ref)
    gphi_ref[...] = jnp.zeros_like(gphi_ref)

    def chunk(step, _):
        i = count - 1 - step
        base = pl.multiple_of(i * CHUNK, CHUNK)
        here = pl.ds(base, CHUNK)
        keys = pl.ds(base, 2 * CHUNK)
        win, lin, far = masks(open_ref, base)
        for g in range(hk):
            rows = [slice(h * hd, (h + 1) * hd) for h in range(g * group, (g + 1) * group)]
            key_rows = slice(g * hd, (g + 1) * hd)
            value_row = slice((hk + g) * hd, (hk + g + 1) * hd)
            q4 = lanes([q_ref[r, here] for r in rows])
            g4 = lanes([g_ref[r, here] for r in rows])
            pairs = [softmax_pair(dot(map_ref[g * group + j], q_ref[rows[j], here])) for j in range(group)]
            phi = [jnp.concatenate([p, n], 0) for p, n in pairs]
            phi4 = lanes([x.astype(BF16) for x in phi])
            scores = dot(k_ref[g, keys, :], q4) * scale
            linear = dot(phi_ref[g, keys, :], phi4)
            g_w = dot(v_ref[g, keys, :], g4)
            shares, g_scores, g_linear, g_ext = [], [], [], []
            for j in range(group):
                cut = slice(j * CHUNK, (j + 1) * CHUNK)
                h = g * group + j
                inv = 1.0 / total_ref[h : h + 1, here]
                g_here = g_ref[rows[j], here].astype(F32)
                g_total = -inv * jnp.sum(g_here * heads_ref[rows[j], here].astype(F32), 0, keepdims=True)
                ex = jnp.where(win, jnp.exp(scores[:, cut]), 0.0)
                w = ex + jnp.where(lin, linear[:, cut], 0.0)
                shares.append((w * inv).astype(BF16))
                g_weight = g_w[:, cut] * inv + g_total
                g_scores.append((g_weight * ex).astype(BF16))
                g_linear.append(jnp.where(lin, g_weight, 0.0).astype(BF16))
                row = lax.broadcasted_iota(jnp.int32, (16, CHUNK), 0) == 0
                g_ext.append(
                    (jnp.concatenate([g_here * inv, jnp.where(row, g_total, 0.0)], 0) * far).astype(BF16)
                )
            shares, g_scores, g_linear, g_ext = map(lanes, (shares, g_scores, g_linear, g_ext))
            gv_ref[key_rows, keys] += dot_nt(g4, shares)
            gk_ref[key_rows, keys] += dot_nt(q4, g_scores) * scale
            gphi_ref[g, :, keys] += dot_nt(phi4, g_linear)
            g_query = dot(kv_ref[key_rows, keys], g_scores) * scale
            past = states_ref[i, g].T
            g_phi = dot(phi_cols_ref[g, :, keys], g_linear) + dot2(past, g_ext)
            for j in range(group):
                cut = slice(j * CHUNK, (j + 1) * CHUNK)
                gl = softmax_pair_back(*pairs[j], g_phi[:, cut]).astype(BF16)
                gl_ref[rows[j], here] = gl
                gq = g_query[:, cut] + dot(map_t_ref[g * group + j], gl)
                gq_ref[rows[j], here] = gq.astype(BF16)
            keep = keep_ref[:, here]
            own = value_rows(kv_ref[value_row, here], keep)
            gphi_ref[g, :, here] += dot2(grad_t[g], own)
            gv_ref[key_rows, here] += dot2(first_ref[g, :hd, :], phi_cols_ref[g, :, here]) * keep
            cont = cont_ref[i]
            first_ref[g] = cont * first_ref[g] + dot_nt(g_ext, phi4)
            grad_t[g] = cont * grad_t[g] + dot_nt(phi4, g_ext)
        return 0

    lax.fori_loop(0, count, chunk, 0)
    for h in range(hq):
        r = slice(h * hd, (h + 1) * hd)
        feat_ref[h] = dot_nt(q_ref[r, :], gl_ref[r, :])


def key_back_kernel(
    kv_ref, phi_cols_ref, map_ref, map_t_ref, gk_ref, gv_ref, gphi_ref, edge_ref, later_ref, last_ref,
    keep_ref, g_ref, feat_ref,
):
    hk, hd = map_ref.shape[:2]
    n = kv_ref.shape[1]
    cut = n - CHUNK

    def joined(own, edge):
        return jnp.concatenate([own[:, : cut - CHUNK], own[:, cut - CHUNK :] + edge.astype(F32)], 1)

    for g in range(hk):
        key_rows = slice(g * hd, (g + 1) * hd)
        k = kv_ref[key_rows, CHUNK:]
        v = kv_ref[(hk + g) * hd : (hk + g + 1) * hd, CHUNK:]
        keep = keep_ref[:, CHUNK:]
        phi = phi_cols_ref[g, :, CHUNK:]
        own = value_rows(v, keep)
        one = value_rows(v[:, cut - CHUNK :], jnp.ones((1, CHUNK), F32))
        later, last = later_ref[g], last_ref[g]
        g_phi = gphi_ref[g, :, CHUNK:] + lanes(
            [dot2(later.T, own[:, : cut - CHUNK]), dot2(last.T, one)]
        )
        g_phi = joined(g_phi, edge_ref[2 * hk * hd + g * 2 * hd : 2 * hk * hd + (g + 1) * 2 * hd, :])
        g_v = gv_ref[key_rows, CHUNK:] + lanes(
            [
                dot2(later[:hd], phi[:, : cut - CHUNK]) * keep[:, : cut - CHUNK],
                dot2(last[:hd], phi[:, cut - CHUNK :]),
            ]
        )
        g_v = joined(g_v, edge_ref[(hk + g) * hd : (hk + g + 1) * hd, :])
        g_ref[(hk + g) * hd : (hk + g + 1) * hd, :] = g_v.astype(BF16)
        p, q = softmax_pair(dot(map_ref[g], k))
        gl = softmax_pair_back(p, q, g_phi).astype(BF16)
        g_k = joined(gk_ref[key_rows, CHUNK:], edge_ref[key_rows, :]) + dot(map_t_ref[g], gl)
        g_ref[key_rows, :] = g_k.astype(BF16)
        feat_ref[g] = dot_nt(k, gl)


def call(us, kernel, outs, args, scratch=(), smem=(), after=()):
    count = len(args)
    vmem = pl.BlockSpec(memory_space=pltpu.VMEM)
    specs = [pl.BlockSpec(memory_space=pltpu.SMEM) if i in smem else vmem for i in range(len(args))]
    return pl.pallas_call(
        lambda *refs: kernel(*refs[:count], *refs[count + len(after) :]),
        out_shape=[jax.ShapeDtypeStruct(s, d) for s, d in outs],
        in_specs=specs + [ANY] * len(after),
        out_specs=[vmem] * len(outs),
        scratch_shapes=[pltpu.VMEM(s, d) for s, d in scratch],
        compiler_params=pltpu.CompilerParams(vmem_limit_bytes=48 * 2**20),
        cost_estimate=cost(us),
    )(*args, *after)


def sum_rows(keep, got):
    rows, width = keep.shape
    count = len(got)
    steps = max(count, 4)
    tile = rows // steps

    def kernel(keep_ref, *refs):
        *got_refs, out_ref = refs
        if count == 1:
            out_ref[...] = (keep_ref[...].astype(F32) + got_refs[0][...].astype(F32)).astype(BF16)
        else:
            for i in range(count):

                @pl.when(pl.program_id(0) == i)
                def _(i=i):
                    out_ref[...] = (keep_ref[...].astype(F32) + got_refs[i][...].astype(F32)).astype(BF16)

    block = pl.BlockSpec((tile, width), lambda i: (i, 0))
    fixed = pl.BlockSpec((tile, width), lambda i: (0, 0))
    return pl.pallas_call(
        kernel,
        grid=(steps,),
        in_specs=[block] + [block if count == 1 else fixed] * count,
        out_specs=block,
        out_shape=jax.ShapeDtypeStruct((rows, width), BF16),
        compiler_params=pltpu.CompilerParams(vmem_limit_bytes=32 * 2**20),
        cost_estimate=cost(2.5),
    )(keep, *got)


def merge_rows(core, own, other, out):
    rows, width = own.shape
    tile = rows // 4

    def kernel(core_ref, own_ref, *refs):
        *other_refs, out_ref = refs
        for b in range(8):
            c, k, h = b // 4, (b // 2) % 2, b % 2

            @pl.when((pl.program_id(0) == b) & (core_ref[0] == k))
            def _(at=2 * c + h):
                out_ref[...] = own_ref[at * tile : (at + 1) * tile, :].astype(out)

            @pl.when((pl.program_id(0) == b) & (core_ref[0] != k))
            def _(at=2 * c + h):
                out_ref[...] = other_refs[at][...].astype(out)

    return pl.pallas_call(
        kernel,
        grid_spec=pltpu.PrefetchScalarGridSpec(
            num_scalar_prefetch=1,
            grid=(8,),
            in_specs=[pl.BlockSpec((rows, width), lambda i, s: (0, 0))]
            + [pl.BlockSpec((tile, width), lambda i, s: (0, 0))] * 4,
            out_specs=pl.BlockSpec((tile, width), lambda i, s: (i, 0)),
        ),
        out_shape=jax.ShapeDtypeStruct((2 * rows, width), out),
        compiler_params=pltpu.CompilerParams(vmem_limit_bytes=32 * 2**20),
        cost_estimate=cost(3.5),
    )(core.astype(jnp.int32)[None], own, *other)


def finish(select, whole, got, turned):
    rows, n = got.shape

    def kernel(sel, own_ref, got_ref, out_ref):
        def put(ref):
            value = ref[...].astype(F32)
            out_ref[...] = value.T if turned else value

        here = pl.program_id(0) == sel[0]

        @pl.when(here)
        def _():
            put(own_ref)

        @pl.when(jnp.logical_not(here))
        def _():
            put(got_ref)

    block = (n, rows) if turned else (rows, n)
    return pl.pallas_call(
        kernel,
        grid_spec=pltpu.PrefetchScalarGridSpec(
            num_scalar_prefetch=1,
            grid=(2,),
            in_specs=[
                pl.BlockSpec((rows, n), lambda j, s: (s[0], 0)),
                pl.BlockSpec((rows, n), lambda j, s: (0, 0)),
            ],
            out_specs=pl.BlockSpec(block, (lambda j, s: (j, 0)) if turned else (lambda j, s: (0, j))),
        ),
        out_shape=jax.ShapeDtypeStruct((2 * n, rows) if turned else (rows, 2 * n), F32),
        compiler_params=pltpu.CompilerParams(vmem_limit_bytes=32 * 2**20),
        cost_estimate=cost(1.0),
    )(select.astype(jnp.int32)[None], whole, got)


def project_kernel(
    x_ref, gain_ref, wq_ref, wk_ref, wv_ref, down_ref, up_ref, normed_ref, q_ref, kv_ref, low_ref
):
    x = x_ref[...].astype(F32)
    rms = lax.rsqrt(jnp.mean(x * x, -1, keepdims=True) + EPSILON)
    normed = (x * rms * gain_ref[...].astype(F32)).astype(BF16)
    normed_ref[...] = normed
    low, rest = halves(dot(normed, down_ref[...]))
    low_ref[...] = low
    qw, kw = wq_ref.shape[1], wk_ref.shape[1]

    def rows(weight, at, width):
        up = up_ref[:, at : at + width]
        return (dot(normed, weight[...]) + dot(low, up) + dot(rest, up)).T.astype(BF16)

    kv_ref[:kw, :] = rows(wk_ref, qw, kw)
    kv_ref[kw:, :] = rows(wv_ref, qw + kw, kw)
    q_ref[...] = rows(wq_ref, 0, qw)


def project(tokens, gain, wq, wk, wv, down, up, tile=256):
    t, d = tokens.shape
    qw, kw = wq.shape[1], wk.shape[1]
    whole = lambda a: pl.BlockSpec(a.shape, lambda i: (0,) * a.ndim)
    row = lambda w: pl.BlockSpec((tile, w), lambda i: (i, 0))
    col = lambda h: pl.BlockSpec((h, tile), lambda i: (0, i))
    gain = gain[None]
    return pl.pallas_call(
        project_kernel,
        grid=(t // tile,),
        in_specs=[row(d)] + [whole(a) for a in (gain, wq, wk, wv, down, up)],
        out_specs=[row(d), col(qw), col(2 * kw), row(down.shape[1])],
        out_shape=[
            jax.ShapeDtypeStruct((t, d), BF16),
            jax.ShapeDtypeStruct((qw, t), BF16),
            jax.ShapeDtypeStruct((2 * kw, t), BF16),
            jax.ShapeDtypeStruct((t, down.shape[1]), BF16),
        ],
        compiler_params=pltpu.CompilerParams(vmem_limit_bytes=48 * 2**20),
        cost_estimate=cost(10.0),
    )(tokens, gain, wq, wk, wv, down, up)


def matmul(pairs, mode, chosen, out, split=None, tile=512, after=()):
    a0, b0 = pairs[0]
    over = 0 if mode in ("left", "both") else 1
    rows = a0.shape[1 - over]
    half = a0.shape[over]
    width = {"rows": b0.shape[0] // 2, "columns": b0.shape[0], "both": b0.shape[0]}.get(mode, b0.shape[1])
    tile = min(tile, width)
    product = {"rows": dot_nt, "columns": dot_nt, "inner": dot, "left": dot_tn, "both": dot_tt}[mode]
    b_spec = {
        "rows": pl.BlockSpec((tile, half), lambda i, s: (s[0] * (width // tile) + i, 0)),
        "columns": pl.BlockSpec((tile, half), lambda i, s: (i, s[0])),
        "inner": pl.BlockSpec((half, tile), lambda i, s: (s[0], i)),
        "left": pl.BlockSpec((half, tile), lambda i, s: (0, i)),
        "both": pl.BlockSpec((tile, half), lambda i, s: (i, 0)),
    }[mode]
    specs, args = [], []
    for a, b in pairs:
        specs += [pl.BlockSpec(a.shape, lambda i, s: (0, 0)), b_spec]
        args += [a, b]
    sub = rows // 4
    core = jnp.zeros((), jnp.int32) if split is None else split

    def kernel(sel, *refs):
        used = refs[: 2 * len(pairs)]
        outs = refs[2 * len(pairs) + len(after) :]

        def block(start):
            total = None
            for a_ref, b_ref in zip(used[::2], used[1::2]):
                a = a_ref[pl.ds(start, sub), :] if over else a_ref[:, pl.ds(start, sub)]
                term = product(a, b_ref[...])
                total = term if total is None else total + term
            return total.astype(out)

        for c in range(2):
            for k in range(2):
                if split is None:
                    at = (2 * c + k) * sub
                    outs[0][at : at + sub, :] = block(at)
                else:
                    other = sel[1] if k == 0 else 1 - sel[1]
                    start = pl.multiple_of((2 * c + other) * sub, sub)
                    outs[k][c * sub : (c + 1) * sub, :] = block(start)

    n_out = 1 if split is None else 2
    us = 1.0 + sum(a.size for a, _ in pairs) * width * 1.5e-9
    made = pl.pallas_call(
        kernel,
        grid_spec=pltpu.PrefetchScalarGridSpec(
            num_scalar_prefetch=1,
            grid=(width // tile,),
            in_specs=specs + [ANY] * len(after),
            out_specs=[pl.BlockSpec((rows // n_out, tile), lambda i, s: (0, i))] * n_out,
        ),
        out_shape=[jax.ShapeDtypeStruct((rows // n_out, width), out)] * n_out,
        compiler_params=pltpu.CompilerParams(vmem_limit_bytes=56 * 2**20),
        cost_estimate=cost(us),
    )(jnp.stack([chosen, core]).astype(jnp.int32), *args, *after)
    return made if split is not None else made[0]


def grad_pair(count, pairs, after=()):
    rows, width = pairs[0][0].shape
    n = pairs[0][1].shape[1]
    block = width // count
    specs = [pl.BlockSpec((rows, block), lambda j: (0, j)), pl.BlockSpec((rows, n), lambda j: (0, 0))]

    def kernel(*refs):
        value = dot_tn(refs[0][...], refs[1][...])
        for i in range(1, len(pairs)):
            value = value + dot_tn(refs[2 * i][...], refs[2 * i + 1][...])
        refs[-1][...] = value.astype(BF16)

    return pl.pallas_call(
        kernel,
        grid=(count,),
        in_specs=specs * len(pairs) + [ANY] * len(after),
        out_specs=pl.BlockSpec((block, n), lambda j: (j, 0)),
        out_shape=jax.ShapeDtypeStruct((width, n), BF16),
        compiler_params=pltpu.CompilerParams(vmem_limit_bytes=48 * 2**20),
        cost_estimate=cost(13.0),
    )(*[x for pair in pairs for x in pair], *after)


def grad_block(line, select, a, b, product, got=None, after=()):
    rows, width = a.shape
    block = width // (2 * line)
    n = b.shape[0] if product is dot_tt else b.shape[1]
    more = [] if got is None else [got]

    def kernel(sel, a_ref, b_ref, *rest):
        value = product(a_ref[...], b_ref[...])
        if got is not None:
            value = value + rest[0][...].astype(F32)
        rest[-1][...] = value.astype(BF16)

    spec = pl.BlockSpec((block, n), lambda j, s: (j, 0))
    return pl.pallas_call(
        kernel,
        grid_spec=pltpu.PrefetchScalarGridSpec(
            num_scalar_prefetch=1,
            grid=(line,),
            in_specs=[
                pl.BlockSpec((rows, block), lambda j, s: (0, 2 * j + s[0])),
                pl.BlockSpec(b.shape, lambda j, s: (0, 0)),
            ]
            + [spec] * len(more)
            + [ANY] * len(after),
            out_specs=spec,
        ),
        out_shape=jax.ShapeDtypeStruct((line * block, n), BF16),
        compiler_params=pltpu.CompilerParams(vmem_limit_bytes=48 * 2**20),
        cost_estimate=cost(1.0),
    )(select.astype(jnp.int32)[None], a, b, *more, *after)


def gated_kernel(sel_ref, own_ref, other_ref, wg_ref, wu_ref, gh_ref, *refs):
    normed_ref, hidden_ref, gate_ref, up_ref = refs[-4:]
    half = own_ref.shape[0]

    @pl.when(pl.program_id(0) == 0)
    def _():
        first = sel_ref[0] == 0

        @pl.when(first)
        def _():
            normed_ref[:half, :] = own_ref[...]
            normed_ref[half:, :] = other_ref[...]

        @pl.when(jnp.logical_not(first))
        def _():
            normed_ref[:half, :] = other_ref[...]
            normed_ref[half:, :] = own_ref[...]

    for r in range(0, 2 * half, half):
        cut = slice(r, r + half)
        x = normed_ref[cut, :]
        gate = dot(x, wg_ref[...])
        up = dot(x, wu_ref[...])
        sig = 1.0 / (1.0 + jnp.exp(-gate))
        silu = gate * sig
        hidden_ref[cut, :] = (silu * up).astype(BF16)
        g = gh_ref[cut, :].astype(F32)
        gate_ref[cut, :] = (g * up * (sig + silu * (1.0 - sig))).astype(BF16)
        up_ref[cut, :] = (g * silu).astype(BF16)


def gated(c, rows, sel, own, other, wg, wu, gh, held, after, tile=256):
    half, d = own.shape
    f = wg.shape[1] // 2
    here = pl.BlockSpec((2 * half, tile), lambda i, s: (c, i))
    weight = pl.BlockSpec((d, tile), lambda i, s: (0, s[1] * (f // tile) + i))
    shapes = [jax.ShapeDtypeStruct((rows, d), BF16)] + [jax.ShapeDtypeStruct((rows, f), BF16)] * 3
    return pl.pallas_call(
        gated_kernel,
        grid_spec=pltpu.PrefetchScalarGridSpec(
            num_scalar_prefetch=1,
            grid=(f // tile,),
            in_specs=[
                pl.BlockSpec((half, d), lambda i, s: (0, 0)),
                pl.BlockSpec((half, d), lambda i, s: (0, 0)),
                weight,
                weight,
                here,
            ]
            + [ANY] * (len(held) + len(after)),
            out_specs=[pl.BlockSpec((2 * half, d), lambda i, s: (c, 0)), here, here, here],
        ),
        out_shape=shapes,
        input_output_aliases={6 + i: i for i in range(len(held))},
        compiler_params=pltpu.CompilerParams(vmem_limit_bytes=56 * 2**20),
        cost_estimate=cost(11.0),
    )(sel, own, other, wg, wu, gh, *held, *after)


def local(
    tokens,
    gain_one,
    query_weight,
    key_weight,
    value_weight,
    query_down,
    query_up,
    key_down,
    key_up,
    value_down,
    value_up,
    query_map,
    key_map,
    output_weight,
    output_down,
    output_up,
    gain_two,
    gate_weight,
    up_weight,
    down_weight,
    start_mask,
    cotangent,
):
    grid = Grid()
    rows = tokens.shape[0]
    rank = query_down.shape[1]
    hd = key_map.shape[-1]
    hk = key_map.shape[0]
    hq = query_map.shape[0]
    group = hq // hk
    count = rows // CHUNK
    length = rows + CHUNK
    index = jnp.arange(rows, dtype=jnp.int32)
    starts = jnp.where(start_mask == 1, index + CHUNK, jnp.int32(-1))
    opened = jnp.max(jnp.where(index[:, None] <= index[None, :], starts[:, None], jnp.int32(-1)), 0)
    ends = jnp.concatenate([jnp.full((1,), -1, jnp.int32), opened[CHUNK - 1 : -1 : CHUNK]])
    cont = (ends < jnp.arange(count, dtype=jnp.int32) * CHUNK).astype(F32)
    place = jnp.arange(length, dtype=jnp.int32)
    ends_at = jnp.concatenate([jnp.repeat(ends, CHUNK), jnp.full((CHUNK,), length, jnp.int32)])
    keep = (place >= ends_at).astype(F32)[None]
    keep_all = ((place >= ends[count - 1]) & (place < rows)).astype(F32)[None]
    opened = opened[None]

    g1 = gain_one.astype(F32)
    g2 = gain_two.astype(F32)
    qup, kup, vup = (u.reshape(rank, -1) for u in (query_up, key_up, value_up))
    qw, kw = hq * hd, hk * hd
    wide = 128 - 3 * rank
    up_all = jnp.pad(jax.scipy.linalg.block_diag(qup, kup, vup), ((0, wide), (0, 0)))
    down_all = jnp.pad(jnp.concatenate([query_down, key_down, value_down], 1), ((0, 0), (0, wide)))
    normed_one, query, kv, low_all = project(
        tokens, gain_one, query_weight, key_weight, value_weight, down_all, up_all
    )
    edge = grid.shift_seq(kv[:, rows - CHUNK :], 1)
    kv = jnp.concatenate([edge, kv], 1)

    query_map_t = jnp.swapaxes(query_map, 1, 2)
    key_map_t = jnp.swapaxes(key_map, 1, 2)
    phi_dim = 2 * hd
    phi_cols, phi, key, value, state = call(
        2.0,
        key_kernel,
        [
            ((hk, phi_dim, length), BF16),
            ((hk, length, phi_dim), BF16),
            ((hk, length, hd), BF16),
            ((hk, length, hd), BF16),
            ((hk, hd + 16, phi_dim), F32),
        ],
        (kv, key_map_t, keep_all),
    )
    prior, _ = grid.sum_before(state, 1, F32)
    parts = 2
    chunk = rows // parts
    core, mine = grid.core.astype(jnp.int32), grid.x.astype(jnp.int32)
    g_hidden = matmul([(cotangent, down_weight)], "rows", mine, F32)
    oup = output_up
    odown = output_down.reshape(-1, rank)
    weight_o = (output_weight.astype(F32) + dot(odown, oup)).astype(BF16)
    weight_qkv = jnp.concatenate([query_weight, key_weight, value_weight], 1)
    weight_qkv = (weight_qkv.astype(F32) + dot(down_all, up_all)).astype(BF16)
    cot_own = grid.own_rows(cotangent, parts)
    prior, g_hidden, weight_o, weight_qkv, cot_own = tie(
        prior, g_hidden, weight_o, weight_qkv, cot_own
    )
    cot_got = grid.swap(cot_own)
    heads, totals, states = call(
        9.0,
        attend_kernel,
        [((qw, rows), BF16), ((hq, rows), F32), ((count, hk, hd + 16, phi_dim), F32)],
        (query, kv, phi_cols, phi, key, query_map_t, prior, opened, keep, cont),
        scratch=[((hk, hd + 16, phi_dim), F32)],
        smem=(9,),
    )

    kept, sent = matmul([(heads, weight_o)], "left", mine, BF16, core)
    cuts = [slice(c * chunk // 2, (c + 1) * chunk // 2) for c in range(parts)]
    half = [grid.core_sum(kept[cut], sent[cut]) for cut in cuts]
    own_tokens = [grid.own_rows(tokens[c * chunk : (c + 1) * chunk], 1) for c in range(parts)]
    own_tokens[0], half[1] = tie(own_tokens[0], half[1])
    terms = [grid.outer_terms(h) for h in half]
    held, held_pair = (), ()
    resid, rms_two, own, got = [], [], [], []
    select = jnp.stack([core, mine])

    def normed(c):
        r = own_tokens[c].astype(F32) + add(terms[c])
        rms = lax.rsqrt(jnp.mean(r * r, -1, keepdims=True) + EPSILON)
        resid.append(r)
        rms_two.append(rms)
        own.append((r * rms * g2).astype(BF16))
        got.append(None)

    def inner(c, mine_c, gh, held, after):
        return gated(
            c, rows, select, mine_c, grid.across_cores(mine_c), gate_weight, up_weight, gh, held, after
        )

    normed(0)
    got[0] = grid.swap(own[0])
    held = list(inner(0, own[0], g_hidden, held, []))
    cot_got, held[2] = tie(cot_got, held[2])
    terms[1][-1], held[1] = tie(terms[1][-1], held[1])
    normed(1)
    got[1] = grid.swap(own[1])
    cot_got, mark = tie(cot_got, own[1])
    cot_pair = grid.gather_rows(cot_got)
    g_pair = matmul([(cot_pair, down_weight)], "rows", mine, F32, after=[mark])
    held = list(inner(1, own[1], g_hidden, held, [g_pair]))
    got[0], held[1] = tie(got[0], held[1])
    held_pair = list(inner(0, got[0], g_pair, held_pair, [held[1]]))
    got[1], held_pair[1] = tie(got[1], held_pair[1])
    held_pair = inner(1, got[1], g_pair, held_pair, [])
    normed_two, hidden, g_gate, g_up = held
    normed_pair, hidden_pair, gate_pair, up_pair = held_pair
    resid = jnp.concatenate(resid, 0)
    rms_two = jnp.concatenate(rms_two, 0)

    count_d = 2 * grid.line
    yours = 1 - mine

    def to_pair(a, b, product=dot_tn, after=()):
        return grad_block(grid.line, yours, a, b, product, None, after)

    def from_pair(a, b, got, product=dot_tn, after=()):
        return grad_block(grid.line, mine, a, b, product, got, after)

    w_d = grad_pair(count_d, [(cotangent, hidden), (cot_pair, hidden_pair)])
    grad_d = grid.line_scatter(w_d)
    kept, sent = matmul(
        [(gate_pair, gate_weight), (up_pair, up_weight)], "columns", mine, BF16, core, after=[w_d]
    )
    theirs = grid.core_sum(kept, sent)
    kept, sent = matmul(
        [(g_gate, gate_weight), (g_up, up_weight)], "columns", mine, BF16, core, after=[kept]
    )
    ours = grid.core_sum(kept, sent)
    w_g = grad_pair(count_d, [(normed_two, g_gate), (normed_pair, gate_pair)], after=[kept])
    theirs = grid.swap(theirs)
    theirs, w_g = tie(theirs, w_g)
    grad_g = grid.line_scatter(w_g)
    half = grid.pair_sum(ours, theirs)
    terms = grid.outer_terms(half)
    down_theirs = matmul([(hidden_pair, down_weight)], "inner", mine, BF16, core, after=[half])
    down_ours = matmul([(hidden, down_weight)], "inner", mine, BF16, core, after=[down_theirs[0]])
    w_u = grad_pair(
        count_d, [(normed_two, g_up), (normed_pair, up_pair)], after=[down_ours[0]]
    )
    terms[-1], w_u, *down_ours = tie(terms[-1], w_u, *down_ours)
    grad_u = grid.line_scatter(w_u)

    g_two = add(terms)
    norm2_part = jnp.sum(g_two * resid * rms_two, 0)
    s_two = g_two * g2
    g_resid = (
        cot_own.astype(F32)
        + rms_two * s_two
        - resid * rms_two**3 * jnp.mean(resid * s_two, -1, keepdims=True)
    )
    own_attn = g_resid.astype(BF16)
    g_attn = grid.gather_rows(own_attn)
    down_got = grid.swap(grid.core_sum(*down_theirs))
    down_half = grid.core_sum(*down_ours)

    g_heads = dot_nt(weight_o, g_attn, BF16)
    g_q, featq_part, gk, gv, gphi, first = call(
        24.0,
        attend_back_kernel,
        [
            ((qw, rows), BF16),
            ((hq, hd, hd), F32),
            ((kw, length), F32),
            ((kw, length), F32),
            ((hk, phi_dim, length), F32),
            ((hk, hd + 16, phi_dim), F32),
        ],
        (
            query, kv, phi_cols, phi, key, value, query_map_t, query_map, states, heads,
            totals, g_heads, opened, keep, cont,
        ),
        scratch=[((qw, rows), BF16), ((hk, phi_dim, hd + 16), F32)],
        smem=(14,),
        after=[grad_d],
    )
    first, down_got, down_half = tie(first, down_got, down_half)
    down_half = grid.pair_sum(down_half, down_got)
    later, near = grid.sum_before(first, -1, BF16)
    back = [gk[:, :CHUNK], gv[:, :CHUNK], gphi[:, :, :CHUNK].reshape(hk * phi_dim, CHUNK)]
    back = grid.shift_seq(jnp.concatenate(back, 0).astype(BF16), -1)
    s_o = to_pair(g_attn, heads, dot_tt, after=[g_q])
    r_o = grid.swap(s_o)
    g_kv, featk_part = call(
        2.0,
        key_back_kernel,
        [((2 * kw, rows), BF16), ((hk, hd, hd), F32)],
        (kv, phi_cols, key_map_t, key_map, gk, gv, gphi, back, later, later - near, keep_all),
        after=[s_o],
    )

    g_qkv = jnp.concatenate([g_q, g_kv], 0)
    kept, sent = matmul([(g_qkv, weight_qkv)], "both", mine, BF16, core)
    half = grid.core_sum(kept, sent)
    half, down_half = tie(half, down_half)
    terms = grid.outer_terms(half)
    down_terms = grid.outer_terms(down_half)
    s_qkv = to_pair(normed_one, g_qkv, dot_tt, after=[half])
    r_qkv = grid.swap(s_qkv)
    g_late, s_qkv = tie(g_attn, s_qkv)
    g_low_o = dot_nt(g_late, oup, BF16)
    low_o = dot_tn(odown, heads, BF16)
    bo_part = dot(low_o, g_late)
    ao_part = dot(heads, g_low_o)
    k_o = from_pair(g_attn, heads, r_o, dot_tt, after=[s_qkv])
    g_low = dot(up_all, g_qkv, BF16)
    a_part = dot(g_low, normed_one)
    b_part = dot_tt(low_all, g_qkv)
    bq_part = b_part[:rank, :qw]
    bk_part = b_part[rank : 2 * rank, qw : qw + kw]
    bv_part = b_part[2 * rank : 3 * rank, qw + kw :]
    n = grid.seq

    def blocks(x, dim):
        shape = x.shape
        x = x.reshape(shape[:dim] + (n, shape[dim] // n) + shape[dim + 1 :])
        return jnp.moveaxis(x, dim, 0).reshape(n, -1)

    both = [(a_part[: 3 * rank], 1), (bo_part, 1)]
    alone = [
        (norm2_part + lax.ppermute(norm2_part, "kv", grid.core_swap), 0),
        (bq_part.reshape(query_up.shape), 2),
        (bk_part.reshape(key_up.shape), 2),
        (bv_part.reshape(value_up.shape), 2),
        (featq_part, 1),
        (featk_part, 1),
        (ao_part.reshape(output_down.shape), 1),
    ]
    cut = [blocks(x, d) for x, d in both + alone]
    bundle = jnp.concatenate(cut, 1)
    terms[-1], bundle, r_qkv, grad_g, k_o = tie(terms[-1], bundle, r_qkv, grad_g, k_o)
    k_qkv = from_pair(normed_one, g_qkv, r_qkv, dot_tt, after=[k_o])

    terms[-1], k_qkv = tie(terms[-1], k_qkv)
    grad_oq = grid.line_scatter(jnp.concatenate([k_o, k_qkv], 1))
    stream = grid.own_rows(tokens, parts).astype(F32)
    rms_one = lax.rsqrt(jnp.mean(stream * stream, -1, keepdims=True) + EPSILON)
    g_one = add(terms)
    norm1_part = jnp.sum(g_one * stream * rms_one, 0)
    s_one = g_one * g1
    own_grad = (
        g_resid
        + rms_one * s_one
        - stream * rms_one**3 * jnp.mean(stream * s_one, -1, keepdims=True)
    ).astype(BF16)
    grad_tokens = grid.gather_rows(own_grad, F32)
    down_terms[-1], grad_tokens = tie(down_terms[-1], grad_tokens)
    fins = grid.swap(jnp.concatenate([grid.pair_half(g) for g in (grad_d, grad_g, grad_u)], 0))
    down_terms[-1], fins = tie(down_terms[-1], fins)
    fins = jnp.split(fins, 3, 0)
    grad_down = finish(mine, grad_d, fins[0], True)
    grad_gate = finish(mine, grad_g, fins[1], False)
    grad_up = finish(mine, grad_u, fins[2], False)
    output = grid.gather_rows((resid + add(down_terms)).astype(BF16))
    grad_wo, grad_qkv = grad_oq[:, :qw].astype(F32), grad_oq[:, qw:].astype(F32)
    norm1 = norm1_part + lax.ppermute(norm1_part, "kv", grid.core_swap)
    norm1 = grid.scatter_blocks(norm1.reshape(n, -1))
    summed = grid.scatter_blocks(bundle)
    n_both = sum(c.shape[1] for c in cut[: len(both)])
    flat = jnp.concatenate([grid.sum_kv(summed[:n_both].astype(BF16)), summed[n_both:]])
    done = []
    at = 0
    for x, d in both + alone:
        shape = list(x.shape)
        shape[d] //= n
        size = x.size // n
        done.append(flat[at : at + size].reshape(shape))
        at += size
    grad_a, grad_bo, norm2, bq, bk, bv, featq, featk, grad_ao = done
    return (
        output,
        grad_tokens,
        norm1,
        grad_qkv[:, :qw],
        grad_qkv[:, qw : qw + kw],
        grad_qkv[:, qw + kw :],
        grad_a[:rank].T,
        bq,
        grad_a[rank : 2 * rank].T,
        bk,
        grad_a[2 * rank :].T,
        bv,
        featq,
        featk,
        grad_wo.T,
        grad_ao,
        grad_bo,
        norm2,
        grad_gate,
        grad_up,
        grad_down,
    )


def solution(mesh):
    placed = (
        P("seq", None),
        P(),
        P(None, "kv"),
        P(None, "kv"),
        P(None, "kv"),
        P(),
        P(None, "kv", None),
        P(),
        P(None, "kv", None),
        P(),
        P(None, "kv", None),
        P("kv", None, None),
        P("kv", None, None),
        P("kv", None),
        P("kv", None, None),
        P(),
        P(),
        P(None, "kv"),
        P(None, "kv"),
        P("kv", None),
        P("seq"),
        P("seq", None),
    )
    return jax.shard_map(
        local,
        mesh=mesh,
        in_specs=placed,
        out_specs=(
            P("seq", None),
            P("seq", None),
            P("seq"),
            P("seq", "kv"),
            P("seq", "kv"),
            P("seq", "kv"),
            P("seq", None),
            P(None, "kv", "seq"),
            P("seq", None),
            P(None, "kv", "seq"),
            P("seq", None),
            P(None, "kv", "seq"),
            P("kv", "seq", None),
            P("kv", "seq", None),
            P("kv", "seq"),
            P("kv", "seq", None),
            P(None, "seq"),
            P("seq"),
            P("seq", "kv"),
            P("seq", "kv"),
            P("kv", "seq"),
        ),
        check_vma=False,
    )
```

```python
import jax
import jax.numpy as jnp
from jax import lax
from jax.experimental import pallas as pl
from jax.experimental.pallas import tpu as pltpu
from jax.sharding import PartitionSpec as P

WIN = 64
CHUNK = 128
ANY = pl.BlockSpec(memory_space=pl.ANY)
EPSILON = 1e-05
EXACT = lax.Precision.HIGHEST
F32 = jnp.float32
BF16 = jnp.bfloat16


def cost(us):
    return pl.CostEstimate(flops=int(us * 0.45e9), bytes_accessed=1, transcendentals=0)


def dot(a, b, out=F32):
    return jnp.dot(a, b, preferred_element_type=F32).astype(out)


def dot_nt(a, b, out=F32):
    return lax.dot_general(a, b, (((1,), (1,)), ((), ())), preferred_element_type=F32).astype(out)


def dot_tn(a, b, out=F32):
    return lax.dot_general(a, b, (((0,), (0,)), ((), ())), preferred_element_type=F32).astype(out)


def dot_tt(a, b, out=F32):
    return lax.dot_general(a, b, (((0,), (1,)), ((), ())), preferred_element_type=F32).astype(out)


def tie(*xs):
    return lax.optimization_barrier(xs)


def add(terms):
    total = terms[0].astype(F32)
    for t in terms[1:]:
        total = total + t.astype(F32)
    return total


def take(x, i):
    return lax.dynamic_index_in_dim(x, i, 0, False)


class Grid:
    def __init__(self):
        self.kv = lax.axis_size("kv")
        self.seq = lax.axis_size("seq")
        self.outer = self.kv // 2
        self.line = self.seq // 2
        k = lax.axis_index("kv")
        s = lax.axis_index("seq")
        self.core, self.y = k % 2, k // 2
        self.x, self.z = s % 2, s // 2
        self.s = s
        self.core_swap = [(i, i ^ 1) for i in range(self.kv)]
        self.x_swap = [(i, i ^ 1) for i in range(self.seq)]
        self.z_groups = [[2 * z + x for z in range(self.line)] for x in range(2)]

    def y_shift(self, j):
        m = self.outer
        return [(y * 2 + c, (y + j) % m * 2 + c) for y in range(m) for c in range(2)]

    def own_rows(self, x, parts):
        rows, width = x.shape
        cut = x.reshape(parts, 2, rows // (2 * parts), width)
        return lax.dynamic_index_in_dim(cut, self.core, 1, False).reshape(rows // 2, width)

    def across_cores(self, x):
        return lax.ppermute(x, "kv", self.core_swap)

    def blocks_across(self, x):
        rows = x.shape[0] // 4
        return [self.across_cores(x[i * rows : (i + 1) * rows]) for i in range(4)]

    def core_sum(self, keep, send):
        return sum_rows(keep, self.blocks_across(send))

    def swap(self, x):
        return lax.ppermute(x, "seq", self.x_swap)

    def pair_sum(self, keep, got):
        return sum_rows(keep, [got])

    def outer_terms(self, half):
        terms = [half] + [lax.ppermute(half, "kv", self.y_shift(j)) for j in range(1, self.outer)]
        if self.outer == 2:
            return terms
        stack = jnp.stack(terms)
        return [take(stack, (self.y - i) % self.outer) for i in range(self.outer)]

    def gather_rows(self, own, out=BF16):
        return merge_rows(self.core, own, self.blocks_across(own), out)

    def sum_kv(self, x):
        x = x + lax.ppermute(x, "kv", self.core_swap).astype(F32)
        total = x
        for j in range(1, self.outer):
            total = total + lax.ppermute(x, "kv", self.y_shift(j))
        return total

    def line_scatter(self, part):
        return lax.psum_scatter(
            part, "seq", scatter_dimension=0, tiled=True, axis_index_groups=self.z_groups
        )

    def pair_half(self, x):
        return take(x.reshape(2, x.shape[0] // 2, x.shape[1]), 1 - self.x)

    def scatter_blocks(self, blocks):
        cut = blocks.reshape(self.line, 2, -1)
        other = lax.dynamic_index_in_dim(cut, 1 - self.x, 1, False).astype(BF16)
        own = lax.dynamic_index_in_dim(cut, self.x, 1, False)
        part = own + lax.ppermute(other, "seq", self.x_swap).astype(F32)
        total = take(part, self.z)
        m = self.line
        for j in range(1, m):
            pairs = [(z * 2 + x, (z + j) % m * 2 + x) for z in range(m) for x in range(2)]
            out = take(part, (self.z + j) % m).astype(BF16)
            total = total + lax.ppermute(out, "seq", pairs).astype(F32)
        return total

    def shift_seq(self, x, by):
        n = self.seq
        pairs = [(i, i + by) for i in range(n) if 0 <= i + by < n]
        return lax.ppermute(x, "seq", pairs)

    def sum_before(self, x, sign, kind):
        near = self.shift_seq(x.astype(kind), sign).astype(F32)
        total = x + near
        by = 2
        while by < self.seq:
            total = total + self.shift_seq(total.astype(kind), sign * by).astype(F32)
            by *= 2
        return total - x, near


def softmax_pair(logits):
    top = jnp.exp(logits - jnp.max(logits, 0, keepdims=True))
    low = jnp.exp(jnp.min(logits, 0, keepdims=True) - logits)
    return top * (1.0 / jnp.sum(top, 0, keepdims=True)), low * (1.0 / jnp.sum(low, 0, keepdims=True))


def softmax_pair_back(p, n, grad):
    hd = p.shape[0]
    up, un = p * grad[:hd], n * grad[hd:]
    return up - p * jnp.sum(up, 0, keepdims=True) - (un - n * jnp.sum(un, 0, keepdims=True))


def halves(x):
    top = x.astype(BF16)
    return top, (x - top.astype(F32)).astype(BF16)


def dot2(x, b):
    top, rest = halves(x)
    return dot(top, b) + dot(rest, b)


def value_rows(v, keep):
    hd, n = v.shape
    ones = (lax.broadcasted_iota(jnp.int32, (16, n), 0) == 0).astype(F32)
    return (jnp.concatenate([v.astype(F32), ones], 0) * keep).astype(BF16)


def key_kernel(kv_ref, map_ref, keep_ref, phi_cols_ref, phi_ref, k_ref, v_ref, state_ref):
    hk, hd = map_ref.shape[:2]
    for g in range(hk):
        k = kv_ref[g * hd : (g + 1) * hd, :]
        v = kv_ref[(hk + g) * hd : (hk + g + 1) * hd, :]
        p, n = softmax_pair(dot(map_ref[g], k))
        phi = jnp.concatenate([p, n], 0)
        phi_cols_ref[g] = phi.astype(BF16)
        phi_ref[g] = phi.T.astype(BF16)
        kv = jnp.concatenate([k, v], 0).astype(F32).T
        k_ref[g] = kv[:, :hd].astype(BF16)
        v_ref[g] = kv[:, hd:].astype(BF16)
        state_ref[g] = dot_nt(value_rows(v, keep_ref[...]), phi.astype(BF16))


def masks(open_ref, base):
    shape = (2 * CHUNK, CHUNK)
    a = lax.broadcasted_iota(jnp.int32, shape, 0)
    b = lax.broadcasted_iota(jnp.int32, shape, 1)
    start = open_ref[:, pl.ds(base, CHUNK)] - base
    doc = a >= start
    near = a > b + (CHUNK - WIN)
    return doc & near & (a <= b + CHUNK), doc & ~near, (start < 0).astype(F32)


def lanes(parts):
    return jnp.concatenate(parts, 1)


def attend_kernel(
    q_ref, kv_ref, phi_cols_ref, phi_ref, k_ref, map_ref, prior_ref, open_ref, keep_ref, cont_ref,
    heads_ref, total_ref, states_ref, state,
):
    hk, hd = phi_ref.shape[0], map_ref.shape[1]
    hq = map_ref.shape[0]
    group = hq // hk
    scale = hd**-0.5
    state[...] = prior_ref[...]

    def chunk(i, _):
        base = pl.multiple_of(i * CHUNK, CHUNK)
        here = pl.ds(base, CHUNK)
        keys = pl.ds(base, 2 * CHUNK)
        win, lin, far = masks(open_ref, base)
        for g in range(hk):
            q = [q_ref[h * hd : (h + 1) * hd, here] for h in range(g * group, (g + 1) * group)]
            phi = []
            for j in range(group):
                p, n = softmax_pair(dot(map_ref[g * group + j], q[j]))
                phi.append(jnp.concatenate([p, n], 0).astype(BF16))
            phi4 = lanes(phi)
            past = state[g]
            states_ref[i, g] = past
            scores = dot(k_ref[g, keys, :], lanes(q)) * scale
            linear = dot(phi_ref[g, keys, :], phi4)
            carried = dot2(past, phi4)
            weights = []
            totals = []
            for j in range(group):
                cut = slice(j * CHUNK, (j + 1) * CHUNK)
                w = jnp.where(win, jnp.exp(scores[:, cut]), 0.0) + jnp.where(lin, linear[:, cut], 0.0)
                weights.append(w.astype(BF16))
                totals.append(jnp.sum(w, 0, keepdims=True) + far * carried[hd : hd + 1, cut])
            v = kv_ref[(hk + g) * hd : (hk + g + 1) * hd, keys]
            mixed = dot(v, lanes(weights))
            for j in range(group):
                cut = slice(j * CHUNK, (j + 1) * CHUNK)
                h = g * group + j
                out = (mixed[:, cut] + far * carried[:hd, cut]) * (1.0 / totals[j])
                heads_ref[h * hd : (h + 1) * hd, here] = out.astype(BF16)
                total_ref[h : h + 1, here] = totals[j]
            own = value_rows(kv_ref[(hk + g) * hd : (hk + g + 1) * hd, here], keep_ref[:, here])
            state[g] = cont_ref[i] * past + dot_nt(own, phi_cols_ref[g, :, here])
        return 0

    lax.fori_loop(0, heads_ref.shape[1] // CHUNK, chunk, 0)


def attend_back_kernel(
    q_ref, kv_ref, phi_cols_ref, phi_ref, k_ref, v_ref, map_ref, map_t_ref, states_ref, heads_ref,
    total_ref, g_ref, open_ref, keep_ref, cont_ref,
    gq_ref, feat_ref, gk_ref, gv_ref, gphi_ref, first_ref, gl_ref, grad_t,
):
    hk, hd = phi_ref.shape[0], map_ref.shape[1]
    hq = map_ref.shape[0]
    group = hq // hk
    scale = hd**-0.5
    count = heads_ref.shape[1] // CHUNK
    first_ref[...] = jnp.zeros_like(first_ref)
    grad_t[...] = jnp.zeros_like(grad_t)
    gk_ref[...] = jnp.zeros_like(gk_ref)
    gv_ref[...] = jnp.zeros_like(gv_ref)
    gphi_ref[...] = jnp.zeros_like(gphi_ref)

    def chunk(step, _):
        i = count - 1 - step
        base = pl.multiple_of(i * CHUNK, CHUNK)
        here = pl.ds(base, CHUNK)
        keys = pl.ds(base, 2 * CHUNK)
        win, lin, far = masks(open_ref, base)
        for g in range(hk):
            rows = [slice(h * hd, (h + 1) * hd) for h in range(g * group, (g + 1) * group)]
            key_rows = slice(g * hd, (g + 1) * hd)
            value_row = slice((hk + g) * hd, (hk + g + 1) * hd)
            q4 = lanes([q_ref[r, here] for r in rows])
            g4 = lanes([g_ref[r, here] for r in rows])
            pairs = [softmax_pair(dot(map_ref[g * group + j], q_ref[rows[j], here])) for j in range(group)]
            phi = [jnp.concatenate([p, n], 0) for p, n in pairs]
            phi4 = lanes([x.astype(BF16) for x in phi])
            scores = dot(k_ref[g, keys, :], q4) * scale
            linear = dot(phi_ref[g, keys, :], phi4)
            g_w = dot(v_ref[g, keys, :], g4)
            shares, g_scores, g_linear, g_ext = [], [], [], []
            for j in range(group):
                cut = slice(j * CHUNK, (j + 1) * CHUNK)
                h = g * group + j
                inv = 1.0 / total_ref[h : h + 1, here]
                g_here = g_ref[rows[j], here].astype(F32)
                g_total = -inv * jnp.sum(g_here * heads_ref[rows[j], here].astype(F32), 0, keepdims=True)
                ex = jnp.where(win, jnp.exp(scores[:, cut]), 0.0)
                w = ex + jnp.where(lin, linear[:, cut], 0.0)
                shares.append((w * inv).astype(BF16))
                g_weight = g_w[:, cut] * inv + g_total
                g_scores.append((g_weight * ex).astype(BF16))
                g_linear.append(jnp.where(lin, g_weight, 0.0).astype(BF16))
                row = lax.broadcasted_iota(jnp.int32, (16, CHUNK), 0) == 0
                g_ext.append(
                    (jnp.concatenate([g_here * inv, jnp.where(row, g_total, 0.0)], 0) * far).astype(BF16)
                )
            shares, g_scores, g_linear, g_ext = map(lanes, (shares, g_scores, g_linear, g_ext))
            gv_ref[key_rows, keys] += dot_nt(g4, shares)
            gk_ref[key_rows, keys] += dot_nt(q4, g_scores) * scale
            gphi_ref[g, :, keys] += dot_nt(phi4, g_linear)
            g_query = dot(kv_ref[key_rows, keys], g_scores) * scale
            past = states_ref[i, g].T
            g_phi = dot(phi_cols_ref[g, :, keys], g_linear) + dot2(past, g_ext)
            for j in range(group):
                cut = slice(j * CHUNK, (j + 1) * CHUNK)
                gl = softmax_pair_back(*pairs[j], g_phi[:, cut]).astype(BF16)
                gl_ref[rows[j], here] = gl
                gq = g_query[:, cut] + dot(map_t_ref[g * group + j], gl)
                gq_ref[rows[j], here] = gq.astype(BF16)
            keep = keep_ref[:, here]
            own = value_rows(kv_ref[value_row, here], keep)
            gphi_ref[g, :, here] += dot2(grad_t[g], own)
            gv_ref[key_rows, here] += dot2(first_ref[g, :hd, :], phi_cols_ref[g, :, here]) * keep
            cont = cont_ref[i]
            first_ref[g] = cont * first_ref[g] + dot_nt(g_ext, phi4)
            grad_t[g] = cont * grad_t[g] + dot_nt(phi4, g_ext)
        return 0

    lax.fori_loop(0, count, chunk, 0)
    for h in range(hq):
        r = slice(h * hd, (h + 1) * hd)
        feat_ref[h] = dot_nt(q_ref[r, :], gl_ref[r, :])


def key_back_kernel(
    kv_ref, phi_cols_ref, map_ref, map_t_ref, gk_ref, gv_ref, gphi_ref, edge_ref, later_ref, last_ref,
    keep_ref, g_ref, feat_ref,
):
    hk, hd = map_ref.shape[:2]
    n = kv_ref.shape[1]
    cut = n - CHUNK

    def joined(own, edge):
        return jnp.concatenate([own[:, : cut - CHUNK], own[:, cut - CHUNK :] + edge.astype(F32)], 1)

    for g in range(hk):
        key_rows = slice(g * hd, (g + 1) * hd)
        k = kv_ref[key_rows, CHUNK:]
        v = kv_ref[(hk + g) * hd : (hk + g + 1) * hd, CHUNK:]
        keep = keep_ref[:, CHUNK:]
        phi = phi_cols_ref[g, :, CHUNK:]
        own = value_rows(v, keep)
        one = value_rows(v[:, cut - CHUNK :], jnp.ones((1, CHUNK), F32))
        later, last = later_ref[g], last_ref[g]
        g_phi = gphi_ref[g, :, CHUNK:] + lanes(
            [dot2(later.T, own[:, : cut - CHUNK]), dot2(last.T, one)]
        )
        g_phi = joined(g_phi, edge_ref[2 * hk * hd + g * 2 * hd : 2 * hk * hd + (g + 1) * 2 * hd, :])
        g_v = gv_ref[key_rows, CHUNK:] + lanes(
            [
                dot2(later[:hd], phi[:, : cut - CHUNK]) * keep[:, : cut - CHUNK],
                dot2(last[:hd], phi[:, cut - CHUNK :]),
            ]
        )
        g_v = joined(g_v, edge_ref[(hk + g) * hd : (hk + g + 1) * hd, :])
        g_ref[(hk + g) * hd : (hk + g + 1) * hd, :] = g_v.astype(BF16)
        p, q = softmax_pair(dot(map_ref[g], k))
        gl = softmax_pair_back(p, q, g_phi).astype(BF16)
        g_k = joined(gk_ref[key_rows, CHUNK:], edge_ref[key_rows, :]) + dot(map_t_ref[g], gl)
        g_ref[key_rows, :] = g_k.astype(BF16)
        feat_ref[g] = dot_nt(k, gl)


def call(us, kernel, outs, args, scratch=(), smem=(), after=()):
    count = len(args)
    vmem = pl.BlockSpec(memory_space=pltpu.VMEM)
    specs = [pl.BlockSpec(memory_space=pltpu.SMEM) if i in smem else vmem for i in range(len(args))]
    return pl.pallas_call(
        lambda *refs: kernel(*refs[:count], *refs[count + len(after) :]),
        out_shape=[jax.ShapeDtypeStruct(s, d) for s, d in outs],
        in_specs=specs + [ANY] * len(after),
        out_specs=[vmem] * len(outs),
        scratch_shapes=[pltpu.VMEM(s, d) for s, d in scratch],
        compiler_params=pltpu.CompilerParams(vmem_limit_bytes=38 * 2**20),
        cost_estimate=cost(us),
    )(*args, *after)


def sum_rows(keep, got):
    rows, width = keep.shape
    count = len(got)
    steps = max(count, 4)
    tile = rows // steps

    def kernel(keep_ref, *refs):
        *got_refs, out_ref = refs
        if count == 1:
            out_ref[...] = (keep_ref[...].astype(F32) + got_refs[0][...].astype(F32)).astype(BF16)
        else:
            for i in range(count):

                @pl.when(pl.program_id(0) == i)
                def _(i=i):
                    out_ref[...] = (keep_ref[...].astype(F32) + got_refs[i][...].astype(F32)).astype(BF16)

    block = pl.BlockSpec((tile, width), lambda i: (i, 0))
    fixed = pl.BlockSpec((tile, width), lambda i: (0, 0))
    return pl.pallas_call(
        kernel,
        grid=(steps,),
        in_specs=[block] + [block if count == 1 else fixed] * count,
        out_specs=block,
        out_shape=jax.ShapeDtypeStruct((rows, width), BF16),
        compiler_params=pltpu.CompilerParams(vmem_limit_bytes=32 * 2**20),
        cost_estimate=cost(2.5),
    )(keep, *got)


def merge_rows(core, own, other, out):
    rows, width = own.shape
    tile = rows // 4

    def kernel(core_ref, own_ref, *refs):
        *other_refs, out_ref = refs
        for b in range(8):
            c, k, h = b // 4, (b // 2) % 2, b % 2

            @pl.when((pl.program_id(0) == b) & (core_ref[0] == k))
            def _(at=2 * c + h):
                out_ref[...] = own_ref[at * tile : (at + 1) * tile, :].astype(out)

            @pl.when((pl.program_id(0) == b) & (core_ref[0] != k))
            def _(at=2 * c + h):
                out_ref[...] = other_refs[at][...].astype(out)

    return pl.pallas_call(
        kernel,
        grid_spec=pltpu.PrefetchScalarGridSpec(
            num_scalar_prefetch=1,
            grid=(8,),
            in_specs=[pl.BlockSpec((rows, width), lambda i, s: (0, 0))]
            + [pl.BlockSpec((tile, width), lambda i, s: (0, 0))] * 4,
            out_specs=pl.BlockSpec((tile, width), lambda i, s: (i, 0)),
        ),
        out_shape=jax.ShapeDtypeStruct((2 * rows, width), out),
        compiler_params=pltpu.CompilerParams(vmem_limit_bytes=32 * 2**20),
        cost_estimate=cost(3.5),
    )(core.astype(jnp.int32)[None], own, *other)


def finish(select, whole, got, turned):
    rows, n = got.shape

    def kernel(sel, own_ref, got_ref, out_ref):
        def put(ref):
            value = ref[...].astype(F32)
            out_ref[...] = value.T if turned else value

        here = pl.program_id(0) == sel[0]

        @pl.when(here)
        def _():
            put(own_ref)

        @pl.when(jnp.logical_not(here))
        def _():
            put(got_ref)

    block = (n, rows) if turned else (rows, n)
    return pl.pallas_call(
        kernel,
        grid_spec=pltpu.PrefetchScalarGridSpec(
            num_scalar_prefetch=1,
            grid=(2,),
            in_specs=[
                pl.BlockSpec((rows, n), lambda j, s: (s[0], 0)),
                pl.BlockSpec((rows, n), lambda j, s: (0, 0)),
            ],
            out_specs=pl.BlockSpec(block, (lambda j, s: (j, 0)) if turned else (lambda j, s: (0, j))),
        ),
        out_shape=jax.ShapeDtypeStruct((2 * n, rows) if turned else (rows, 2 * n), F32),
        compiler_params=pltpu.CompilerParams(vmem_limit_bytes=32 * 2**20),
        cost_estimate=cost(1.0),
    )(select.astype(jnp.int32)[None], whole, got)


def project_kernel(
    x_ref, gain_ref, wq_ref, wk_ref, wv_ref, down_ref, up_ref, normed_ref, q_ref, kv_ref, low_ref
):
    x = x_ref[...].astype(F32)
    rms = lax.rsqrt(jnp.mean(x * x, -1, keepdims=True) + EPSILON)
    normed = (x * rms * gain_ref[...].astype(F32)).astype(BF16)
    normed_ref[...] = normed
    low, rest = halves(dot(normed, down_ref[...]))
    low_ref[...] = low
    qw, kw = wq_ref.shape[1], wk_ref.shape[1]

    def rows(weight, at, width):
        up = up_ref[:, at : at + width]
        return (dot(normed, weight[...]) + dot(low, up) + dot(rest, up)).T.astype(BF16)

    kv_ref[:kw, :] = rows(wk_ref, qw, kw)
    kv_ref[kw:, :] = rows(wv_ref, qw + kw, kw)
    q_ref[...] = rows(wq_ref, 0, qw)


def project(tokens, gain, wq, wk, wv, down, up, tile=256):
    t, d = tokens.shape
    qw, kw = wq.shape[1], wk.shape[1]
    whole = lambda a: pl.BlockSpec(a.shape, lambda i: (0,) * a.ndim)
    row = lambda w: pl.BlockSpec((tile, w), lambda i: (i, 0))
    col = lambda h: pl.BlockSpec((h, tile), lambda i: (0, i))
    gain = gain[None]
    return pl.pallas_call(
        project_kernel,
        grid=(t // tile,),
        in_specs=[row(d)] + [whole(a) for a in (gain, wq, wk, wv, down, up)],
        out_specs=[row(d), col(qw), col(2 * kw), row(down.shape[1])],
        out_shape=[
            jax.ShapeDtypeStruct((t, d), BF16),
            jax.ShapeDtypeStruct((qw, t), BF16),
            jax.ShapeDtypeStruct((2 * kw, t), BF16),
            jax.ShapeDtypeStruct((t, down.shape[1]), BF16),
        ],
        compiler_params=pltpu.CompilerParams(vmem_limit_bytes=38 * 2**20),
        cost_estimate=cost(10.0),
    )(tokens, gain, wq, wk, wv, down, up)


def matmul(pairs, mode, chosen, out, split=None, tile=512, after=()):
    a0, b0 = pairs[0]
    over = 0 if mode in ("left", "both") else 1
    rows = a0.shape[1 - over]
    half = a0.shape[over]
    width = {"rows": b0.shape[0] // 2, "columns": b0.shape[0], "both": b0.shape[0]}.get(mode, b0.shape[1])
    tile = min(tile, width)
    product = {"rows": dot_nt, "columns": dot_nt, "inner": dot, "left": dot_tn, "both": dot_tt}[mode]
    b_spec = {
        "rows": pl.BlockSpec((tile, half), lambda i, s: (s[0] * (width // tile) + i, 0)),
        "columns": pl.BlockSpec((tile, half), lambda i, s: (i, s[0])),
        "inner": pl.BlockSpec((half, tile), lambda i, s: (s[0], i)),
        "left": pl.BlockSpec((half, tile), lambda i, s: (0, i)),
        "both": pl.BlockSpec((tile, half), lambda i, s: (i, 0)),
    }[mode]
    specs, args = [], []
    for a, b in pairs:
        specs += [pl.BlockSpec(a.shape, lambda i, s: (0, 0)), b_spec]
        args += [a, b]
    sub = rows // 4
    core = jnp.zeros((), jnp.int32) if split is None else split

    def kernel(sel, *refs):
        used = refs[: 2 * len(pairs)]
        outs = refs[2 * len(pairs) + len(after) :]

        def block(start):
            total = None
            for a_ref, b_ref in zip(used[::2], used[1::2]):
                a = a_ref[pl.ds(start, sub), :] if over else a_ref[:, pl.ds(start, sub)]
                term = product(a, b_ref[...])
                total = term if total is None else total + term
            return total.astype(out)

        for c in range(2):
            for k in range(2):
                if split is None:
                    at = (2 * c + k) * sub
                    outs[0][at : at + sub, :] = block(at)
                else:
                    other = sel[1] if k == 0 else 1 - sel[1]
                    start = pl.multiple_of((2 * c + other) * sub, sub)
                    outs[k][c * sub : (c + 1) * sub, :] = block(start)

    n_out = 1 if split is None else 2
    us = 1.0 + sum(a.size for a, _ in pairs) * width * 1.5e-9
    made = pl.pallas_call(
        kernel,
        grid_spec=pltpu.PrefetchScalarGridSpec(
            num_scalar_prefetch=1,
            grid=(width // tile,),
            in_specs=specs + [ANY] * len(after),
            out_specs=[pl.BlockSpec((rows // n_out, tile), lambda i, s: (0, i))] * n_out,
        ),
        out_shape=[jax.ShapeDtypeStruct((rows // n_out, width), out)] * n_out,
        compiler_params=pltpu.CompilerParams(vmem_limit_bytes=38 * 2**20),
        cost_estimate=cost(us),
    )(jnp.stack([chosen, core]).astype(jnp.int32), *args, *after)
    return made if split is not None else made[0]


def grad_pair(count, pairs, after=()):
    rows, width = pairs[0][0].shape
    n = pairs[0][1].shape[1]
    block = width // count
    specs = [pl.BlockSpec((rows, block), lambda j: (0, j)), pl.BlockSpec((rows, n), lambda j: (0, 0))]

    def kernel(*refs):
        value = dot_tn(refs[0][...], refs[1][...])
        for i in range(1, len(pairs)):
            value = value + dot_tn(refs[2 * i][...], refs[2 * i + 1][...])
        refs[-1][...] = value.astype(BF16)

    return pl.pallas_call(
        kernel,
        grid=(count,),
        in_specs=specs * len(pairs) + [ANY] * len(after),
        out_specs=pl.BlockSpec((block, n), lambda j: (j, 0)),
        out_shape=jax.ShapeDtypeStruct((width, n), BF16),
        compiler_params=pltpu.CompilerParams(vmem_limit_bytes=38 * 2**20),
        cost_estimate=cost(13.0),
    )(*[x for pair in pairs for x in pair], *after)


def grad_block(line, select, a, b, product, got=None, after=()):
    rows, width = a.shape
    block = width // (2 * line)
    n = b.shape[0] if product is dot_tt else b.shape[1]
    more = [] if got is None else [got]

    def kernel(sel, a_ref, b_ref, *rest):
        value = product(a_ref[...], b_ref[...])
        if got is not None:
            value = value + rest[0][...].astype(F32)
        rest[-1][...] = value.astype(BF16)

    spec = pl.BlockSpec((block, n), lambda j, s: (j, 0))
    return pl.pallas_call(
        kernel,
        grid_spec=pltpu.PrefetchScalarGridSpec(
            num_scalar_prefetch=1,
            grid=(line,),
            in_specs=[
                pl.BlockSpec((rows, block), lambda j, s: (0, 2 * j + s[0])),
                pl.BlockSpec(b.shape, lambda j, s: (0, 0)),
            ]
            + [spec] * len(more)
            + [ANY] * len(after),
            out_specs=spec,
        ),
        out_shape=jax.ShapeDtypeStruct((line * block, n), BF16),
        compiler_params=pltpu.CompilerParams(vmem_limit_bytes=38 * 2**20),
        cost_estimate=cost(1.0),
    )(select.astype(jnp.int32)[None], a, b, *more, *after)


def gated_kernel(sel_ref, own_ref, other_ref, wg_ref, wu_ref, gh_ref, *refs):
    normed_ref, hidden_ref, gate_ref, up_ref = refs[-4:]
    half = own_ref.shape[0]

    @pl.when(pl.program_id(0) == 0)
    def _():
        first = sel_ref[0] == 0

        @pl.when(first)
        def _():
            normed_ref[:half, :] = own_ref[...]
            normed_ref[half:, :] = other_ref[...]

        @pl.when(jnp.logical_not(first))
        def _():
            normed_ref[:half, :] = other_ref[...]
            normed_ref[half:, :] = own_ref[...]

    for r in range(0, 2 * half, half):
        cut = slice(r, r + half)
        x = normed_ref[cut, :]
        gate = dot(x, wg_ref[...])
        up = dot(x, wu_ref[...])
        sig = 1.0 / (1.0 + jnp.exp(-gate))
        silu = gate * sig
        hidden_ref[cut, :] = (silu * up).astype(BF16)
        g = gh_ref[cut, :].astype(F32)
        gate_ref[cut, :] = (g * up * (sig + silu * (1.0 - sig))).astype(BF16)
        up_ref[cut, :] = (g * silu).astype(BF16)


def gated(c, rows, sel, own, other, wg, wu, gh, held, after, tile=256):
    half, d = own.shape
    f = wg.shape[1] // 2
    here = pl.BlockSpec((2 * half, tile), lambda i, s: (c, i))
    weight = pl.BlockSpec((d, tile), lambda i, s: (0, s[1] * (f // tile) + i))
    shapes = [jax.ShapeDtypeStruct((rows, d), BF16)] + [jax.ShapeDtypeStruct((rows, f), BF16)] * 3
    return pl.pallas_call(
        gated_kernel,
        grid_spec=pltpu.PrefetchScalarGridSpec(
            num_scalar_prefetch=1,
            grid=(f // tile,),
            in_specs=[
                pl.BlockSpec((half, d), lambda i, s: (0, 0)),
                pl.BlockSpec((half, d), lambda i, s: (0, 0)),
                weight,
                weight,
                here,
            ]
            + [ANY] * (len(held) + len(after)),
            out_specs=[pl.BlockSpec((2 * half, d), lambda i, s: (c, 0)), here, here, here],
        ),
        out_shape=shapes,
        input_output_aliases={6 + i: i for i in range(len(held))},
        compiler_params=pltpu.CompilerParams(vmem_limit_bytes=38 * 2**20),
        cost_estimate=cost(11.0),
    )(sel, own, other, wg, wu, gh, *held, *after)


def local(
    tokens,
    gain_one,
    query_weight,
    key_weight,
    value_weight,
    query_down,
    query_up,
    key_down,
    key_up,
    value_down,
    value_up,
    query_map,
    key_map,
    output_weight,
    output_down,
    output_up,
    gain_two,
    gate_weight,
    up_weight,
    down_weight,
    start_mask,
    cotangent,
):
    grid = Grid()
    rows = tokens.shape[0]
    rank = query_down.shape[1]
    hd = key_map.shape[-1]
    hk = key_map.shape[0]
    hq = query_map.shape[0]
    group = hq // hk
    count = rows // CHUNK
    length = rows + CHUNK
    index = jnp.arange(rows, dtype=jnp.int32)
    starts = jnp.where(start_mask == 1, index + CHUNK, jnp.int32(-1))
    opened = jnp.max(jnp.where(index[:, None] <= index[None, :], starts[:, None], jnp.int32(-1)), 0)
    ends = jnp.concatenate([jnp.full((1,), -1, jnp.int32), opened[CHUNK - 1 : -1 : CHUNK]])
    cont = (ends < jnp.arange(count, dtype=jnp.int32) * CHUNK).astype(F32)
    place = jnp.arange(length, dtype=jnp.int32)
    ends_at = jnp.concatenate([jnp.repeat(ends, CHUNK), jnp.full((CHUNK,), length, jnp.int32)])
    keep = (place >= ends_at).astype(F32)[None]
    keep_all = ((place >= ends[count - 1]) & (place < rows)).astype(F32)[None]
    opened = opened[None]

    g1 = gain_one.astype(F32)
    g2 = gain_two.astype(F32)
    qup, kup, vup = (u.reshape(rank, -1) for u in (query_up, key_up, value_up))
    qw, kw = hq * hd, hk * hd
    wide = 128 - 3 * rank
    up_all = jnp.pad(jax.scipy.linalg.block_diag(qup, kup, vup), ((0, wide), (0, 0)))
    down_all = jnp.pad(jnp.concatenate([query_down, key_down, value_down], 1), ((0, 0), (0, wide)))
    normed_one, query, kv, low_all = project(
        tokens, gain_one, query_weight, key_weight, value_weight, down_all, up_all
    )
    edge = grid.shift_seq(kv[:, rows - CHUNK :], 1)
    kv = jnp.concatenate([edge, kv], 1)

    query_map_t = jnp.swapaxes(query_map, 1, 2)
    key_map_t = jnp.swapaxes(key_map, 1, 2)
    phi_dim = 2 * hd
    phi_cols, phi, key, value, state = call(
        2.0,
        key_kernel,
        [
            ((hk, phi_dim, length), BF16),
            ((hk, length, phi_dim), BF16),
            ((hk, length, hd), BF16),
            ((hk, length, hd), BF16),
            ((hk, hd + 16, phi_dim), F32),
        ],
        (kv, key_map_t, keep_all),
    )
    prior, _ = grid.sum_before(state, 1, F32)
    parts = 2
    chunk = rows // parts
    core, mine = grid.core.astype(jnp.int32), grid.x.astype(jnp.int32)
    g_hidden = matmul([(cotangent, down_weight)], "rows", mine, F32)
    oup = output_up
    odown = output_down.reshape(-1, rank)
    weight_o = (output_weight.astype(F32) + dot(odown, oup)).astype(BF16)
    weight_qkv = jnp.concatenate([query_weight, key_weight, value_weight], 1)
    weight_qkv = (weight_qkv.astype(F32) + dot(down_all, up_all)).astype(BF16)
    cot_own = grid.own_rows(cotangent, parts)
    prior, g_hidden, weight_o, weight_qkv, cot_own = tie(
        prior, g_hidden, weight_o, weight_qkv, cot_own
    )
    cot_got = grid.swap(cot_own)
    heads, totals, states = call(
        9.0,
        attend_kernel,
        [((qw, rows), BF16), ((hq, rows), F32), ((count, hk, hd + 16, phi_dim), F32)],
        (query, kv, phi_cols, phi, key, query_map_t, prior, opened, keep, cont),
        scratch=[((hk, hd + 16, phi_dim), F32)],
        smem=(9,),
    )

    kept, sent = matmul([(heads, weight_o)], "left", mine, BF16, core)
    cuts = [slice(c * chunk // 2, (c + 1) * chunk // 2) for c in range(parts)]
    half = [grid.core_sum(kept[cut], sent[cut]) for cut in cuts]
    own_tokens = [grid.own_rows(tokens[c * chunk : (c + 1) * chunk], 1) for c in range(parts)]
    own_tokens[0], half[1] = tie(own_tokens[0], half[1])
    terms = [grid.outer_terms(h) for h in half]
    held, held_pair = (), ()
    resid, rms_two, own, got = [], [], [], []
    select = jnp.stack([core, mine])

    def normed(c):
        r = own_tokens[c].astype(F32) + add(terms[c])
        rms = lax.rsqrt(jnp.mean(r * r, -1, keepdims=True) + EPSILON)
        resid.append(r)
        rms_two.append(rms)
        own.append((r * rms * g2).astype(BF16))
        got.append(None)

    def inner(c, mine_c, gh, held, after):
        return gated(
            c, rows, select, mine_c, grid.across_cores(mine_c), gate_weight, up_weight, gh, held, after
        )

    normed(0)
    got[0] = grid.swap(own[0])
    held = list(inner(0, own[0], g_hidden, held, []))
    cot_got, held[2] = tie(cot_got, held[2])
    terms[1][-1], held[1] = tie(terms[1][-1], held[1])
    normed(1)
    got[1] = grid.swap(own[1])
    cot_got, mark = tie(cot_got, own[1])
    cot_pair = grid.gather_rows(cot_got)
    g_pair = matmul([(cot_pair, down_weight)], "rows", mine, F32, after=[mark])
    held = list(inner(1, own[1], g_hidden, held, [g_pair]))
    got[0], held[1] = tie(got[0], held[1])
    held_pair = list(inner(0, got[0], g_pair, held_pair, [held[1]]))
    got[1], held_pair[1] = tie(got[1], held_pair[1])
    held_pair = inner(1, got[1], g_pair, held_pair, [])
    normed_two, hidden, g_gate, g_up = held
    normed_pair, hidden_pair, gate_pair, up_pair = held_pair
    resid = jnp.concatenate(resid, 0)
    rms_two = jnp.concatenate(rms_two, 0)

    count_d = 2 * grid.line
    yours = 1 - mine

    def to_pair(a, b, product=dot_tn, after=()):
        return grad_block(grid.line, yours, a, b, product, None, after)

    def from_pair(a, b, got, product=dot_tn, after=()):
        return grad_block(grid.line, mine, a, b, product, got, after)

    w_d = grad_pair(count_d, [(cotangent, hidden), (cot_pair, hidden_pair)])
    grad_d = grid.line_scatter(w_d)
    kept, sent = matmul(
        [(gate_pair, gate_weight), (up_pair, up_weight)], "columns", mine, BF16, core, after=[w_d]
    )
    theirs = grid.core_sum(kept, sent)
    kept, sent = matmul(
        [(g_gate, gate_weight), (g_up, up_weight)], "columns", mine, BF16, core, after=[kept]
    )
    ours = grid.core_sum(kept, sent)
    w_g = grad_pair(count_d, [(normed_two, g_gate), (normed_pair, gate_pair)], after=[kept])
    theirs = grid.swap(theirs)
    theirs, w_g = tie(theirs, w_g)
    grad_g = grid.line_scatter(w_g)
    half = grid.pair_sum(ours, theirs)
    terms = grid.outer_terms(half)
    down_theirs = matmul([(hidden_pair, down_weight)], "inner", mine, BF16, core, after=[half])
    down_ours = matmul([(hidden, down_weight)], "inner", mine, BF16, core, after=[down_theirs[0]])
    w_u = grad_pair(
        count_d, [(normed_two, g_up), (normed_pair, up_pair)], after=[down_ours[0]]
    )
    terms[-1], w_u, *down_ours = tie(terms[-1], w_u, *down_ours)
    grad_u = grid.line_scatter(w_u)

    g_two = add(terms)
    norm2_part = jnp.sum(g_two * resid * rms_two, 0)
    s_two = g_two * g2
    g_resid = (
        cot_own.astype(F32)
        + rms_two * s_two
        - resid * rms_two**3 * jnp.mean(resid * s_two, -1, keepdims=True)
    )
    own_attn = g_resid.astype(BF16)
    g_attn = grid.gather_rows(own_attn)
    down_got = grid.swap(grid.core_sum(*down_theirs))
    down_half = grid.core_sum(*down_ours)

    g_heads = dot_nt(weight_o, g_attn, BF16)
    g_q, featq_part, gk, gv, gphi, first = call(
        24.0,
        attend_back_kernel,
        [
            ((qw, rows), BF16),
            ((hq, hd, hd), F32),
            ((kw, length), F32),
            ((kw, length), F32),
            ((hk, phi_dim, length), F32),
            ((hk, hd + 16, phi_dim), F32),
        ],
        (
            query, kv, phi_cols, phi, key, value, query_map_t, query_map, states, heads,
            totals, g_heads, opened, keep, cont,
        ),
        scratch=[((qw, rows), BF16), ((hk, phi_dim, hd + 16), F32)],
        smem=(14,),
        after=[grad_d],
    )
    first, down_got, down_half = tie(first, down_got, down_half)
    down_half = grid.pair_sum(down_half, down_got)
    later, near = grid.sum_before(first, -1, BF16)
    back = [gk[:, :CHUNK], gv[:, :CHUNK], gphi[:, :, :CHUNK].reshape(hk * phi_dim, CHUNK)]
    back = grid.shift_seq(jnp.concatenate(back, 0).astype(BF16), -1)
    s_o = to_pair(g_attn, heads, dot_tt, after=[g_q])
    r_o = grid.swap(s_o)
    g_kv, featk_part = call(
        2.0,
        key_back_kernel,
        [((2 * kw, rows), BF16), ((hk, hd, hd), F32)],
        (kv, phi_cols, key_map_t, key_map, gk, gv, gphi, back, later, later - near, keep_all),
        after=[s_o],
    )

    g_qkv = jnp.concatenate([g_q, g_kv], 0)
    kept, sent = matmul([(g_qkv, weight_qkv)], "both", mine, BF16, core)
    half = grid.core_sum(kept, sent)
    half, down_half = tie(half, down_half)
    terms = grid.outer_terms(half)
    down_terms = grid.outer_terms(down_half)
    s_qkv = to_pair(normed_one, g_qkv, dot_tt, after=[half])
    r_qkv = grid.swap(s_qkv)
    g_late, s_qkv = tie(g_attn, s_qkv)
    g_low_o = dot_nt(g_late, oup, BF16)
    low_o = dot_tn(odown, heads, BF16)
    bo_part = dot(low_o, g_late)
    ao_part = dot(heads, g_low_o)
    k_o = from_pair(g_attn, heads, r_o, dot_tt, after=[s_qkv])
    g_low = dot(up_all, g_qkv, BF16)
    a_part = dot(g_low, normed_one)
    b_part = dot_tt(low_all, g_qkv)
    bq_part = b_part[:rank, :qw]
    bk_part = b_part[rank : 2 * rank, qw : qw + kw]
    bv_part = b_part[2 * rank : 3 * rank, qw + kw :]
    n = grid.seq

    def blocks(x, dim):
        shape = x.shape
        x = x.reshape(shape[:dim] + (n, shape[dim] // n) + shape[dim + 1 :])
        return jnp.moveaxis(x, dim, 0).reshape(n, -1)

    both = [(a_part[: 3 * rank], 1), (bo_part, 1)]
    alone = [
        (norm2_part + lax.ppermute(norm2_part, "kv", grid.core_swap), 0),
        (bq_part.reshape(query_up.shape), 2),
        (bk_part.reshape(key_up.shape), 2),
        (bv_part.reshape(value_up.shape), 2),
        (featq_part, 1),
        (featk_part, 1),
        (ao_part.reshape(output_down.shape), 1),
    ]
    cut = [blocks(x, d) for x, d in both + alone]
    bundle = jnp.concatenate(cut, 1)
    terms[-1], bundle, r_qkv, grad_g, k_o = tie(terms[-1], bundle, r_qkv, grad_g, k_o)
    k_qkv = from_pair(normed_one, g_qkv, r_qkv, dot_tt, after=[k_o])

    terms[-1], k_qkv = tie(terms[-1], k_qkv)
    grad_oq = grid.line_scatter(jnp.concatenate([k_o, k_qkv], 1))
    stream = grid.own_rows(tokens, parts).astype(F32)
    rms_one = lax.rsqrt(jnp.mean(stream * stream, -1, keepdims=True) + EPSILON)
    g_one = add(terms)
    norm1_part = jnp.sum(g_one * stream * rms_one, 0)
    s_one = g_one * g1
    own_grad = (
        g_resid
        + rms_one * s_one
        - stream * rms_one**3 * jnp.mean(stream * s_one, -1, keepdims=True)
    ).astype(BF16)
    own_blocks = grid.blocks_across(own_grad)
    fins = grid.swap(jnp.concatenate([grid.pair_half(g) for g in (grad_d, grad_g, grad_u)], 0))
    own_grad, fins = tie(own_grad, fins)
    grad_tokens = merge_rows(grid.core, own_grad, own_blocks, F32)
    down_terms[-1], grad_tokens = tie(down_terms[-1], grad_tokens)
    down_terms[-1], fins = tie(down_terms[-1], fins)
    fins = jnp.split(fins, 3, 0)
    grad_down = finish(mine, grad_d, fins[0], True)
    grad_gate = finish(mine, grad_g, fins[1], False)
    grad_up = finish(mine, grad_u, fins[2], False)
    output = grid.gather_rows((resid + add(down_terms)).astype(BF16))
    grad_wo, grad_qkv = grad_oq[:, :qw].astype(F32), grad_oq[:, qw:].astype(F32)
    norm1 = norm1_part + lax.ppermute(norm1_part, "kv", grid.core_swap)
    norm1 = grid.scatter_blocks(norm1.reshape(n, -1))
    summed = grid.scatter_blocks(bundle)
    n_both = sum(c.shape[1] for c in cut[: len(both)])
    flat = jnp.concatenate([grid.sum_kv(summed[:n_both].astype(BF16)), summed[n_both:]])
    done = []
    at = 0
    for x, d in both + alone:
        shape = list(x.shape)
        shape[d] //= n
        size = x.size // n
        done.append(flat[at : at + size].reshape(shape))
        at += size
    grad_a, grad_bo, norm2, bq, bk, bv, featq, featk, grad_ao = done
    return (
        output,
        grad_tokens,
        norm1,
        grad_qkv[:, :qw],
        grad_qkv[:, qw : qw + kw],
        grad_qkv[:, qw + kw :],
        grad_a[:rank].T,
        bq,
        grad_a[rank : 2 * rank].T,
        bk,
        grad_a[2 * rank :].T,
        bv,
        featq,
        featk,
        grad_wo.T,
        grad_ao,
        grad_bo,
        norm2,
        grad_gate,
        grad_up,
        grad_down,
    )


def solution(mesh):
    placed = (
        P("seq", None),
        P(),
        P(None, "kv"),
        P(None, "kv"),
        P(None, "kv"),
        P(),
        P(None, "kv", None),
        P(),
        P(None, "kv", None),
        P(),
        P(None, "kv", None),
        P("kv", None, None),
        P("kv", None, None),
        P("kv", None),
        P("kv", None, None),
        P(),
        P(),
        P(None, "kv"),
        P(None, "kv"),
        P("kv", None),
        P("seq"),
        P("seq", None),
    )
    return jax.shard_map(
        local,
        mesh=mesh,
        in_specs=placed,
        out_specs=(
            P("seq", None),
            P("seq", None),
            P("seq"),
            P("seq", "kv"),
            P("seq", "kv"),
            P("seq", "kv"),
            P("seq", None),
            P(None, "kv", "seq"),
            P("seq", None),
            P(None, "kv", "seq"),
            P("seq", None),
            P(None, "kv", "seq"),
            P("kv", "seq", None),
            P("kv", "seq", None),
            P("kv", "seq"),
            P("kv", "seq", None),
            P(None, "seq"),
            P("seq"),
            P("seq", "kv"),
            P("seq", "kv"),
            P("kv", "seq"),
        ),
        check_vma=False,
    )
```

```python
import jax
import jax.numpy as jnp
from jax import lax
from jax.experimental import pallas as pl
from jax.experimental.pallas import tpu as pltpu
from jax.sharding import PartitionSpec as P

WIN = 64
CHUNK = 128
ANY = pl.BlockSpec(memory_space=pl.ANY)
EPSILON = 1e-05
EXACT = lax.Precision.HIGHEST
F32 = jnp.float32
BF16 = jnp.bfloat16


def cost(us):
    return pl.CostEstimate(flops=int(us * 0.3e9), bytes_accessed=1, transcendentals=0)


def dot(a, b, out=F32):
    return jnp.dot(a, b, preferred_element_type=F32).astype(out)


def dot_nt(a, b, out=F32):
    return lax.dot_general(a, b, (((1,), (1,)), ((), ())), preferred_element_type=F32).astype(out)


def dot_tn(a, b, out=F32):
    return lax.dot_general(a, b, (((0,), (0,)), ((), ())), preferred_element_type=F32).astype(out)


def dot_tt(a, b, out=F32):
    return lax.dot_general(a, b, (((0,), (1,)), ((), ())), preferred_element_type=F32).astype(out)


def tie(*xs):
    return lax.optimization_barrier(xs)


def add(terms):
    total = terms[0].astype(F32)
    for t in terms[1:]:
        total = total + t.astype(F32)
    return total


def take(x, i):
    return lax.dynamic_index_in_dim(x, i, 0, False)


class Grid:
    def __init__(self):
        self.kv = lax.axis_size("kv")
        self.seq = lax.axis_size("seq")
        self.outer = self.kv // 2
        self.line = self.seq // 2
        k = lax.axis_index("kv")
        s = lax.axis_index("seq")
        self.core, self.y = k % 2, k // 2
        self.x, self.z = s % 2, s // 2
        self.s = s
        self.core_swap = [(i, i ^ 1) for i in range(self.kv)]
        self.x_swap = [(i, i ^ 1) for i in range(self.seq)]
        self.z_groups = [[2 * z + x for z in range(self.line)] for x in range(2)]

    def y_shift(self, j):
        m = self.outer
        return [(y * 2 + c, (y + j) % m * 2 + c) for y in range(m) for c in range(2)]

    def own_rows(self, x, parts):
        rows, width = x.shape
        cut = x.reshape(parts, 2, rows // (2 * parts), width)
        return lax.dynamic_index_in_dim(cut, self.core, 1, False).reshape(rows // 2, width)

    def across_cores(self, x):
        return lax.ppermute(x, "kv", self.core_swap)

    def blocks_across(self, x):
        rows = x.shape[0] // 4
        return [self.across_cores(x[i * rows : (i + 1) * rows]) for i in range(4)]

    def core_sum(self, keep, send):
        return sum_rows(keep, self.blocks_across(send))

    def swap(self, x):
        return lax.ppermute(x, "seq", self.x_swap)

    def pair_sum(self, keep, got):
        return sum_rows(keep, [got])

    def outer_terms(self, half):
        terms = [half] + [lax.ppermute(half, "kv", self.y_shift(j)) for j in range(1, self.outer)]
        if self.outer == 2:
            return terms
        stack = jnp.stack(terms)
        return [take(stack, (self.y - i) % self.outer) for i in range(self.outer)]

    def gather_rows(self, own, out=BF16):
        return merge_rows(self.core, own, self.blocks_across(own), out)

    def sum_kv(self, x):
        x = x + lax.ppermute(x, "kv", self.core_swap).astype(F32)
        total = x
        for j in range(1, self.outer):
            total = total + lax.ppermute(x, "kv", self.y_shift(j))
        return total

    def line_scatter(self, part):
        return lax.psum_scatter(
            part, "seq", scatter_dimension=0, tiled=True, axis_index_groups=self.z_groups
        )

    def pair_half(self, x):
        return take(x.reshape(2, x.shape[0] // 2, x.shape[1]), 1 - self.x)

    def scatter_blocks(self, blocks):
        cut = blocks.reshape(self.line, 2, -1)
        other = lax.dynamic_index_in_dim(cut, 1 - self.x, 1, False).astype(BF16)
        own = lax.dynamic_index_in_dim(cut, self.x, 1, False)
        part = own + lax.ppermute(other, "seq", self.x_swap).astype(F32)
        total = take(part, self.z)
        m = self.line
        for j in range(1, m):
            pairs = [(z * 2 + x, (z + j) % m * 2 + x) for z in range(m) for x in range(2)]
            out = take(part, (self.z + j) % m).astype(BF16)
            total = total + lax.ppermute(out, "seq", pairs).astype(F32)
        return total

    def shift_seq(self, x, by):
        n = self.seq
        pairs = [(i, i + by) for i in range(n) if 0 <= i + by < n]
        return lax.ppermute(x, "seq", pairs)

    def sum_before(self, x, sign, kind):
        near = self.shift_seq(x.astype(kind), sign).astype(F32)
        total = x + near
        by = 2
        while by < self.seq:
            total = total + self.shift_seq(total.astype(kind), sign * by).astype(F32)
            by *= 2
        return total - x, near


def softmax_pair(logits):
    top = jnp.exp(logits - jnp.max(logits, 0, keepdims=True))
    low = jnp.exp(jnp.min(logits, 0, keepdims=True) - logits)
    return top * (1.0 / jnp.sum(top, 0, keepdims=True)), low * (1.0 / jnp.sum(low, 0, keepdims=True))


def softmax_pair_back(p, n, grad):
    hd = p.shape[0]
    up, un = p * grad[:hd], n * grad[hd:]
    return up - p * jnp.sum(up, 0, keepdims=True) - (un - n * jnp.sum(un, 0, keepdims=True))


def halves(x):
    top = x.astype(BF16)
    return top, (x - top.astype(F32)).astype(BF16)


def dot2(x, b):
    top, rest = halves(x)
    return dot(top, b) + dot(rest, b)


def value_rows(v, keep):
    hd, n = v.shape
    ones = (lax.broadcasted_iota(jnp.int32, (16, n), 0) == 0).astype(F32)
    return (jnp.concatenate([v.astype(F32), ones], 0) * keep).astype(BF16)


def key_kernel(kv_ref, map_ref, keep_ref, phi_cols_ref, phi_ref, k_ref, v_ref, state_ref):
    hk, hd = map_ref.shape[:2]
    for g in range(hk):
        k = kv_ref[g * hd : (g + 1) * hd, :]
        v = kv_ref[(hk + g) * hd : (hk + g + 1) * hd, :]
        p, n = softmax_pair(dot(map_ref[g], k))
        phi = jnp.concatenate([p, n], 0)
        phi_cols_ref[g] = phi.astype(BF16)
        phi_ref[g] = phi.T.astype(BF16)
        kv = jnp.concatenate([k, v], 0).astype(F32).T
        k_ref[g] = kv[:, :hd].astype(BF16)
        v_ref[g] = kv[:, hd:].astype(BF16)
        state_ref[g] = dot_nt(value_rows(v, keep_ref[...]), phi.astype(BF16))


def masks(open_ref, base):
    shape = (2 * CHUNK, CHUNK)
    a = lax.broadcasted_iota(jnp.int32, shape, 0)
    b = lax.broadcasted_iota(jnp.int32, shape, 1)
    start = open_ref[:, pl.ds(base, CHUNK)] - base
    doc = a >= start
    near = a > b + (CHUNK - WIN)
    return doc & near & (a <= b + CHUNK), doc & ~near, (start < 0).astype(F32)


def lanes(parts):
    return jnp.concatenate(parts, 1)


def attend_kernel(
    q_ref, kv_ref, phi_cols_ref, phi_ref, k_ref, map_ref, prior_ref, open_ref, keep_ref, cont_ref,
    heads_ref, total_ref, states_ref, state,
):
    hk, hd = phi_ref.shape[0], map_ref.shape[1]
    hq = map_ref.shape[0]
    group = hq // hk
    scale = hd**-0.5
    state[...] = prior_ref[...]

    def chunk(i, _):
        base = pl.multiple_of(i * CHUNK, CHUNK)
        here = pl.ds(base, CHUNK)
        keys = pl.ds(base, 2 * CHUNK)
        win, lin, far = masks(open_ref, base)
        for g in range(hk):
            q = [q_ref[h * hd : (h + 1) * hd, here] for h in range(g * group, (g + 1) * group)]
            phi = []
            for j in range(group):
                p, n = softmax_pair(dot(map_ref[g * group + j], q[j]))
                phi.append(jnp.concatenate([p, n], 0).astype(BF16))
            phi4 = lanes(phi)
            past = state[g]
            states_ref[i, g] = past
            scores = dot(k_ref[g, keys, :], lanes(q)) * scale
            linear = dot(phi_ref[g, keys, :], phi4)
            carried = dot2(past, phi4)
            weights = []
            totals = []
            for j in range(group):
                cut = slice(j * CHUNK, (j + 1) * CHUNK)
                w = jnp.where(win, jnp.exp(scores[:, cut]), 0.0) + jnp.where(lin, linear[:, cut], 0.0)
                weights.append(w.astype(BF16))
                totals.append(jnp.sum(w, 0, keepdims=True) + far * carried[hd : hd + 1, cut])
            v = kv_ref[(hk + g) * hd : (hk + g + 1) * hd, keys]
            mixed = dot(v, lanes(weights))
            for j in range(group):
                cut = slice(j * CHUNK, (j + 1) * CHUNK)
                h = g * group + j
                out = (mixed[:, cut] + far * carried[:hd, cut]) * (1.0 / totals[j])
                heads_ref[h * hd : (h + 1) * hd, here] = out.astype(BF16)
                total_ref[h : h + 1, here] = totals[j]
            own = value_rows(kv_ref[(hk + g) * hd : (hk + g + 1) * hd, here], keep_ref[:, here])
            state[g] = cont_ref[i] * past + dot_nt(own, phi_cols_ref[g, :, here])
        return 0

    lax.fori_loop(0, heads_ref.shape[1] // CHUNK, chunk, 0)


def attend_back_kernel(
    q_ref, kv_ref, phi_cols_ref, phi_ref, k_ref, v_ref, map_ref, map_t_ref, states_ref, heads_ref,
    total_ref, g_ref, open_ref, keep_ref, cont_ref,
    gq_ref, feat_ref, gk_ref, gv_ref, gphi_ref, first_ref, gl_ref, grad_t,
):
    hk, hd = phi_ref.shape[0], map_ref.shape[1]
    hq = map_ref.shape[0]
    group = hq // hk
    scale = hd**-0.5
    count = heads_ref.shape[1] // CHUNK
    first_ref[...] = jnp.zeros_like(first_ref)
    grad_t[...] = jnp.zeros_like(grad_t)
    gk_ref[...] = jnp.zeros_like(gk_ref)
    gv_ref[...] = jnp.zeros_like(gv_ref)
    gphi_ref[...] = jnp.zeros_like(gphi_ref)

    def chunk(step, _):
        i = count - 1 - step
        base = pl.multiple_of(i * CHUNK, CHUNK)
        here = pl.ds(base, CHUNK)
        keys = pl.ds(base, 2 * CHUNK)
        win, lin, far = masks(open_ref, base)
        for g in range(hk):
            rows = [slice(h * hd, (h + 1) * hd) for h in range(g * group, (g + 1) * group)]
            key_rows = slice(g * hd, (g + 1) * hd)
            value_row = slice((hk + g) * hd, (hk + g + 1) * hd)
            q4 = lanes([q_ref[r, here] for r in rows])
            g4 = lanes([g_ref[r, here] for r in rows])
            pairs = [softmax_pair(dot(map_ref[g * group + j], q_ref[rows[j], here])) for j in range(group)]
            phi = [jnp.concatenate([p, n], 0) for p, n in pairs]
            phi4 = lanes([x.astype(BF16) for x in phi])
            scores = dot(k_ref[g, keys, :], q4) * scale
            linear = dot(phi_ref[g, keys, :], phi4)
            g_w = dot(v_ref[g, keys, :], g4)
            shares, g_scores, g_linear, g_ext = [], [], [], []
            for j in range(group):
                cut = slice(j * CHUNK, (j + 1) * CHUNK)
                h = g * group + j
                inv = 1.0 / total_ref[h : h + 1, here]
                g_here = g_ref[rows[j], here].astype(F32)
                g_total = -inv * jnp.sum(g_here * heads_ref[rows[j], here].astype(F32), 0, keepdims=True)
                ex = jnp.where(win, jnp.exp(scores[:, cut]), 0.0)
                w = ex + jnp.where(lin, linear[:, cut], 0.0)
                shares.append((w * inv).astype(BF16))
                g_weight = g_w[:, cut] * inv + g_total
                g_scores.append((g_weight * ex).astype(BF16))
                g_linear.append(jnp.where(lin, g_weight, 0.0).astype(BF16))
                row = lax.broadcasted_iota(jnp.int32, (16, CHUNK), 0) == 0
                g_ext.append(
                    (jnp.concatenate([g_here * inv, jnp.where(row, g_total, 0.0)], 0) * far).astype(BF16)
                )
            shares, g_scores, g_linear, g_ext = map(lanes, (shares, g_scores, g_linear, g_ext))
            gv_ref[key_rows, keys] += dot_nt(g4, shares)
            gk_ref[key_rows, keys] += dot_nt(q4, g_scores) * scale
            gphi_ref[g, :, keys] += dot_nt(phi4, g_linear)
            g_query = dot(kv_ref[key_rows, keys], g_scores) * scale
            past = states_ref[i, g].T
            g_phi = dot(phi_cols_ref[g, :, keys], g_linear) + dot2(past, g_ext)
            for j in range(group):
                cut = slice(j * CHUNK, (j + 1) * CHUNK)
                gl = softmax_pair_back(*pairs[j], g_phi[:, cut]).astype(BF16)
                gl_ref[rows[j], here] = gl
                gq = g_query[:, cut] + dot(map_t_ref[g * group + j], gl)
                gq_ref[rows[j], here] = gq.astype(BF16)
            keep = keep_ref[:, here]
            own = value_rows(kv_ref[value_row, here], keep)
            gphi_ref[g, :, here] += dot2(grad_t[g], own)
            gv_ref[key_rows, here] += dot2(first_ref[g, :hd, :], phi_cols_ref[g, :, here]) * keep
            cont = cont_ref[i]
            first_ref[g] = cont * first_ref[g] + dot_nt(g_ext, phi4)
            grad_t[g] = cont * grad_t[g] + dot_nt(phi4, g_ext)
        return 0

    lax.fori_loop(0, count, chunk, 0)
    for h in range(hq):
        r = slice(h * hd, (h + 1) * hd)
        feat_ref[h] = dot_nt(q_ref[r, :], gl_ref[r, :])


def key_back_kernel(
    kv_ref, phi_cols_ref, map_ref, map_t_ref, gk_ref, gv_ref, gphi_ref, edge_ref, later_ref, last_ref,
    keep_ref, g_ref, feat_ref,
):
    hk, hd = map_ref.shape[:2]
    n = kv_ref.shape[1]
    cut = n - CHUNK

    def joined(own, edge):
        return jnp.concatenate([own[:, : cut - CHUNK], own[:, cut - CHUNK :] + edge.astype(F32)], 1)

    for g in range(hk):
        key_rows = slice(g * hd, (g + 1) * hd)
        k = kv_ref[key_rows, CHUNK:]
        v = kv_ref[(hk + g) * hd : (hk + g + 1) * hd, CHUNK:]
        keep = keep_ref[:, CHUNK:]
        phi = phi_cols_ref[g, :, CHUNK:]
        own = value_rows(v, keep)
        one = value_rows(v[:, cut - CHUNK :], jnp.ones((1, CHUNK), F32))
        later, last = later_ref[g], last_ref[g]
        g_phi = gphi_ref[g, :, CHUNK:] + lanes(
            [dot2(later.T, own[:, : cut - CHUNK]), dot2(last.T, one)]
        )
        g_phi = joined(g_phi, edge_ref[2 * hk * hd + g * 2 * hd : 2 * hk * hd + (g + 1) * 2 * hd, :])
        g_v = gv_ref[key_rows, CHUNK:] + lanes(
            [
                dot2(later[:hd], phi[:, : cut - CHUNK]) * keep[:, : cut - CHUNK],
                dot2(last[:hd], phi[:, cut - CHUNK :]),
            ]
        )
        g_v = joined(g_v, edge_ref[(hk + g) * hd : (hk + g + 1) * hd, :])
        g_ref[(hk + g) * hd : (hk + g + 1) * hd, :] = g_v.astype(BF16)
        p, q = softmax_pair(dot(map_ref[g], k))
        gl = softmax_pair_back(p, q, g_phi).astype(BF16)
        g_k = joined(gk_ref[key_rows, CHUNK:], edge_ref[key_rows, :]) + dot(map_t_ref[g], gl)
        g_ref[key_rows, :] = g_k.astype(BF16)
        feat_ref[g] = dot_nt(k, gl)


def call(us, kernel, outs, args, scratch=(), smem=(), after=()):
    count = len(args)
    vmem = pl.BlockSpec(memory_space=pltpu.VMEM)
    specs = [pl.BlockSpec(memory_space=pltpu.SMEM) if i in smem else vmem for i in range(len(args))]
    return pl.pallas_call(
        lambda *refs: kernel(*refs[:count], *refs[count + len(after) :]),
        out_shape=[jax.ShapeDtypeStruct(s, d) for s, d in outs],
        in_specs=specs + [ANY] * len(after),
        out_specs=[vmem] * len(outs),
        scratch_shapes=[pltpu.VMEM(s, d) for s, d in scratch],
        compiler_params=pltpu.CompilerParams(vmem_limit_bytes=38 * 2**20),
        cost_estimate=cost(us),
    )(*args, *after)


def sum_rows(keep, got):
    rows, width = keep.shape
    count = len(got)
    steps = max(count, 4)
    tile = rows // steps

    def kernel(keep_ref, *refs):
        *got_refs, out_ref = refs
        if count == 1:
            out_ref[...] = (keep_ref[...].astype(F32) + got_refs[0][...].astype(F32)).astype(BF16)
        else:
            for i in range(count):

                @pl.when(pl.program_id(0) == i)
                def _(i=i):
                    out_ref[...] = (keep_ref[...].astype(F32) + got_refs[i][...].astype(F32)).astype(BF16)

    block = pl.BlockSpec((tile, width), lambda i: (i, 0))
    fixed = pl.BlockSpec((tile, width), lambda i: (0, 0))
    return pl.pallas_call(
        kernel,
        grid=(steps,),
        in_specs=[block] + [block if count == 1 else fixed] * count,
        out_specs=block,
        out_shape=jax.ShapeDtypeStruct((rows, width), BF16),
        compiler_params=pltpu.CompilerParams(vmem_limit_bytes=32 * 2**20),
        cost_estimate=cost(2.5),
    )(keep, *got)


def merge_rows(core, own, other, out):
    rows, width = own.shape
    tile = rows // 4

    def kernel(core_ref, own_ref, *refs):
        *other_refs, out_ref = refs
        for b in range(8):
            c, k, h = b // 4, (b // 2) % 2, b % 2

            @pl.when((pl.program_id(0) == b) & (core_ref[0] == k))
            def _(at=2 * c + h):
                out_ref[...] = own_ref[at * tile : (at + 1) * tile, :].astype(out)

            @pl.when((pl.program_id(0) == b) & (core_ref[0] != k))
            def _(at=2 * c + h):
                out_ref[...] = other_refs[at][...].astype(out)

    return pl.pallas_call(
        kernel,
        grid_spec=pltpu.PrefetchScalarGridSpec(
            num_scalar_prefetch=1,
            grid=(8,),
            in_specs=[pl.BlockSpec((rows, width), lambda i, s: (0, 0))]
            + [pl.BlockSpec((tile, width), lambda i, s: (0, 0))] * 4,
            out_specs=pl.BlockSpec((tile, width), lambda i, s: (i, 0)),
        ),
        out_shape=jax.ShapeDtypeStruct((2 * rows, width), out),
        compiler_params=pltpu.CompilerParams(vmem_limit_bytes=32 * 2**20),
        cost_estimate=cost(3.5),
    )(core.astype(jnp.int32)[None], own, *other)


def finish(select, whole, got, turned):
    rows, n = got.shape

    def kernel(sel, own_ref, got_ref, out_ref):
        def put(ref):
            value = ref[...].astype(F32)
            out_ref[...] = value.T if turned else value

        here = pl.program_id(0) == sel[0]

        @pl.when(here)
        def _():
            put(own_ref)

        @pl.when(jnp.logical_not(here))
        def _():
            put(got_ref)

    block = (n, rows) if turned else (rows, n)
    return pl.pallas_call(
        kernel,
        grid_spec=pltpu.PrefetchScalarGridSpec(
            num_scalar_prefetch=1,
            grid=(2,),
            in_specs=[
                pl.BlockSpec((rows, n), lambda j, s: (s[0], 0)),
                pl.BlockSpec((rows, n), lambda j, s: (0, 0)),
            ],
            out_specs=pl.BlockSpec(block, (lambda j, s: (j, 0)) if turned else (lambda j, s: (0, j))),
        ),
        out_shape=jax.ShapeDtypeStruct((2 * n, rows) if turned else (rows, 2 * n), F32),
        compiler_params=pltpu.CompilerParams(vmem_limit_bytes=32 * 2**20),
        cost_estimate=cost(1.0),
    )(select.astype(jnp.int32)[None], whole, got)


def project_kernel(
    x_ref, gain_ref, wq_ref, wk_ref, wv_ref, down_ref, up_ref, normed_ref, q_ref, kv_ref, low_ref
):
    x = x_ref[...].astype(F32)
    rms = lax.rsqrt(jnp.mean(x * x, -1, keepdims=True) + EPSILON)
    normed = (x * rms * gain_ref[...].astype(F32)).astype(BF16)
    normed_ref[...] = normed
    low, rest = halves(dot(normed, down_ref[...]))
    low_ref[...] = low
    qw, kw = wq_ref.shape[1], wk_ref.shape[1]

    def rows(weight, at, width):
        up = up_ref[:, at : at + width]
        return (dot(normed, weight[...]) + dot(low, up) + dot(rest, up)).T.astype(BF16)

    kv_ref[:kw, :] = rows(wk_ref, qw, kw)
    kv_ref[kw:, :] = rows(wv_ref, qw + kw, kw)
    q_ref[...] = rows(wq_ref, 0, qw)


def project(tokens, gain, wq, wk, wv, down, up, tile=256):
    t, d = tokens.shape
    qw, kw = wq.shape[1], wk.shape[1]
    whole = lambda a: pl.BlockSpec(a.shape, lambda i: (0,) * a.ndim)
    row = lambda w: pl.BlockSpec((tile, w), lambda i: (i, 0))
    col = lambda h: pl.BlockSpec((h, tile), lambda i: (0, i))
    gain = gain[None]
    return pl.pallas_call(
        project_kernel,
        grid=(t // tile,),
        in_specs=[row(d)] + [whole(a) for a in (gain, wq, wk, wv, down, up)],
        out_specs=[row(d), col(qw), col(2 * kw), row(down.shape[1])],
        out_shape=[
            jax.ShapeDtypeStruct((t, d), BF16),
            jax.ShapeDtypeStruct((qw, t), BF16),
            jax.ShapeDtypeStruct((2 * kw, t), BF16),
            jax.ShapeDtypeStruct((t, down.shape[1]), BF16),
        ],
        compiler_params=pltpu.CompilerParams(vmem_limit_bytes=38 * 2**20),
        cost_estimate=cost(10.0),
    )(tokens, gain, wq, wk, wv, down, up)


def matmul(pairs, mode, chosen, out, split=None, tile=512, after=()):
    a0, b0 = pairs[0]
    over = 0 if mode in ("left", "both") else 1
    rows = a0.shape[1 - over]
    half = a0.shape[over]
    width = {"rows": b0.shape[0] // 2, "columns": b0.shape[0], "both": b0.shape[0]}.get(mode, b0.shape[1])
    tile = min(tile, width)
    product = {"rows": dot_nt, "columns": dot_nt, "inner": dot, "left": dot_tn, "both": dot_tt}[mode]
    b_spec = {
        "rows": pl.BlockSpec((tile, half), lambda i, s: (s[0] * (width // tile) + i, 0)),
        "columns": pl.BlockSpec((tile, half), lambda i, s: (i, s[0])),
        "inner": pl.BlockSpec((half, tile), lambda i, s: (s[0], i)),
        "left": pl.BlockSpec((half, tile), lambda i, s: (0, i)),
        "both": pl.BlockSpec((tile, half), lambda i, s: (i, 0)),
    }[mode]
    specs, args = [], []
    for a, b in pairs:
        specs += [pl.BlockSpec(a.shape, lambda i, s: (0, 0)), b_spec]
        args += [a, b]
    sub = rows // 4
    core = jnp.zeros((), jnp.int32) if split is None else split

    def kernel(sel, *refs):
        used = refs[: 2 * len(pairs)]
        outs = refs[2 * len(pairs) + len(after) :]

        def block(start):
            total = None
            for a_ref, b_ref in zip(used[::2], used[1::2]):
                a = a_ref[pl.ds(start, sub), :] if over else a_ref[:, pl.ds(start, sub)]
                term = product(a, b_ref[...])
                total = term if total is None else total + term
            return total.astype(out)

        for c in range(2):
            for k in range(2):
                if split is None:
                    at = (2 * c + k) * sub
                    outs[0][at : at + sub, :] = block(at)
                else:
                    other = sel[1] if k == 0 else 1 - sel[1]
                    start = pl.multiple_of((2 * c + other) * sub, sub)
                    outs[k][c * sub : (c + 1) * sub, :] = block(start)

    n_out = 1 if split is None else 2
    us = 1.0 + sum(a.size for a, _ in pairs) * width * 1.5e-9
    made = pl.pallas_call(
        kernel,
        grid_spec=pltpu.PrefetchScalarGridSpec(
            num_scalar_prefetch=1,
            grid=(width // tile,),
            in_specs=specs + [ANY] * len(after),
            out_specs=[pl.BlockSpec((rows // n_out, tile), lambda i, s: (0, i))] * n_out,
        ),
        out_shape=[jax.ShapeDtypeStruct((rows // n_out, width), out)] * n_out,
        compiler_params=pltpu.CompilerParams(vmem_limit_bytes=38 * 2**20),
        cost_estimate=cost(us),
    )(jnp.stack([chosen, core]).astype(jnp.int32), *args, *after)
    return made if split is not None else made[0]


def grad_pair(count, pairs, after=()):
    rows, width = pairs[0][0].shape
    n = pairs[0][1].shape[1]
    block = width // count
    specs = [pl.BlockSpec((rows, block), lambda j: (0, j)), pl.BlockSpec((rows, n), lambda j: (0, 0))]

    def kernel(*refs):
        value = dot_tn(refs[0][...], refs[1][...])
        for i in range(1, len(pairs)):
            value = value + dot_tn(refs[2 * i][...], refs[2 * i + 1][...])
        refs[-1][...] = value.astype(BF16)

    return pl.pallas_call(
        kernel,
        grid=(count,),
        in_specs=specs * len(pairs) + [ANY] * len(after),
        out_specs=pl.BlockSpec((block, n), lambda j: (j, 0)),
        out_shape=jax.ShapeDtypeStruct((width, n), BF16),
        compiler_params=pltpu.CompilerParams(vmem_limit_bytes=38 * 2**20),
        cost_estimate=cost(13.0),
    )(*[x for pair in pairs for x in pair], *after)


def grad_block(line, select, a, b, product, got=None, after=()):
    rows, width = a.shape
    block = width // (2 * line)
    n = b.shape[0] if product is dot_tt else b.shape[1]
    more = [] if got is None else [got]

    def kernel(sel, a_ref, b_ref, *rest):
        value = product(a_ref[...], b_ref[...])
        if got is not None:
            value = value + rest[0][...].astype(F32)
        rest[-1][...] = value.astype(BF16)

    spec = pl.BlockSpec((block, n), lambda j, s: (j, 0))
    return pl.pallas_call(
        kernel,
        grid_spec=pltpu.PrefetchScalarGridSpec(
            num_scalar_prefetch=1,
            grid=(line,),
            in_specs=[
                pl.BlockSpec((rows, block), lambda j, s: (0, 2 * j + s[0])),
                pl.BlockSpec(b.shape, lambda j, s: (0, 0)),
            ]
            + [spec] * len(more)
            + [ANY] * len(after),
            out_specs=spec,
        ),
        out_shape=jax.ShapeDtypeStruct((line * block, n), BF16),
        compiler_params=pltpu.CompilerParams(vmem_limit_bytes=38 * 2**20),
        cost_estimate=cost(1.0),
    )(select.astype(jnp.int32)[None], a, b, *more, *after)


def gated_kernel(sel_ref, own_ref, other_ref, wg_ref, wu_ref, gh_ref, *refs):
    normed_ref, hidden_ref, gate_ref, up_ref = refs[-4:]
    half = own_ref.shape[0]

    @pl.when(pl.program_id(0) == 0)
    def _():
        first = sel_ref[0] == 0

        @pl.when(first)
        def _():
            normed_ref[:half, :] = own_ref[...]
            normed_ref[half:, :] = other_ref[...]

        @pl.when(jnp.logical_not(first))
        def _():
            normed_ref[:half, :] = other_ref[...]
            normed_ref[half:, :] = own_ref[...]

    for r in range(0, 2 * half, half):
        cut = slice(r, r + half)
        x = normed_ref[cut, :]
        gate = dot(x, wg_ref[...])
        up = dot(x, wu_ref[...])
        sig = 1.0 / (1.0 + jnp.exp(-gate))
        silu = gate * sig
        hidden_ref[cut, :] = (silu * up).astype(BF16)
        g = gh_ref[cut, :].astype(F32)
        gate_ref[cut, :] = (g * up * (sig + silu * (1.0 - sig))).astype(BF16)
        up_ref[cut, :] = (g * silu).astype(BF16)


def gated(c, rows, sel, own, other, wg, wu, gh, held, after, tile=256):
    half, d = own.shape
    f = wg.shape[1] // 2
    here = pl.BlockSpec((2 * half, tile), lambda i, s: (c, i))
    weight = pl.BlockSpec((d, tile), lambda i, s: (0, s[1] * (f // tile) + i))
    shapes = [jax.ShapeDtypeStruct((rows, d), BF16)] + [jax.ShapeDtypeStruct((rows, f), BF16)] * 3
    return pl.pallas_call(
        gated_kernel,
        grid_spec=pltpu.PrefetchScalarGridSpec(
            num_scalar_prefetch=1,
            grid=(f // tile,),
            in_specs=[
                pl.BlockSpec((half, d), lambda i, s: (0, 0)),
                pl.BlockSpec((half, d), lambda i, s: (0, 0)),
                weight,
                weight,
                here,
            ]
            + [ANY] * (len(held) + len(after)),
            out_specs=[pl.BlockSpec((2 * half, d), lambda i, s: (c, 0)), here, here, here],
        ),
        out_shape=shapes,
        input_output_aliases={6 + i: i for i in range(len(held))},
        compiler_params=pltpu.CompilerParams(vmem_limit_bytes=38 * 2**20),
        cost_estimate=cost(11.0),
    )(sel, own, other, wg, wu, gh, *held, *after)


def local(
    tokens,
    gain_one,
    query_weight,
    key_weight,
    value_weight,
    query_down,
    query_up,
    key_down,
    key_up,
    value_down,
    value_up,
    query_map,
    key_map,
    output_weight,
    output_down,
    output_up,
    gain_two,
    gate_weight,
    up_weight,
    down_weight,
    start_mask,
    cotangent,
):
    grid = Grid()
    rows = tokens.shape[0]
    rank = query_down.shape[1]
    hd = key_map.shape[-1]
    hk = key_map.shape[0]
    hq = query_map.shape[0]
    group = hq // hk
    count = rows // CHUNK
    length = rows + CHUNK
    index = jnp.arange(rows, dtype=jnp.int32)
    starts = jnp.where(start_mask == 1, index + CHUNK, jnp.int32(-1))
    opened = jnp.max(jnp.where(index[:, None] <= index[None, :], starts[:, None], jnp.int32(-1)), 0)
    ends = jnp.concatenate([jnp.full((1,), -1, jnp.int32), opened[CHUNK - 1 : -1 : CHUNK]])
    cont = (ends < jnp.arange(count, dtype=jnp.int32) * CHUNK).astype(F32)
    place = jnp.arange(length, dtype=jnp.int32)
    ends_at = jnp.concatenate([jnp.repeat(ends, CHUNK), jnp.full((CHUNK,), length, jnp.int32)])
    keep = (place >= ends_at).astype(F32)[None]
    keep_all = ((place >= ends[count - 1]) & (place < rows)).astype(F32)[None]
    opened = opened[None]

    g1 = gain_one.astype(F32)
    g2 = gain_two.astype(F32)
    qup, kup, vup = (u.reshape(rank, -1) for u in (query_up, key_up, value_up))
    qw, kw = hq * hd, hk * hd
    wide = 128 - 3 * rank
    up_all = jnp.pad(jax.scipy.linalg.block_diag(qup, kup, vup), ((0, wide), (0, 0)))
    down_all = jnp.pad(jnp.concatenate([query_down, key_down, value_down], 1), ((0, 0), (0, wide)))
    normed_one, query, kv, low_all = project(
        tokens, gain_one, query_weight, key_weight, value_weight, down_all, up_all
    )
    edge = grid.shift_seq(kv[:, rows - CHUNK :], 1)
    kv = jnp.concatenate([edge, kv], 1)

    query_map_t = jnp.swapaxes(query_map, 1, 2)
    key_map_t = jnp.swapaxes(key_map, 1, 2)
    phi_dim = 2 * hd
    phi_cols, phi, key, value, state = call(
        2.0,
        key_kernel,
        [
            ((hk, phi_dim, length), BF16),
            ((hk, length, phi_dim), BF16),
            ((hk, length, hd), BF16),
            ((hk, length, hd), BF16),
            ((hk, hd + 16, phi_dim), F32),
        ],
        (kv, key_map_t, keep_all),
    )
    prior, _ = grid.sum_before(state, 1, F32)
    parts = 2
    chunk = rows // parts
    core, mine = grid.core.astype(jnp.int32), grid.x.astype(jnp.int32)
    g_hidden = matmul([(cotangent, down_weight)], "rows", mine, F32)
    oup = output_up
    odown = output_down.reshape(-1, rank)
    weight_o = (output_weight.astype(F32) + dot(odown, oup)).astype(BF16)
    weight_qkv = jnp.concatenate([query_weight, key_weight, value_weight], 1)
    weight_qkv = (weight_qkv.astype(F32) + dot(down_all, up_all)).astype(BF16)
    cot_own = grid.own_rows(cotangent, parts)
    prior, g_hidden, weight_o, weight_qkv, cot_own = tie(
        prior, g_hidden, weight_o, weight_qkv, cot_own
    )
    cot_got = grid.swap(cot_own)
    heads, totals, states = call(
        9.0,
        attend_kernel,
        [((qw, rows), BF16), ((hq, rows), F32), ((count, hk, hd + 16, phi_dim), F32)],
        (query, kv, phi_cols, phi, key, query_map_t, prior, opened, keep, cont),
        scratch=[((hk, hd + 16, phi_dim), F32)],
        smem=(9,),
    )

    kept, sent = matmul([(heads, weight_o)], "left", mine, BF16, core)
    cuts = [slice(c * chunk // 2, (c + 1) * chunk // 2) for c in range(parts)]
    half = [grid.core_sum(kept[cut], sent[cut]) for cut in cuts]
    own_tokens = [grid.own_rows(tokens[c * chunk : (c + 1) * chunk], 1) for c in range(parts)]
    own_tokens[0], half[1] = tie(own_tokens[0], half[1])
    terms = [grid.outer_terms(h) for h in half]
    held, held_pair = (), ()
    resid, rms_two, own, got = [], [], [], []
    select = jnp.stack([core, mine])

    def normed(c):
        r = own_tokens[c].astype(F32) + add(terms[c])
        rms = lax.rsqrt(jnp.mean(r * r, -1, keepdims=True) + EPSILON)
        resid.append(r)
        rms_two.append(rms)
        own.append((r * rms * g2).astype(BF16))
        got.append(None)

    def inner(c, mine_c, gh, held, after):
        return gated(
            c, rows, select, mine_c, grid.across_cores(mine_c), gate_weight, up_weight, gh, held, after
        )

    normed(0)
    got[0] = grid.swap(own[0])
    held = list(inner(0, own[0], g_hidden, held, []))
    cot_got, held[2] = tie(cot_got, held[2])
    terms[1][-1], held[1] = tie(terms[1][-1], held[1])
    normed(1)
    got[1] = grid.swap(own[1])
    cot_got, mark = tie(cot_got, own[1])
    cot_pair = grid.gather_rows(cot_got)
    g_pair = matmul([(cot_pair, down_weight)], "rows", mine, F32, after=[mark])
    held = list(inner(1, own[1], g_hidden, held, [g_pair]))
    got[0], held[1] = tie(got[0], held[1])
    held_pair = list(inner(0, got[0], g_pair, held_pair, [held[1]]))
    got[1], held_pair[1] = tie(got[1], held_pair[1])
    held_pair = inner(1, got[1], g_pair, held_pair, [])
    normed_two, hidden, g_gate, g_up = held
    normed_pair, hidden_pair, gate_pair, up_pair = held_pair
    resid = jnp.concatenate(resid, 0)
    rms_two = jnp.concatenate(rms_two, 0)

    count_d = 2 * grid.line
    yours = 1 - mine

    def to_pair(a, b, product=dot_tn, after=()):
        return grad_block(grid.line, yours, a, b, product, None, after)

    def from_pair(a, b, got, product=dot_tn, after=()):
        return grad_block(grid.line, mine, a, b, product, got, after)

    w_d = grad_pair(count_d, [(cotangent, hidden), (cot_pair, hidden_pair)])
    grad_d = grid.line_scatter(w_d)
    kept, sent = matmul(
        [(gate_pair, gate_weight), (up_pair, up_weight)], "columns", mine, BF16, core, after=[w_d]
    )
    theirs = grid.core_sum(kept, sent)
    kept, sent = matmul(
        [(g_gate, gate_weight), (g_up, up_weight)], "columns", mine, BF16, core, after=[kept]
    )
    ours = grid.core_sum(kept, sent)
    w_g = grad_pair(count_d, [(normed_two, g_gate), (normed_pair, gate_pair)], after=[kept])
    theirs = grid.swap(theirs)
    theirs, w_g = tie(theirs, w_g)
    grad_g = grid.line_scatter(w_g)
    half = grid.pair_sum(ours, theirs)
    terms = grid.outer_terms(half)
    down_theirs = matmul([(hidden_pair, down_weight)], "inner", mine, BF16, core, after=[half])
    down_ours = matmul([(hidden, down_weight)], "inner", mine, BF16, core, after=[down_theirs[0]])
    w_u = grad_pair(
        count_d, [(normed_two, g_up), (normed_pair, up_pair)], after=[down_ours[0]]
    )
    terms[-1], w_u, *down_ours = tie(terms[-1], w_u, *down_ours)
    grad_u = grid.line_scatter(w_u)

    g_two = add(terms)
    norm2_part = jnp.sum(g_two * resid * rms_two, 0)
    s_two = g_two * g2
    g_resid = (
        cot_own.astype(F32)
        + rms_two * s_two
        - resid * rms_two**3 * jnp.mean(resid * s_two, -1, keepdims=True)
    )
    own_attn = g_resid.astype(BF16)
    g_attn = grid.gather_rows(own_attn)
    down_got = grid.swap(grid.core_sum(*down_theirs))
    down_half = grid.core_sum(*down_ours)

    g_heads = dot_nt(weight_o, g_attn, BF16)
    g_q, featq_part, gk, gv, gphi, first = call(
        24.0,
        attend_back_kernel,
        [
            ((qw, rows), BF16),
            ((hq, hd, hd), F32),
            ((kw, length), F32),
            ((kw, length), F32),
            ((hk, phi_dim, length), F32),
            ((hk, hd + 16, phi_dim), F32),
        ],
        (
            query, kv, phi_cols, phi, key, value, query_map_t, query_map, states, heads,
            totals, g_heads, opened, keep, cont,
        ),
        scratch=[((qw, rows), BF16), ((hk, phi_dim, hd + 16), F32)],
        smem=(14,),
        after=[grad_d],
    )
    first, down_got, down_half = tie(first, down_got, down_half)
    down_half = grid.pair_sum(down_half, down_got)
    later, near = grid.sum_before(first, -1, BF16)
    back = [gk[:, :CHUNK], gv[:, :CHUNK], gphi[:, :, :CHUNK].reshape(hk * phi_dim, CHUNK)]
    back = grid.shift_seq(jnp.concatenate(back, 0).astype(BF16), -1)
    s_o = to_pair(g_attn, heads, dot_tt, after=[g_q])
    r_o = grid.swap(s_o)
    g_kv, featk_part = call(
        2.0,
        key_back_kernel,
        [((2 * kw, rows), BF16), ((hk, hd, hd), F32)],
        (kv, phi_cols, key_map_t, key_map, gk, gv, gphi, back, later, later - near, keep_all),
        after=[s_o],
    )

    g_qkv = jnp.concatenate([g_q, g_kv], 0)
    kept, sent = matmul([(g_qkv, weight_qkv)], "both", mine, BF16, core)
    half = grid.core_sum(kept, sent)
    half, down_half = tie(half, down_half)
    terms = grid.outer_terms(half)
    down_terms = grid.outer_terms(down_half)
    s_qkv = to_pair(normed_one, g_qkv, dot_tt, after=[half])
    r_qkv = grid.swap(s_qkv)
    g_late, s_qkv = tie(g_attn, s_qkv)
    g_low_o = dot_nt(g_late, oup, BF16)
    low_o = dot_tn(odown, heads, BF16)
    bo_part = dot(low_o, g_late)
    ao_part = dot(heads, g_low_o)
    k_o = from_pair(g_attn, heads, r_o, dot_tt, after=[s_qkv])
    g_low = dot(up_all, g_qkv, BF16)
    a_part = dot(g_low, normed_one)
    b_part = dot_tt(low_all, g_qkv)
    bq_part = b_part[:rank, :qw]
    bk_part = b_part[rank : 2 * rank, qw : qw + kw]
    bv_part = b_part[2 * rank : 3 * rank, qw + kw :]
    n = grid.seq

    def blocks(x, dim):
        shape = x.shape
        x = x.reshape(shape[:dim] + (n, shape[dim] // n) + shape[dim + 1 :])
        return jnp.moveaxis(x, dim, 0).reshape(n, -1)

    both = [(a_part[: 3 * rank], 1), (bo_part, 1)]
    alone = [
        (norm2_part + lax.ppermute(norm2_part, "kv", grid.core_swap), 0),
        (bq_part.reshape(query_up.shape), 2),
        (bk_part.reshape(key_up.shape), 2),
        (bv_part.reshape(value_up.shape), 2),
        (featq_part, 1),
        (featk_part, 1),
        (ao_part.reshape(output_down.shape), 1),
    ]
    cut = [blocks(x, d) for x, d in both + alone]
    bundle = jnp.concatenate(cut, 1)
    terms[-1], bundle, r_qkv, grad_g, k_o = tie(terms[-1], bundle, r_qkv, grad_g, k_o)
    k_qkv = from_pair(normed_one, g_qkv, r_qkv, dot_tt, after=[k_o])

    terms[-1], k_qkv = tie(terms[-1], k_qkv)
    grad_oq = grid.line_scatter(jnp.concatenate([k_o, k_qkv], 1))
    stream = grid.own_rows(tokens, parts).astype(F32)
    rms_one = lax.rsqrt(jnp.mean(stream * stream, -1, keepdims=True) + EPSILON)
    g_one = add(terms)
    norm1_part = jnp.sum(g_one * stream * rms_one, 0)
    s_one = g_one * g1
    own_grad = (
        g_resid
        + rms_one * s_one
        - stream * rms_one**3 * jnp.mean(stream * s_one, -1, keepdims=True)
    ).astype(BF16)
    own_blocks = grid.blocks_across(own_grad)
    fins = grid.swap(jnp.concatenate([grid.pair_half(g) for g in (grad_d, grad_g, grad_u)], 0))
    own_grad, fins = tie(own_grad, fins)
    grad_tokens = merge_rows(grid.core, own_grad, own_blocks, F32)
    down_terms[-1], grad_tokens = tie(down_terms[-1], grad_tokens)
    down_terms[-1], fins = tie(down_terms[-1], fins)
    fins = jnp.split(fins, 3, 0)
    grad_down = finish(mine, grad_d, fins[0], True)
    grad_gate = finish(mine, grad_g, fins[1], False)
    grad_up = finish(mine, grad_u, fins[2], False)
    output = grid.gather_rows((resid + add(down_terms)).astype(BF16))
    grad_wo, grad_qkv = grad_oq[:, :qw].astype(F32), grad_oq[:, qw:].astype(F32)
    norm1 = norm1_part + lax.ppermute(norm1_part, "kv", grid.core_swap)
    norm1 = grid.scatter_blocks(norm1.reshape(n, -1))
    summed = grid.scatter_blocks(bundle)
    n_both = sum(c.shape[1] for c in cut[: len(both)])
    flat = jnp.concatenate([grid.sum_kv(summed[:n_both].astype(BF16)), summed[n_both:]])
    done = []
    at = 0
    for x, d in both + alone:
        shape = list(x.shape)
        shape[d] //= n
        size = x.size // n
        done.append(flat[at : at + size].reshape(shape))
        at += size
    grad_a, grad_bo, norm2, bq, bk, bv, featq, featk, grad_ao = done
    return (
        output,
        grad_tokens,
        norm1,
        grad_qkv[:, :qw],
        grad_qkv[:, qw : qw + kw],
        grad_qkv[:, qw + kw :],
        grad_a[:rank].T,
        bq,
        grad_a[rank : 2 * rank].T,
        bk,
        grad_a[2 * rank :].T,
        bv,
        featq,
        featk,
        grad_wo.T,
        grad_ao,
        grad_bo,
        norm2,
        grad_gate,
        grad_up,
        grad_down,
    )


def solution(mesh):
    placed = (
        P("seq", None),
        P(),
        P(None, "kv"),
        P(None, "kv"),
        P(None, "kv"),
        P(),
        P(None, "kv", None),
        P(),
        P(None, "kv", None),
        P(),
        P(None, "kv", None),
        P("kv", None, None),
        P("kv", None, None),
        P("kv", None),
        P("kv", None, None),
        P(),
        P(),
        P(None, "kv"),
        P(None, "kv"),
        P("kv", None),
        P("seq"),
        P("seq", None),
    )
    return jax.shard_map(
        local,
        mesh=mesh,
        in_specs=placed,
        out_specs=(
            P("seq", None),
            P("seq", None),
            P("seq"),
            P("seq", "kv"),
            P("seq", "kv"),
            P("seq", "kv"),
            P("seq", None),
            P(None, "kv", "seq"),
            P("seq", None),
            P(None, "kv", "seq"),
            P("seq", None),
            P(None, "kv", "seq"),
            P("kv", "seq", None),
            P("kv", "seq", None),
            P("kv", "seq"),
            P("kv", "seq", None),
            P(None, "seq"),
            P("seq"),
            P("seq", "kv"),
            P("seq", "kv"),
            P("kv", "seq"),
        ),
        check_vma=False,
    )
```
